32 devices in a mesh: event: 4 (over x, core), row: 8 (over z, y).
Axes of the slice: x: 2, y: 2, z: 4, core: 2. Of those that a mesh axis runs over, the one named last changes fastest.
Arguments:
- initial_head: float32 [4, 48, 32, 384], P('event', None, 'row'), may hold values from -6 to -1.5
- sat_conductivity: float32 [64], replicated, may hold values from 0.3 to 3
- vg_alpha: float32 [64], replicated, may hold values from 0.25 to 1
- vg_n: float32 [64], replicated, may hold values from 1.3 to 2.5
- zone_map: int32 [16, 192], P('row'), may hold values from 0 to 63, as said below
- forcing_plan: int32 [4, 2, 16], P('event', None, 'row'), may hold values from 0 to 3
- tensiometer_cells: int32 [4, 2048], P('event', 'row'), may hold values from 0 to 73727
- tensiometer_heads: float32 [4, 2048], P('event', 'row'), may hold values from -6 to -1
Outputs:
- final_head: float32 [4, 48, 32, 384], P('event', None, 'row')
- misfit: float32 [], replicated
- grad_conductivity: float32 [64], replicated
- grad_alpha: float32 [64], replicated
- grad_n: float32 [64], replicated
The draws below stay inside these ranges and needn't reach their ends.
Inputs may be any that keep to these rules, and one draw needn't show every extreme that they name: `zone_map`: the zone of a block in block row a lies among the 16 zones from a * 2 * 2 onward, taken modulo 64. `tensiometer_cells`: tensiometer j lies in the rows j // 256 * 4 to j // 256 * 4 + 3; the entry is its offset inside that block of rows, as depth * 4 * 384 + row offset * 384 + column.
All inputs are finite; a program needn't handle non-finite values.
Results may differ from the reference program's by a relative error of at most 0.0003.
Values sent between devices are 32-bit elements; how exact they have to be, the bound alone decides.
A program may use at most 64 MiB of HBM per device.

```python
import math
import jax
import jax.numpy as jnp
from jax import lax

ROWS_DEV = 4
NY = 384
NZ = 48
STEPS = 2
SENS_DEV = 256
ZONES_DEV = 8
NX = 32
EVENTS = 4
SENSORS = 2048
ZONES = 64


def draw_zone_map(key, part):
    key = jax.random.fold_in(key, 11)
    block_rows = jnp.arange(NX // 2, dtype=jnp.int32)
    base = block_rows * (2 * ZONES_DEV) // ROWS_DEV
    offset = jax.random.randint(key, (NX // 2, NY // 2), 0, 2 * ZONES_DEV, dtype=jnp.int32)
    return (base[:, None] + offset) % ZONES


def place_ends(result, own_key, low, top_value):
    longest = result.shape.index(max(result.shape))
    spots = []
    for shift in (0, 1):
        where = [jax.random.randint(jax.random.fold_in(own_key, axis), (), 0, length) for axis, length in enumerate(result.shape)]
        where[longest] = (where[longest] + shift) % result.shape[longest]
        spots.append(tuple(where))
    return result.at[spots[0]].set(low).at[spots[1]].set(top_value)


def block_scale(key, dims, split, smallest, top_value):
    gain, own = 1.0, jax.random.fold_in(key, 6)
    for dim, blocks in split:
        steps = jnp.exp(jax.random.uniform(jax.random.fold_in(own, dim), (blocks,), jnp.float32, smallest / len(split), top_value / len(split)))
        gain = gain * jnp.repeat(steps, dims[dim] // blocks).reshape([-1 if axis == dim else 1 for axis in range(len(dims))])
    return gain


def setup_inputs(seed: int = 0) -> dict:
    streams_of = jax.random.split(jax.random.key(seed), 9)
    initial_head = jnp.clip(-6.0 + 4.5 * jax.random.uniform(streams_of[0], (EVENTS, NZ, NX, NY), jnp.float32) ** block_scale(streams_of[0], (EVENTS, NZ, NX, NY), ((0, 4), (2, 8)), -0.2, 0.2), -6.0, -1.5)
    sat_conductivity = jnp.clip(jnp.exp(jax.random.uniform(streams_of[1], (ZONES,), jnp.float32, math.log(0.3), math.log(3.0))), 0.3, 3.0)
    vg_alpha = jnp.clip(jnp.exp(jax.random.uniform(streams_of[2], (ZONES,), jnp.float32, math.log(0.25), math.log(1.0))), 0.25, 1.0)
    vg_n = jnp.clip(jax.random.uniform(streams_of[3], (ZONES,), jnp.float32, 1.3, 2.5), 1.3, 2.5)
    zone_map = draw_zone_map(jax.random.fold_in(streams_of[8], 71), 0)
    forcing_plan = place_ends(jax.random.randint(streams_of[5], (EVENTS, STEPS, NX // 2), 0, 4), jax.random.fold_in(streams_of[5], 1), 0, 3).astype(jnp.int32)
    tensiometer_cells = place_ends(jax.random.randint(streams_of[6], (EVENTS, SENSORS), 0, NZ * ROWS_DEV * NY), jax.random.fold_in(streams_of[6], 1), 0, (NZ * ROWS_DEV * NY) - 1).astype(jnp.int32)
    tensiometer_heads = jnp.clip(-6.0 + 5.0 * jax.random.uniform(streams_of[7], (EVENTS, SENSORS), jnp.float32) ** block_scale(streams_of[7], (EVENTS, SENSORS), ((0, 4), (1, 8)), -0.2, 0.2), -6.0, -1.0)
    return {"initial_head": initial_head, "sat_conductivity": sat_conductivity, "vg_alpha": vg_alpha, "vg_n": vg_n, "zone_map": zone_map, "forcing_plan": forcing_plan, "tensiometer_cells": tensiometer_cells, "tensiometer_heads": tensiometer_heads}


CFL = 0.4
IRRIGATION = 0.2
WATER_RANGE = 0.35

def conductivity(head_now, sat_cond, air_entry, shape_n):
    x = air_entry * -head_now
    u = jnp.power(x, shape_n)
    m = 1.0 - 1.0 / shape_n
    frac = u / (1.0 + u)
    saturation = jnp.power(1.0 + u, -m)
    return sat_cond * jnp.sqrt(saturation) * jnp.square(1.0 - jnp.power(frac, m))

def capacity(head_now, air_entry, shape_n):
    x = air_entry * -head_now
    u = jnp.power(x, shape_n)
    m = 1.0 - 1.0 / shape_n
    return WATER_RANGE * m * shape_n * air_entry * jnp.power(x, shape_n - 1.0) * jnp.power(1.0 + u, -m - 1.0)

def fluxes(head_pad, cond_pad, level_top, open_mask):
    head_mid = head_pad[:, 1:-1]
    cond_mid = cond_pad[:, 1:-1]
    face_x = 0.5 * (cond_pad[:, :-1] + cond_pad[:, 1:]) * open_mask[None, :, None]
    flow_x = face_x * (head_pad[:, 1:] - head_pad[:, :-1])
    net_x = flow_x[:, 1:] - flow_x[:, :-1]
    face_y = 0.5 * (cond_mid[:, :, :-1] + cond_mid[:, :, 1:])
    flow_y = face_y * (head_mid[:, :, 1:] - head_mid[:, :, :-1])
    zero_y = jnp.zeros_like(cond_mid[:, :, :1])
    flow_y = jnp.concatenate([zero_y, flow_y, zero_y], 2)
    net_y = flow_y[:, :, 1:] - flow_y[:, :, :-1]
    face_y = jnp.concatenate([zero_y, face_y, zero_y], 2)
    face_z = 0.5 * (cond_mid[:-1] + cond_mid[1:])
    flow_z = face_z * (1.0 + head_mid[:-1] - head_mid[1:])
    top_flow = level_top[None] * IRRIGATION * cond_mid[:1]
    flow_z = jnp.concatenate([top_flow, flow_z, cond_mid[-1:]], 0)
    net_z = flow_z[:-1] - flow_z[1:]
    face_z = jnp.concatenate([cond_mid[:1], face_z, cond_mid[-1:]], 0)
    cond_sum = face_x[:, 1:] + face_x[:, :-1] + (face_y[:, :, 1:] + face_y[:, :, :-1]) + (face_z[:-1] + face_z[1:])
    return (net_x + net_y + net_z, cond_sum)

def reference(initial_head, sat_conductivity, vg_alpha, vg_n, zone_map, forcing_plan, tensiometer_cells, tensiometer_heads):
    open_mask = jnp.concatenate([jnp.zeros((1,), jnp.float32), jnp.ones((NX - 1,), jnp.float32), jnp.zeros((1,), jnp.float32)])
    sensor = jnp.arange(SENSORS, dtype=jnp.int32)

    def spread(table):
        return jnp.repeat(jnp.repeat(table[zone_map], 2, axis=0), 2, axis=1)

    def one_event(inputs):
        head_start, plan, cells, targets = inputs
        levels = jnp.repeat(plan.astype(jnp.float32), 2, axis=1)
        depth_index = (cells // (ROWS_DEV * NY)).astype(jnp.int32)
        row_index = (sensor // SENS_DEV * ROWS_DEV + cells // NY % ROWS_DEV).astype(jnp.int32)
        column_index = (cells % NY).astype(jnp.int32)

        def misfit_of(tables):
            sat_cond = spread(tables[0])
            air_entry = spread(tables[1])
            shape_n = spread(tables[2])
            head_now = head_start
            for step in range(STEPS):
                cond = conductivity(head_now, sat_cond, air_entry, shape_n)
                store = capacity(head_now, air_entry, shape_n)
                head_pad = jnp.pad(head_now, ((0, 0), (1, 1), (0, 0)))
                cond_pad = jnp.pad(cond, ((0, 0), (1, 1), (0, 0)))
                net_flow, cond_sum = fluxes(head_pad, cond_pad, levels[step][:, None], open_mask)
                step_size = lax.stop_gradient(CFL / jnp.max(cond_sum / store))
                head_now = head_now + step_size * net_flow / store
            picked = head_now[depth_index, row_index, column_index]
            diff = picked - targets
            return (0.5 / EVENTS * jnp.sum(diff * diff), head_now)
        loss, vjp_fn, final = jax.vjp(misfit_of, (sat_conductivity, vg_alpha, vg_n), has_aux=True)
        grads = vjp_fn(jnp.ones_like(loss))[0]
        return (final, loss, grads[0], grads[1], grads[2])
    finals, losses, grad_k, grad_a, grad_m = lax.map(one_event, (initial_head, forcing_plan, tensiometer_cells, tensiometer_heads))
    return (finals, jnp.sum(losses), lax.optimization_barrier(jnp.sum(grad_k, 0)), lax.optimization_barrier(jnp.sum(grad_a, 0)), lax.optimization_barrier(jnp.sum(grad_m, 0)))
```

```python
import functools

import jax
import jax.numpy as jnp
from jax import lax
from jax.experimental import pallas as pl
from jax.experimental.pallas import tpu as pltpu
from jax.sharding import PartitionSpec as P

STEPS = 2
CFL = 0.4
IRRIGATION = 0.2
WATER_RANGE = 0.35
HIGHEST = lax.Precision.HIGHEST
F32 = jnp.float32
BF16 = jnp.bfloat16
LINKS = 7


def nt_dot(a, b, precision=None):
    return lax.dot_general(
        a, b, (((1,), (1,)), ((), ())), precision=precision, preferred_element_type=F32
    )


def fold(x):
    return jnp.sum(x.reshape(x.shape[0] // 8, 8, x.shape[1]), axis=0)


def kernel(
    count,
    groups,
    events,
    x_ref,
    sat_ref,
    alpha_ref,
    n_ref,
    zone_ref,
    plan_ref,
    cells_ref,
    heads_ref,
    out_ref,
    small_ref,
    HB,
    KB,
    AB,
    IC,
    LG,
    LV,
    WW,
    RV,
    QQ,
    GB,
    LAM,
    WB,
    TM,
    PB,
    TAB,
    OH,
    NC,
    NT,
    RATE,
    ACC,
    MX,
    SUMR,
    SUME,
    link_send,
    link_recv,
    max_send,
    max_recv,
    sum_send,
    sum_recv,
    ev_send,
    ev_recv,
):
    rows, depth, width = x_ref.shape
    zp = OH.shape[1]
    zones = sat_ref.shape[1]
    pos = lax.axis_index("row")
    me_event = lax.axis_index("event")
    up, down = pos - 1, pos + 1
    has_up, has_down = pos > 0, pos < count - 1
    lower_open = has_up.astype(F32)
    upper_open = has_down.astype(F32)

    def dev(row):
        return (me_event, row)

    barrier = pltpu.get_barrier_semaphore()
    for k in range(1, count):
        pl.semaphore_signal(
            barrier, 1, device_id=dev(lax.rem(pos + k, count)), device_id_type=pl.DeviceIdType.MESH
        )
    for k in range(1, groups):
        pl.semaphore_signal(
            barrier,
            1,
            device_id=(lax.rem(me_event + k, groups), pos),
            device_id_type=pl.DeviceIdType.MESH,
        )
    pl.semaphore_wait(barrier, count - 1 + groups - 1)

    def link(number, side, src, dst):
        return pltpu.make_async_remote_copy(
            src_ref=src,
            dst_ref=dst,
            send_sem=link_send.at[number, side],
            recv_sem=link_recv.at[number, side],
            device_id=dev(up if side == 0 else down),
            device_id_type=pl.DeviceIdType.MESH,
        )

    def start_pair(number, to_up, to_down):
        @pl.when(has_up)
        def _():
            link(number, 0, *to_up).start()

        @pl.when(has_down)
        def _():
            link(number, 1, *to_down).start()

    def recv_pair(number, to_up, to_down):
        @pl.when(has_down)
        def _():
            link(number, 0, *to_up).wait_recv()

        @pl.when(has_up)
        def _():
            link(number, 1, *to_down).wait_recv()

    def sent_pair(number, to_up, to_down):
        @pl.when(has_up)
        def _():
            link(number, 0, *to_up).wait_send()

        @pl.when(has_down)
        def _():
            link(number, 1, *to_down).wait_send()

    pairs = [
        ((x_ref.at[0], HB.at[0, rows + 1]), (x_ref.at[rows - 1], HB.at[0, 0])),
        ((PB.at[1], PB.at[3]), (PB.at[2], PB.at[0])),
        ((cells_ref, NC.at[1]), (cells_ref, NC.at[0])),
        ((heads_ref, NT.at[1]), (heads_ref, NT.at[0])),
        ((AB.at[0, 1], AB.at[0, rows + 1]), (AB.at[0, rows], AB.at[0, 0])),
        ((AB.at[1, 1], AB.at[1, rows + 1]), (AB.at[1, rows], AB.at[1, 0])),
        ((GB.at[0, 1], GB.at[0, rows + 1]), (GB.at[0, rows], GB.at[0, 0])),
    ]

    def start(number):
        start_pair(number, *pairs[number])

    def recv(number):
        recv_pair(number, *pairs[number])

    start(0)
    start(2)
    start(3)

    TAB[...] = jnp.zeros_like(TAB)
    TAB[0:1, :zones] = sat_ref[...]
    TAB[1:2, :zones] = alpha_ref[...]
    TAB[2:3, :zones] = n_ref[...]
    blocks = zone_ref.shape[1]
    spread = (
        lax.broadcasted_iota(jnp.int32, (blocks, width), 1) // 2
        == lax.broadcasted_iota(jnp.int32, (blocks, width), 0)
    ).astype(F32)
    ids = jnp.dot(zone_ref[...].astype(F32), spread, preferred_element_type=F32, precision=HIGHEST)
    zone_of = lax.broadcasted_iota(jnp.int32, (zp, width), 0).astype(F32)
    for pair in range(2):
        OH[pair] = jnp.where(zone_of == ids[pair : pair + 1], 1.0, 0.0)
        PB[pair + 1] = jnp.dot(TAB[...], OH[pair], precision=HIGHEST, preferred_element_type=F32)
    start(1)

    @pl.when(jnp.logical_not(has_up))
    def _():
        HB[0, 0] = x_ref[0]
        PB[0] = PB[1]
        NC[0] = cells_ref[...]
        NT[0] = heads_ref[...]
        for step in range(STEPS):
            AB[step, 0] = jnp.zeros((depth, width), F32)
        GB[0, 0] = jnp.zeros((depth, width), F32)

    @pl.when(jnp.logical_not(has_down))
    def _():
        HB[0, rows + 1] = x_ref[rows - 1]
        PB[3] = PB[2]
        NC[1] = cells_ref[...]
        NT[1] = heads_ref[...]
        for step in range(STEPS):
            AB[step, rows + 1] = jnp.zeros((depth, width), F32)
        GB[0, rows + 1] = jnp.zeros((depth, width), F32)

    ACC[...] = jnp.zeros_like(ACC)

    column = lax.broadcasted_iota(jnp.int32, (1, width), 1)
    layer = lax.broadcasted_iota(jnp.int32, (depth, 1), 0)
    right_half = jnp.where(column < width - 1, 0.5, 0.0)
    below_half = jnp.where(layer < depth - 1, 0.5, 0.0)
    ends = jnp.where((layer == 0) | (layer == depth - 1), 1.0, 0.0)

    def left(v):
        return pltpu.roll(v, width - 1, 1)

    def right(v):
        return pltpu.roll(v, 1, 1)

    def above(v):
        return pltpu.roll(v, 1, 0)

    def below(v):
        return pltpu.roll(v, depth - 1, 0)

    def over(indices, body):
        first, stride, number = indices

        def go(j, carry):
            body(first + stride * j)
            return carry

        lax.fori_loop(0, number, go, 0)

    own = (1, 1, rows)
    inner = (2, 1, rows - 2)
    edges = (1, rows - 1, 2)
    halo = (0, rows + 1, 2)

    def params(i):
        block = PB[(i + 1) // 2]
        return block[0:1], block[1:2], block[2:3]

    def face(i):
        return jnp.where(i == 0, lower_open, jnp.where(i == rows, upper_open, 1.0))

    def forcing(step, i):
        level = jnp.where(i > 2, plan_ref[step, 1], plan_ref[step, 0]).astype(F32)
        return jnp.where(layer == 0, level * IRRIGATION, jnp.where(layer == depth - 1, -1.0, 0.0))

    def cell(step, i, head):
        sat, alpha, n = params(i)
        m = 1.0 - 1.0 / n
        x = alpha * -head
        log_x = jnp.log(x)
        power = jnp.exp((n - 1.0) * log_x)
        v = 1.0 + x * power
        log_v = jnp.log(v)
        root = jnp.exp((-0.5 * m) * log_v)
        w = power * (root * root)
        rest = 1.0 - w
        q = sat * root * rest
        KB[step, i] = q * rest
        IC[step, i] = v / ((WATER_RANGE * (n - 1.0) * alpha) * w)
        LG[step, i] = log_x
        LV[step, i] = log_v
        WW[step, i] = w
        RV[step, i] = 1.0 / v
        QQ[step, i] = q

    def flow(step, i):
        h, k = HB[step, i], KB[step, i]
        inv = IC[step, i]
        k_up = (0.5 * face(i - 1)) * (KB[step, i - 1] + k)
        k_down = (0.5 * face(i)) * (k + KB[step, i + 1])
        k_y = right_half * (k + left(k))
        k_z = below_half * (k + below(k))
        f_y = k_y * (left(h) - h)
        f_z = k_z * (1.0 + h - below(h))
        net = (
            k_down * (HB[step, i + 1] - h)
            + k_up * (HB[step, i - 1] - h)
            + (f_y - right(f_y))
            + (above(f_z) - f_z)
            + forcing(step, i) * k
        )
        total = k_up + k_down + (k_y + right(k_y)) + (k_z + above(k_z)) + ends * k
        AB[step, i] = net * inv
        rate = jnp.max((total * inv).reshape(depth // 8, 8, width), axis=0)
        RATE[step] = jnp.maximum(RATE[step], rate)

    def max_copy(step, k):
        return pltpu.make_async_remote_copy(
            src_ref=MX.at[step, pos],
            dst_ref=MX.at[step, pos],
            send_sem=max_send.at[step, k],
            recv_sem=max_recv.at[step, pos],
            device_id=dev(lax.rem(pos + k, count)),
            device_id_type=pl.DeviceIdType.MESH,
        )

    def max_got(step, k):
        src = lax.rem(pos + k, count)
        return pltpu.make_async_remote_copy(
            src_ref=MX.at[step, src],
            dst_ref=MX.at[step, src],
            send_sem=max_send.at[step, k],
            recv_sem=max_recv.at[step, src],
            device_id=dev(src),
            device_id_type=pl.DeviceIdType.MESH,
        )

    def send_rate(step):
        rate = RATE[step]
        tile = rate[:, :128]
        for start_lane in range(128, width, 128):
            tile = jnp.maximum(tile, rate[:, start_lane : start_lane + 128])
        MX[step, pos] = tile
        for k in range(1, count):
            max_copy(step, k).start()

    def step_size(step):
        for k in range(1, count):
            max_got(step, k).wait_recv()
        top = jnp.max(MX[step], axis=0)
        return CFL / jnp.max(top, keepdims=True)

    RATE[...] = jnp.zeros_like(RATE)

    def first_cell(i):
        HB[0, i] = x_ref[i - 1]
        cell(0, i, x_ref[i - 1])

    over(own, first_cell)
    over(inner, functools.partial(flow, 0))
    recv(0)
    recv(1)
    over(halo, lambda i: cell(0, i, HB[0, i]))
    over(edges, functools.partial(flow, 0))
    send_rate(0)
    start(4)

    def places(cells):
        index = cells.astype(F32)
        line = jnp.floor((index + 0.5) * (1.0 / width))
        col = index - width * line
        level = jnp.floor((line + 0.5) * (1.0 / rows))
        return level, line - rows * level, col

    def pieces(t):
        one = t.astype(BF16)
        rest = t - one.astype(F32)
        two = rest.astype(BF16)
        return one, two, (rest - two.astype(F32)).astype(BF16)

    sensors = cells_ref.shape[1]
    col_of = lax.broadcasted_iota(jnp.int32, (width, sensors), 0).astype(F32)

    def counts(cells, targets, wanted):
        level, row, col = places(cells)
        cols = jnp.where(col_of == col, 1.0, 0.0)
        cols16 = cols.astype(BF16)
        if wanted is None:
            spot = row * depth + level
            lines = rows * depth
        else:
            spot = jnp.where(row == wanted, level, -1.0)
            lines = depth
        line_of = lax.broadcasted_iota(jnp.int32, (lines, sensors), 0).astype(F32)
        hit = line_of == spot
        number = nt_dot(jnp.where(hit, 1.0, 0.0).astype(BF16), cols16)
        total = None
        for piece in pieces(targets):
            part = nt_dot(jnp.where(hit, piece.astype(F32), 0.0).astype(BF16), cols16)
            total = part if total is None else total + part
        return number, total / jnp.maximum(number, 1.0), hit, cols

    number, mean, hit, cols = counts(cells_ref[...], heads_ref[...], None)
    WB[1 : rows + 1] = number.reshape(rows, depth, width)
    TM[1 : rows + 1] = mean.reshape(rows, depth, width)
    at_sensor = jnp.dot(mean, cols, precision=HIGHEST, preferred_element_type=F32)
    own_mean = jnp.sum(jnp.where(hit, at_sensor, 0.0), axis=0, keepdims=True)
    spread_sum = jnp.sum((heads_ref[...] - own_mean) ** 2, keepdims=True)
    recv(2)
    recv(3)
    for side, wanted, place in ((0, rows - 1, 0), (1, 0, rows + 1)):
        number, mean, _, _ = counts(NC[side], NT[side], wanted)
        WB[place] = number
        TM[place] = mean

    dt0 = step_size(0)

    def next_cell(i):
        head = HB[0, i] + dt0 * AB[0, i]
        HB[1, i] = head
        cell(1, i, head)

    over(own, next_cell)
    over(inner, functools.partial(flow, 1))
    recv(4)
    over(halo, next_cell)
    over(edges, functools.partial(flow, 1))
    send_rate(1)
    start(5)
    dt1 = step_size(1)
    scale = 1.0 / events

    def last_head(i):
        head = HB[1, i] + dt1 * AB[1, i]
        off = head - TM[i]
        pull = (scale * WB[i]) * off
        GB[1, i] = pull * dt1 * IC[1, i]
        return head, off * pull, pull

    def finish(i):
        head, square, pull = last_head(i)
        out_ref[i - 1] = head
        LAM[1, i] = pull
        ACC[2, 0] += fold(square)

    over(own, finish)
    recv(5)
    over(halo, lambda i: (last_head(i), None)[1])

    def pull_back(step, dt, i):
        sat, alpha, n = params(i)
        h, k, g, lam = HB[step, i], KB[step, i], GB[step, i], LAM[step, i]
        hu, hd = HB[step, i - 1], HB[step, i + 1]
        gu, gd = GB[step, i - 1], GB[step, i + 1]
        d_y = left(h) - h
        d_z = 1.0 + h - below(h)
        e_y = left(g) - g
        e_z = below(g) - g
        s_up, s_down = 0.5 * face(i - 1), 0.5 * face(i)
        c_y = right_half * d_y * e_y
        c_z = below_half * d_z * e_z
        grad_k = (
            s_down * ((hd - h) * (g - gd))
            + s_up * ((hu - h) * (g - gu))
            - (c_y + right(c_y))
            + (c_z + above(c_z))
            + forcing(step, i) * g
        )
        change = -lam * (dt * AB[step, i])
        n1 = n - 1.0
        m = 1.0 - 1.0 / n
        inv_n2 = 1.0 / (n * n)
        log_x, log_v, w, r = LG[step, i], LV[step, i], WW[step, i], RV[step, i]
        f = 1.0 - r
        wq = 2.0 * w * QQ[step, i]
        n1r = n1 * r
        fk = f * k
        grad_log = change * (n1r - n * f) - grad_k * ((0.5 * n1) * fk + n1r * wq)
        fl = f * log_x
        d_w = log_x - inv_n2 * log_v - m * fl
        grad_n = change * (1.0 / n1 + d_w - fl) - grad_k * (
            (0.5 * k) * (inv_n2 * log_v + m * fl) + wq * d_w
        )
        pair = (i - 1) // 2
        ACC[pair, 0] += fold(grad_k * k)
        ACC[pair, 1] += fold(grad_log + change)
        ACC[pair, 2] += fold(grad_n)
        if step == 0:
            return
        k_up = s_up * (KB[step, i - 1] + k)
        k_down = s_down * (k + KB[step, i + 1])
        f_y = right_half * (k + left(k)) * e_y
        f_z = below_half * (k + below(k)) * e_z
        lap = k_down * (gd - g) + k_up * (gu - g) + (f_y - right(f_y)) + (f_z - above(f_z))
        before = lam + lap + grad_log / h
        LAM[0, i] = before
        GB[0, i] = before * dt0 * IC[0, i]

    back1 = functools.partial(pull_back, 1, dt1)
    back0 = functools.partial(pull_back, 0, dt0)
    over(edges, back1)
    start(6)
    over(inner, back1)
    over(inner, back0)
    recv(6)
    over(edges, back0)

    zone_sums = None
    line = lax.broadcasted_iota(jnp.int32, (8, width), 0)
    for pair in range(2):
        sat, alpha, _ = params(1 + 2 * pair)
        grads = [
            jnp.sum(ACC[pair, 0], axis=0, keepdims=True) / sat,
            jnp.sum(ACC[pair, 1], axis=0, keepdims=True) / alpha,
            jnp.sum(ACC[pair, 2], axis=0, keepdims=True),
        ]
        block = jnp.zeros((8, width), F32)
        for place, grad in enumerate(grads):
            block = jnp.where(line == place, grad, block)
        part = nt_dot(block, OH[pair], HIGHEST)
        zone_sums = part if zone_sums is None else zone_sums + part
    loss = 0.5 * (jnp.sum(ACC[2, 0], keepdims=True) + scale * spread_sum)
    zone_line = lax.broadcasted_iota(jnp.int32, (8, zp), 0)
    SUMR[pos] = jnp.where(zone_line == 3, loss, zone_sums)

    def row_copy(k, src):
        return pltpu.make_async_remote_copy(
            src_ref=SUMR.at[src],
            dst_ref=SUMR.at[src],
            send_sem=sum_send.at[k],
            recv_sem=sum_recv.at[src],
            device_id=dev(lax.rem(pos + k, count)),
            device_id_type=pl.DeviceIdType.MESH,
        )

    def event_copy(k, src):
        return pltpu.make_async_remote_copy(
            src_ref=SUME.at[src],
            dst_ref=SUME.at[src],
            send_sem=ev_send.at[k],
            recv_sem=ev_recv.at[src],
            device_id=(lax.rem(me_event + k, groups), pos),
            device_id_type=pl.DeviceIdType.MESH,
        )

    for k in range(1, count):
        row_copy(k, pos).start()
    for k in range(1, count):
        row_copy(k, lax.rem(pos + k, count)).wait_recv()
    SUME[me_event] = jnp.sum(SUMR[...], axis=0)
    for k in range(1, groups):
        event_copy(k, me_event).start()
    for k in range(1, groups):
        event_copy(k, lax.rem(me_event + k, groups)).wait_recv()
    small_ref[...] = jnp.sum(SUME[...], axis=0)

    for number in range(LINKS):
        sent_pair(number, *pairs[number])
    for k in range(1, count):
        max_copy(0, k).wait_send()
        max_copy(1, k).wait_send()
        row_copy(k, pos).wait_send()
    for k in range(1, groups):
        event_copy(k, me_event).wait_send()


def local(
    initial_head,
    sat_conductivity,
    vg_alpha,
    vg_n,
    zone_map,
    forcing_plan,
    tensiometer_cells,
    tensiometer_heads,
):
    _, depth, rows, width = initial_head.shape
    zones = sat_conductivity.shape[0]
    zp = -(-zones // 128) * 128
    count = lax.axis_size("row")
    groups = lax.axis_size("event")
    sensors = tensiometer_cells.shape[1]
    vmem = pl.BlockSpec(memory_space=pltpu.VMEM)
    smem = pl.BlockSpec(memory_space=pltpu.SMEM)
    full = pltpu.VMEM((STEPS, rows + 2, depth, width), F32)
    single = pltpu.VMEM((rows + 2, depth, width), F32)
    dma = pltpu.SemaphoreType.DMA
    head, small = pl.pallas_call(
        functools.partial(kernel, count, groups, groups * initial_head.shape[0]),
        out_shape=(
            jax.ShapeDtypeStruct((rows, depth, width), F32),
            jax.ShapeDtypeStruct((8, zp), F32),
        ),
        in_specs=[vmem] * 5 + [smem] + [vmem] * 2,
        out_specs=(vmem, vmem),
        scratch_shapes=[
            full,
            full,
            full,
            full,
            full,
            full,
            full,
            full,
            full,
            full,
            full,
            single,
            single,
            pltpu.VMEM((4, 8, width), F32),
            pltpu.VMEM((8, zp), F32),
            pltpu.VMEM((2, zp, width), F32),
            pltpu.VMEM((2, 1, sensors), jnp.int32),
            pltpu.VMEM((2, 1, sensors), F32),
            pltpu.VMEM((STEPS, 8, width), F32),
            pltpu.VMEM((3, 3, 8, width), F32),
            pltpu.VMEM((STEPS, count, 8, 128), F32),
            pltpu.VMEM((count, 8, zp), F32),
            pltpu.VMEM((groups, 8, zp), F32),
            dma((LINKS, 2)),
            dma((LINKS, 2)),
            dma((STEPS, count)),
            dma((STEPS, count)),
            dma((count,)),
            dma((count,)),
            dma((groups,)),
            dma((groups,)),
        ],
        compiler_params=pltpu.CompilerParams(
            collective_id=0, has_side_effects=True, vmem_limit_bytes=48 * 1024 * 1024
        ),
    )(
        jnp.transpose(initial_head[0], (1, 0, 2)),
        sat_conductivity[None],
        vg_alpha[None],
        vg_n[None],
        zone_map,
        forcing_plan[0],
        tensiometer_cells,
        tensiometer_heads,
    )
    final = jnp.transpose(head, (1, 0, 2))[None]
    return (final, small[3, 0], small[0, :zones], small[1, :zones], small[2, :zones])


def solution(mesh):
    return jax.shard_map(
        local,
        mesh=mesh,
        in_specs=(
            P("event", None, "row", None),
            P(),
            P(),
            P(),
            P("row", None),
            P("event", None, "row"),
            P("event", "row"),
            P("event", "row"),
        ),
        out_specs=(P("event", None, "row", None), P(), P(), P(), P()),
        check_vma=False,
    )
```

```python
import functools

import jax
import jax.numpy as jnp
from jax import lax
from jax.experimental import pallas as pl
from jax.experimental.pallas import tpu as pltpu
from jax.sharding import PartitionSpec as P

STEPS = 2
CFL = 0.4
IRRIGATION = 0.2
WATER_RANGE = 0.35
HIGHEST = lax.Precision.HIGHEST
F32 = jnp.float32
BF16 = jnp.bfloat16
LINKS = 6
DIRECT = 64


def nt_dot(a, b, precision=None):
    return lax.dot_general(
        a, b, (((1,), (1,)), ((), ())), precision=precision, preferred_element_type=F32
    )


def fold(x):
    return jnp.sum(x.reshape(x.shape[0] // 8, 8, x.shape[1]), axis=0)


def kernel(
    count,
    groups,
    events,
    x_ref,
    sat_ref,
    alpha_ref,
    n_ref,
    zone_ref,
    plan_ref,
    cells_ref,
    heads_ref,
    out_ref,
    small_ref,
    HB,
    KB,
    AB,
    IC,
    LG,
    LV,
    WW,
    RV,
    QQ,
    GB,
    LAM,
    WB,
    TM,
    PB,
    TAB,
    OH,
    NC,
    NT,
    SV,
    NV,
    RATE,
    ACC,
    MX,
    SUMR,
    SUME,
    link_send,
    link_recv,
    max_send,
    max_recv,
    sum_send,
    sum_recv,
    ev_send,
    ev_recv,
):
    depth, rows, width = x_ref.shape
    zp = OH.shape[1]
    zones = sat_ref.shape[1]
    pos = lax.axis_index("row")
    me_event = lax.axis_index("event")
    up, down = pos - 1, pos + 1
    has_up, has_down = pos > 0, pos < count - 1
    lower_open = has_up.astype(F32)
    upper_open = has_down.astype(F32)

    def dev(row):
        return (me_event, row)

    total_devices = count * groups
    direct = total_devices <= DIRECT
    index = me_event * count + pos

    def other(k):
        at = lax.rem(index + k, total_devices)
        return at // count, lax.rem(at, count)

    barrier = pltpu.get_barrier_semaphore()
    if direct:
        greeted = [other(k) for k in range(1, total_devices)]
    else:
        greeted = [dev(lax.rem(pos + k, count)) for k in range(1, count)]
        greeted += [(lax.rem(me_event + k, groups), pos) for k in range(1, groups)]
    for device in greeted:
        pl.semaphore_signal(barrier, 1, device_id=device, device_id_type=pl.DeviceIdType.MESH)

    def link(number, side, src, dst):
        return pltpu.make_async_remote_copy(
            src_ref=src,
            dst_ref=dst,
            send_sem=link_send.at[number, side],
            recv_sem=link_recv.at[number, side],
            device_id=dev(up if side == 0 else down),
            device_id_type=pl.DeviceIdType.MESH,
        )

    def start_pair(number, to_up, to_down):
        @pl.when(has_up)
        def _():
            link(number, 0, *to_up).start()

        @pl.when(has_down)
        def _():
            link(number, 1, *to_down).start()

    def recv_pair(number, to_up, to_down):
        @pl.when(has_down)
        def _():
            link(number, 0, *to_up).wait_recv()

        @pl.when(has_up)
        def _():
            link(number, 1, *to_down).wait_recv()

    def sent_pair(number, to_up, to_down):
        @pl.when(has_up)
        def _():
            link(number, 0, *to_up).wait_send()

        @pl.when(has_down)
        def _():
            link(number, 1, *to_down).wait_send()

    pairs = [
        ((HB.at[0, 1], HB.at[0, rows + 1]), (HB.at[0, rows], HB.at[0, 0])),
        ((PB.at[1], PB.at[3]), (PB.at[2], PB.at[0])),
        ((cells_ref, NC.at[1]), (cells_ref, NC.at[0])),
        ((heads_ref, NT.at[1]), (heads_ref, NT.at[0])),
        ((AB.at[0, 1], AB.at[0, rows + 1]), (AB.at[0, rows], AB.at[0, 0])),
        ((SV.at[0], NV.at[1]), (SV.at[1], NV.at[0])),
    ]

    def start(number):
        start_pair(number, *pairs[number])

    def recv(number):
        recv_pair(number, *pairs[number])

    for i in range(rows):
        HB[0, i + 1] = x_ref[:, i, :]

    TAB[...] = jnp.zeros_like(TAB)
    TAB[0:1, :zones] = sat_ref[...]
    TAB[1:2, :zones] = alpha_ref[...]
    TAB[2:3, :zones] = n_ref[...]
    blocks = zone_ref.shape[1]
    spread = (
        lax.broadcasted_iota(jnp.int32, (blocks, width), 1) // 2
        == lax.broadcasted_iota(jnp.int32, (blocks, width), 0)
    ).astype(F32)
    ids = jnp.dot(zone_ref[...].astype(F32), spread, preferred_element_type=F32, precision=HIGHEST)
    packed = 2 * zones <= zp
    period = zp // 2 if packed else zp
    zone_of = (lax.broadcasted_iota(jnp.int32, (zp, width), 0) % period).astype(F32)
    part_line = lax.broadcasted_iota(jnp.int32, (8, width), 0)
    for pair in range(2):
        own_ids = ids[pair : pair + 1]
        OH[pair + 1] = jnp.where(zone_of == own_ids, 1.0, 0.0)
        block = jnp.dot(TAB[...], OH[pair + 1], precision=HIGHEST, preferred_element_type=F32)
        PB[pair + 1] = jnp.where(part_line == 3, own_ids, block)
    pl.semaphore_wait(barrier, len(greeted))
    start(0)
    start(1)
    start(2)
    start(3)

    @pl.when(jnp.logical_not(has_up))
    def _():
        HB[0, 0] = HB[0, 1]
        PB[0] = PB[1]
        NC[0] = cells_ref[...]
        NT[0] = heads_ref[...]
        NV[0] = jnp.zeros_like(NV[0])
        AB[0, 0] = jnp.zeros((depth, width), F32)

    @pl.when(jnp.logical_not(has_down))
    def _():
        HB[0, rows + 1] = HB[0, rows]
        PB[3] = PB[2]
        NC[1] = cells_ref[...]
        NT[1] = heads_ref[...]
        NV[1] = jnp.zeros_like(NV[1])
        AB[0, rows + 1] = jnp.zeros((depth, width), F32)

    ACC[...] = jnp.zeros_like(ACC)

    column = lax.broadcasted_iota(jnp.int32, (1, width), 1)
    layer = lax.broadcasted_iota(jnp.int32, (depth, 1), 0)
    right_half = jnp.where(column < width - 1, 0.5, 0.0)
    below_half = jnp.where(layer < depth - 1, 0.5, 0.0)
    ends = jnp.where((layer == 0) | (layer == depth - 1), 1.0, 0.0)

    def left(v):
        return pltpu.roll(v, width - 1, 1)

    def right(v):
        return pltpu.roll(v, 1, 1)

    def above(v):
        return pltpu.roll(v, 1, 0)

    def below(v):
        return pltpu.roll(v, depth - 1, 0)

    def over(indices, body):
        first, stride, number = indices

        def go(j, carry):
            body(first + stride * j)
            return carry

        lax.fori_loop(0, number, go, 0)

    own = (1, 1, rows)
    inner = (2, 1, rows - 2)
    edges = (1, rows - 1, 2)
    halo = (0, rows + 1, 2)

    def params(i):
        block = PB[(i + 1) // 2]
        return block[0:1], block[1:2], block[2:3]

    def face(i):
        return jnp.where(i == 0, lower_open, jnp.where(i == rows, upper_open, 1.0))

    def forcing(step, i):
        level = jnp.where(i > 2, plan_ref[step, 1], plan_ref[step, 0]).astype(F32)
        return jnp.where(layer == 0, level * IRRIGATION, jnp.where(layer == depth - 1, -1.0, 0.0))

    def cell(step, i, head):
        sat, alpha, n = params(i)
        m = 1.0 - 1.0 / n
        x = alpha * -head
        log_x = jnp.log(x)
        power = jnp.exp((n - 1.0) * log_x)
        v = 1.0 + x * power
        log_v = jnp.log(v)
        root = jnp.exp((-0.5 * m) * log_v)
        w = power * (root * root)
        rest = 1.0 - w
        q = sat * root * rest
        KB[step, i] = q * rest
        IC[step, i] = v / ((WATER_RANGE * (n - 1.0) * alpha) * w)
        LG[step, i] = log_x
        LV[step, i] = log_v
        WW[step, i] = w
        RV[step, i] = 1.0 / v
        QQ[step, i] = q

    def flow(step, i):
        h, k = HB[step, i], KB[step, i]
        inv = IC[step, i]
        k_up = (0.5 * face(i - 1)) * (KB[step, i - 1] + k)
        k_down = (0.5 * face(i)) * (k + KB[step, i + 1])
        k_y = right_half * (k + left(k))
        k_z = below_half * (k + below(k))
        f_y = k_y * (left(h) - h)
        f_z = k_z * (1.0 + h - below(h))
        net = (
            k_down * (HB[step, i + 1] - h)
            + k_up * (HB[step, i - 1] - h)
            + (f_y - right(f_y))
            + (above(f_z) - f_z)
            + forcing(step, i) * k
        )
        total = k_up + k_down + (k_y + right(k_y)) + (k_z + above(k_z)) + ends * k
        AB[step, i] = net * inv
        rate = jnp.max((total * inv).reshape(depth // 8, 8, width), axis=0)
        RATE[step] = jnp.maximum(RATE[step], rate)

    def max_copy(step, k):
        return pltpu.make_async_remote_copy(
            src_ref=MX.at[step, pos],
            dst_ref=MX.at[step, pos],
            send_sem=max_send.at[step, k],
            recv_sem=max_recv.at[step, pos],
            device_id=dev(lax.rem(pos + k, count)),
            device_id_type=pl.DeviceIdType.MESH,
        )

    def max_got(step, k):
        src = lax.rem(pos + k, count)
        return pltpu.make_async_remote_copy(
            src_ref=MX.at[step, src],
            dst_ref=MX.at[step, src],
            send_sem=max_send.at[step, k],
            recv_sem=max_recv.at[step, src],
            device_id=dev(src),
            device_id_type=pl.DeviceIdType.MESH,
        )

    def send_rate(step):
        rate = RATE[step]
        tile = rate[:, :128]
        for start_lane in range(128, width, 128):
            tile = jnp.maximum(tile, rate[:, start_lane : start_lane + 128])
        MX[step, pos] = tile
        for k in range(1, count):
            max_copy(step, k).start()

    def step_size(step):
        for k in range(1, count):
            max_got(step, k).wait_recv()
        top = jnp.max(MX[step], axis=0)
        return CFL / jnp.max(top, keepdims=True)

    RATE[...] = jnp.zeros_like(RATE)

    def first_cell(i):
        cell(0, i, HB[0, i])

    over(own, first_cell)
    over(inner, functools.partial(flow, 0))
    recv(0)
    recv(1)
    over(halo, first_cell)
    over(edges, functools.partial(flow, 0))
    send_rate(0)
    start(4)

    for pair in (0, 3):
        OH[pair] = jnp.where(zone_of == PB[pair][3:4], 1.0, 0.0)

    def places(cells):
        index = cells.astype(F32)
        line = jnp.floor((index + 0.5) * (1.0 / width))
        col = index - width * line
        level = jnp.floor((line + 0.5) * (1.0 / rows))
        return level, line - rows * level, col

    def pieces(t):
        one = t.astype(BF16)
        rest = t - one.astype(F32)
        two = rest.astype(BF16)
        return one, two, (rest - two.astype(F32)).astype(BF16)

    sensors = cells_ref.shape[1]
    col_of = lax.broadcasted_iota(jnp.int32, (width, sensors), 0).astype(F32)

    def counts(cells, targets, wanted):
        level, row, col = places(cells)
        cols = jnp.where(col_of == col, 1.0, 0.0)
        cols16 = cols.astype(BF16)
        if wanted is None:
            spot = row * depth + level
            lines = rows * depth
        else:
            spot = jnp.where(row == wanted, level, -1.0)
            lines = depth
        line_of = lax.broadcasted_iota(jnp.int32, (lines, sensors), 0).astype(F32)
        hit = line_of == spot
        number = nt_dot(jnp.where(hit, 1.0, 0.0).astype(BF16), cols16)
        total = put(targets, hit, cols16)
        return number, total / jnp.maximum(number, 1.0), hit, cols

    def put(values, hit, cols16):
        total = None
        for piece in pieces(values):
            part = nt_dot(jnp.where(hit, piece.astype(F32), 0.0).astype(BF16), cols16)
            total = part if total is None else total + part
        return total

    def take(field, hit, cols):
        at_sensor = jnp.dot(field, cols, precision=HIGHEST, preferred_element_type=F32)
        return jnp.sum(jnp.where(hit, at_sensor, 0.0), axis=0, keepdims=True)

    number, mean, own_hit, own_cols = counts(cells_ref[...], heads_ref[...], None)
    WB[1 : rows + 1] = number.reshape(rows, depth, width)
    TM[1 : rows + 1] = mean.reshape(rows, depth, width)
    own_mean = take(mean, own_hit, own_cols)
    spread_sum = jnp.sum((heads_ref[...] - own_mean) ** 2, keepdims=True)
    recv(2)
    recv(3)
    halo_spots = []
    for side, wanted, place in ((0, rows - 1, 0), (1, 0, rows + 1)):
        number, mean, hit, cols = counts(NC[side], NT[side], wanted)
        WB[place] = number
        TM[place] = mean
        halo_spots.append((side, place, hit, cols))

    dt0 = step_size(0)

    def next_cell(i):
        head = HB[0, i] + dt0 * AB[0, i]
        HB[1, i] = head
        cell(1, i, head)

    over(own, next_cell)
    over(inner, functools.partial(flow, 1))
    recv(4)
    over(halo, next_cell)
    over(edges, functools.partial(flow, 1))
    send_rate(1)
    SV[0] = take(AB[1, 1], own_hit[:depth], own_cols)
    SV[1] = take(AB[1, rows], own_hit[(rows - 1) * depth :], own_cols)
    start(5)
    recv(5)
    for side, place, hit, cols in halo_spots:
        AB[1, place] = put(NV[side], hit, cols.astype(BF16)) / jnp.maximum(WB[place], 1.0)
    dt1 = step_size(1)
    scale = 1.0 / events

    def last_head(i):
        head = HB[1, i] + dt1 * AB[1, i]
        off = head - TM[i]
        pull = (scale * WB[i]) * off
        GB[1, i] = pull * dt1 * IC[1, i]
        return head, off * pull, pull

    def finish(i):
        head, square, pull = last_head(i)
        out_ref[i - 1] = head
        LAM[1, i] = pull
        ACC[4, 0] += fold(square)

    over(own, finish)
    over(halo, lambda i: (last_head(i), None)[1])

    def slopes(step, i, grad_k, change):
        _, _, n = params(i)
        n1 = n - 1.0
        m = 1.0 - 1.0 / n
        inv_n2 = 1.0 / (n * n)
        k, log_x, log_v = KB[step, i], LG[step, i], LV[step, i]
        w, r = WW[step, i], RV[step, i]
        f = 1.0 - r
        wq = 2.0 * w * QQ[step, i]
        n1r = n1 * r
        fl = f * log_x
        d_w = log_x - inv_n2 * log_v - m * fl
        by_log = -grad_k * ((0.5 * n1) * (f * k) + n1r * wq)
        by_n = -grad_k * ((0.5 * k) * (inv_n2 * log_v + m * fl) + wq * d_w)
        by_alpha = by_log
        if change is not None:
            by_log = by_log + change * (n1r - n * f)
            by_n = by_n + change * (1.0 / n1 + d_w - fl)
            by_alpha = by_log + change
        pair = (i + 1) // 2
        ACC[pair, 0] += fold(grad_k * k)
        ACC[pair, 1] += fold(by_alpha)
        ACC[pair, 2] += fold(by_n)
        return by_log

    def pull_back(step, dt, i):
        h, k, g, lam = HB[step, i], KB[step, i], GB[step, i], LAM[step, i]
        hu, hd = HB[step, i - 1], HB[step, i + 1]
        gu, gd = GB[step, i - 1], GB[step, i + 1]
        d_y = left(h) - h
        d_z = 1.0 + h - below(h)
        e_y = left(g) - g
        e_z = below(g) - g
        s_up, s_down = 0.5 * face(i - 1), 0.5 * face(i)
        c_y = right_half * d_y * e_y
        c_z = below_half * d_z * e_z
        grad_k = (
            s_down * ((hd - h) * (g - gd))
            + s_up * ((hu - h) * (g - gu))
            - (c_y + right(c_y))
            + (c_z + above(c_z))
            + forcing(step, i) * g
        )
        by_log = slopes(step, i, grad_k, -lam * (dt * AB[step, i]))
        if step == 0:
            return
        k_up = s_up * (KB[step, i - 1] + k)
        k_down = s_down * (k + KB[step, i + 1])
        f_y = right_half * (k + left(k)) * e_y
        f_z = below_half * (k + below(k)) * e_z
        lap = k_down * (gd - g) + k_up * (gu - g) + (f_y - right(f_y)) + (f_z - above(f_z))
        before = lam + lap + by_log / h
        LAM[0, i] = before
        GB[0, i] = before * dt0 * IC[0, i]

    over(own, functools.partial(pull_back, 1, dt1))

    GB[0, 0] = jnp.zeros((depth, width), F32)
    GB[0, rows + 1] = jnp.zeros((depth, width), F32)
    over(own, functools.partial(pull_back, 0, dt0))

    def pull_halo(i):
        near = jnp.where(i == 0, 1, rows)
        half = jnp.where(i == 0, 0.5 * lower_open, 0.5 * upper_open)
        slopes(0, i, half * ((HB[0, i] - HB[0, near]) * GB[0, near]), None)

    over(halo, pull_halo)

    zone_sums = None
    line = lax.broadcasted_iota(jnp.int32, (8, width), 0)
    for pair in range(4):
        sat, alpha, _ = params(2 * pair - 1)
        grads = [
            jnp.sum(ACC[pair, 0], axis=0, keepdims=True) / sat,
            jnp.sum(ACC[pair, 1], axis=0, keepdims=True) / alpha,
            jnp.sum(ACC[pair, 2], axis=0, keepdims=True),
        ]
        block = jnp.zeros((8, width), F32)
        for place, grad in enumerate(grads):
            block = jnp.where(line == place, grad, block)
        part = nt_dot(block, OH[pair], HIGHEST)
        zone_sums = part if zone_sums is None else zone_sums + part
    loss = 0.5 * (jnp.sum(ACC[4, 0], keepdims=True) + scale * spread_sum)
    if packed:
        lane = lax.broadcasted_iota(jnp.int32, (1, zp), 1) < period
        lines = [
            jnp.where(lane, zone_sums[0:1], zone_sums[1:2]),
            jnp.where(lane, zone_sums[2:3], loss),
        ]
    else:
        lines = [zone_sums[0:1], zone_sums[1:2], zone_sums[2:3], loss + jnp.zeros((1, zp), F32)]
    message = jnp.concatenate(lines, axis=0)

    def row_copy(k, src):
        return pltpu.make_async_remote_copy(
            src_ref=SUMR.at[src],
            dst_ref=SUMR.at[src],
            send_sem=sum_send.at[k],
            recv_sem=sum_recv.at[src],
            device_id=dev(lax.rem(pos + k, count)),
            device_id_type=pl.DeviceIdType.MESH,
        )

    def event_copy(k, src):
        return pltpu.make_async_remote_copy(
            src_ref=SUME.at[src],
            dst_ref=SUME.at[src],
            send_sem=ev_send.at[k],
            recv_sem=ev_recv.at[src],
            device_id=(lax.rem(me_event + k, groups), pos),
            device_id_type=pl.DeviceIdType.MESH,
        )

    def all_copy(k, src):
        return pltpu.make_async_remote_copy(
            src_ref=SUMR.at[src],
            dst_ref=SUMR.at[src],
            send_sem=sum_send.at[k],
            recv_sem=sum_recv.at[src],
            device_id=other(k),
            device_id_type=pl.DeviceIdType.MESH,
        )

    if direct:
        SUMR[index] = message
        for k in range(1, total_devices):
            all_copy(k, index).start()
        for k in range(1, total_devices):
            all_copy(k, lax.rem(index + k, total_devices)).wait_recv()
        small_ref[...] = jnp.sum(SUMR[...], axis=0)
    else:
        SUMR[pos] = message
        for k in range(1, count):
            row_copy(k, pos).start()
        for k in range(1, count):
            row_copy(k, lax.rem(pos + k, count)).wait_recv()
        SUME[me_event] = jnp.sum(SUMR[...], axis=0)
        for k in range(1, groups):
            event_copy(k, me_event).start()
        for k in range(1, groups):
            event_copy(k, lax.rem(me_event + k, groups)).wait_recv()
        small_ref[...] = jnp.sum(SUME[...], axis=0)

    for number in range(LINKS):
        sent_pair(number, *pairs[number])
    for k in range(1, count):
        max_copy(0, k).wait_send()
        max_copy(1, k).wait_send()
    if direct:
        for k in range(1, total_devices):
            all_copy(k, index).wait_send()
    else:
        for k in range(1, count):
            row_copy(k, pos).wait_send()
        for k in range(1, groups):
            event_copy(k, me_event).wait_send()


def local(
    initial_head,
    sat_conductivity,
    vg_alpha,
    vg_n,
    zone_map,
    forcing_plan,
    tensiometer_cells,
    tensiometer_heads,
):
    _, depth, rows, width = initial_head.shape
    zones = sat_conductivity.shape[0]
    zp = -(-zones // 128) * 128
    count = lax.axis_size("row")
    groups = lax.axis_size("event")
    sensors = tensiometer_cells.shape[1]
    lines = 2 if 2 * zones <= zp else 4
    senders = count * groups if count * groups <= DIRECT else count
    vmem = pl.BlockSpec(memory_space=pltpu.VMEM)
    smem = pl.BlockSpec(memory_space=pltpu.SMEM)
    full = pltpu.VMEM((STEPS, rows + 2, depth, width), F32)
    single = pltpu.VMEM((rows + 2, depth, width), F32)
    dma = pltpu.SemaphoreType.DMA
    head, small = pl.pallas_call(
        functools.partial(kernel, count, groups, groups * initial_head.shape[0]),
        out_shape=(
            jax.ShapeDtypeStruct((rows, depth, width), F32),
            jax.ShapeDtypeStruct((lines, zp), F32),
        ),
        in_specs=[vmem] * 5 + [smem] + [vmem] * 2,
        out_specs=(vmem, vmem),
        scratch_shapes=[
            full,
            full,
            full,
            full,
            full,
            full,
            full,
            full,
            full,
            full,
            full,
            single,
            single,
            pltpu.VMEM((4, 8, width), F32),
            pltpu.VMEM((8, zp), F32),
            pltpu.VMEM((4, zp, width), F32),
            pltpu.VMEM((2, 1, sensors), jnp.int32),
            pltpu.VMEM((2, 1, sensors), F32),
            pltpu.VMEM((2, 1, sensors), F32),
            pltpu.VMEM((2, 1, sensors), F32),
            pltpu.VMEM((STEPS, 8, width), F32),
            pltpu.VMEM((5, 3, 8, width), F32),
            pltpu.VMEM((STEPS, count, 8, 128), F32),
            pltpu.VMEM((senders, lines, zp), F32),
            pltpu.VMEM((groups, lines, zp), F32),
            dma((LINKS, 2)),
            dma((LINKS, 2)),
            dma((STEPS, count)),
            dma((STEPS, count)),
            dma((senders,)),
            dma((senders,)),
            dma((groups,)),
            dma((groups,)),
        ],
        compiler_params=pltpu.CompilerParams(
            collective_id=0, has_side_effects=True, vmem_limit_bytes=48 * 1024 * 1024
        ),
    )(
        initial_head[0],
        sat_conductivity[None],
        vg_alpha[None],
        vg_n[None],
        zone_map,
        forcing_plan[0],
        tensiometer_cells,
        tensiometer_heads,
    )
    final = jnp.transpose(head, (1, 0, 2))[None]
    if lines == 2:
        half = zp // 2
        grads = (small[0, :zones], small[0, half : half + zones], small[1, :zones])
        return (final, small[1, half], *grads)
    return (final, small[3, 0], small[0, :zones], small[1, :zones], small[2, :zones])


def solution(mesh):
    return jax.shard_map(
        local,
        mesh=mesh,
        in_specs=(
            P("event", None, "row", None),
            P(),
            P(),
            P(),
            P("row", None),
            P("event", None, "row"),
            P("event", "row"),
            P("event", "row"),
        ),
        out_specs=(P("event", None, "row", None), P(), P(), P(), P()),
        check_vma=False,
    )
```

```python
import functools

import jax
import jax.numpy as jnp
from jax import lax
from jax.experimental import pallas as pl
from jax.experimental.pallas import tpu as pltpu
from jax.sharding import PartitionSpec as P

STEPS = 2
CFL = 0.4
IRRIGATION = 0.2
WATER_RANGE = 0.35
HIGHEST = lax.Precision.HIGHEST
F32 = jnp.float32
BF16 = jnp.bfloat16
LAYERS = 16
PAD = 8
LINKS = 6
DIRECT = 64


def nt_dot(a, b):
    return lax.dot_general(a, b, (((1,), (1,)), ((), ())), preferred_element_type=F32)


def pieces(t):
    one = t.astype(BF16).astype(F32)
    two = (t - one).astype(BF16).astype(F32)
    return one, two, t - one - two


def three(t, product):
    size = t.shape[0]
    out = product(jnp.concatenate(pieces(t), axis=0).astype(BF16))
    return out[:size] + out[size : 2 * size] + out[2 * size :]


def fold(x):
    return jnp.sum(x.reshape(x.shape[0] // 8, 8, x.shape[1]), axis=0)


def kernel(
    count,
    groups,
    events,
    x_ref,
    sat_ref,
    alpha_ref,
    n_ref,
    zone_ref,
    plan_ref,
    cells_ref,
    heads_ref,
    out_ref,
    small_ref,
    HB,
    KB,
    AB,
    IC,
    LG,
    LV,
    WW,
    RV,
    QQ,
    GB,
    LAM,
    WB,
    TM,
    PB,
    TAB,
    OH,
    NC,
    NT,
    SV,
    NV,
    XV,
    RATE,
    ACC,
    MX,
    SUMR,
    SUME,
    link_send,
    link_recv,
    max_send,
    max_recv,
    sum_send,
    sum_recv,
    ev_send,
    ev_recv,
    x_sem,
):
    fetch = pltpu.make_async_copy(x_ref, XV, x_sem)
    fetch.start()
    depth, rows, width = x_ref.shape
    zp = OH.shape[1]
    zones = sat_ref.shape[1]
    pos = lax.axis_index("row")
    me_event = lax.axis_index("event")
    up, down = pos - 1, pos + 1
    has_up, has_down = pos > 0, pos < count - 1
    lower_open = has_up.astype(F32)
    upper_open = has_down.astype(F32)

    def dev(row):
        return (me_event, row)

    total_devices = count * groups
    direct = total_devices <= DIRECT
    index = me_event * count + pos

    def other(k):
        at = lax.rem(index + k, total_devices)
        return at // count, lax.rem(at, count)

    barrier = pltpu.get_barrier_semaphore()
    if direct:
        greeted = [other(k) for k in range(1, total_devices)]
    else:
        greeted = [dev(lax.rem(pos + k, count)) for k in range(1, count)]
        greeted += [(lax.rem(me_event + k, groups), pos) for k in range(1, groups)]
    for device in greeted:
        pl.semaphore_signal(barrier, 1, device_id=device, device_id_type=pl.DeviceIdType.MESH)

    deep = pl.ds(PAD, depth)

    def link(number, side, src, dst):
        return pltpu.make_async_remote_copy(
            src_ref=src,
            dst_ref=dst,
            send_sem=link_send.at[number, side],
            recv_sem=link_recv.at[number, side],
            device_id=dev(up if side == 0 else down),
            device_id_type=pl.DeviceIdType.MESH,
        )

    def start_pair(number, to_up, to_down):
        @pl.when(has_up)
        def _():
            link(number, 0, *to_up).start()

        @pl.when(has_down)
        def _():
            link(number, 1, *to_down).start()

    def recv_pair(number, to_up, to_down):
        @pl.when(has_down)
        def _():
            link(number, 0, *to_up).wait_recv()

        @pl.when(has_up)
        def _():
            link(number, 1, *to_down).wait_recv()

    def sent_pair(number, to_up, to_down):
        @pl.when(has_up)
        def _():
            link(number, 0, *to_up).wait_send()

        @pl.when(has_down)
        def _():
            link(number, 1, *to_down).wait_send()

    pairs = [
        ((HB.at[0, 1, deep], HB.at[0, rows + 1, deep]), (HB.at[0, rows, deep], HB.at[0, 0, deep])),
        ((PB.at[1], PB.at[3]), (PB.at[2], PB.at[0])),
        ((cells_ref, NC.at[1]), (cells_ref, NC.at[0])),
        ((heads_ref, NT.at[1]), (heads_ref, NT.at[0])),
        ((AB.at[0, 1], AB.at[0, rows + 1]), (AB.at[0, rows], AB.at[0, 0])),
        ((SV.at[0], NV.at[1]), (SV.at[1], NV.at[0])),
    ]

    def start(number):
        start_pair(number, *pairs[number])

    def recv(number):
        recv_pair(number, *pairs[number])

    TAB[...] = jnp.zeros_like(TAB)
    TAB[0:1, :zones] = sat_ref[...]
    TAB[1:2, :zones] = alpha_ref[...]
    TAB[2:3, :zones] = n_ref[...]
    blocks = zone_ref.shape[1]
    spread = (
        lax.broadcasted_iota(jnp.int32, (blocks, width), 1) // 2
        == lax.broadcasted_iota(jnp.int32, (blocks, width), 0)
    ).astype(F32)
    exact = None if zones <= 256 else HIGHEST
    ids = jnp.dot(
        zone_ref[...].astype(F32), spread, preferred_element_type=F32, precision=exact
    )
    packed = 2 * zones <= zp
    period = zp // 2 if packed else zp
    zone_of = (lax.broadcasted_iota(jnp.int32, (zp, width), 0) % period).astype(F32)
    part_line = lax.broadcasted_iota(jnp.int32, (8, width), 0)
    for pair in range(2):
        own_ids = ids[pair : pair + 1]
        OH[pair + 1] = jnp.where(zone_of == own_ids, 1.0, 0.0).astype(BF16)
        block = three(TAB[...], lambda t: jnp.dot(t, OH[pair + 1], preferred_element_type=F32))
        PB[pair + 1] = jnp.where(part_line == 3, own_ids, block)
    for ref in (HB, KB, GB):
        for step in range(STEPS):
            for i in range(1, rows + 1):
                ref[step, i, 0:PAD] = jnp.zeros((PAD, width), F32)
                ref[step, i, PAD + depth :] = jnp.zeros((PAD, width), F32)
    fetch.wait()
    for i in range(rows):
        HB[0, i + 1, deep] = XV[:, i, :]
    pl.semaphore_wait(barrier, len(greeted))
    start(0)
    start(1)
    start(2)
    start(3)

    @pl.when(jnp.logical_not(has_up))
    def _():
        HB[0, 0, deep] = HB[0, 1, deep]
        PB[0] = PB[1]
        NC[0] = cells_ref[...]
        NT[0] = heads_ref[...]
        NV[0] = jnp.zeros_like(NV[0])
        AB[0, 0] = jnp.zeros((depth, width), F32)

    @pl.when(jnp.logical_not(has_down))
    def _():
        HB[0, rows + 1, deep] = HB[0, rows, deep]
        PB[3] = PB[2]
        NC[1] = cells_ref[...]
        NT[1] = heads_ref[...]
        NV[1] = jnp.zeros_like(NV[1])
        AB[0, rows + 1] = jnp.zeros((depth, width), F32)

    ACC[...] = jnp.zeros_like(ACC)

    column = lax.broadcasted_iota(jnp.int32, (1, width), 1)
    layer = lax.broadcasted_iota(jnp.int32, (depth, 1), 0)
    right_half = jnp.where(column < width - 1, 0.5, 0.0)
    chunk_layer = lax.broadcasted_iota(jnp.int32, (LAYERS, 1), 0)

    class Chunk:
        def __init__(self, first):
            last = first + LAYERS == depth
            self.bare = pl.ds(first, LAYERS)
            self.here = pl.ds(PAD + first, LAYERS)
            self.above = pl.ds(PAD + first - 1, LAYERS)
            self.below = pl.ds(PAD + first + 1, LAYERS)
            self.top = chunk_layer == 0 if first == 0 else None
            self.bottom = chunk_layer == LAYERS - 1 if last else None
            self.half_above = 0.5 if self.top is None else jnp.where(self.top, 0.0, 0.5)
            self.half_below = 0.5 if self.bottom is None else jnp.where(self.bottom, 0.0, 0.5)

        def forcing(self, level, v):
            out = 0.0
            if self.top is not None:
                out = out + jnp.where(self.top, level * IRRIGATION, 0.0) * v
            if self.bottom is not None:
                out = out - jnp.where(self.bottom, v, 0.0)
            return out

        def ends(self, v):
            out = 0.0
            if self.top is not None:
                out = out + jnp.where(self.top, v, 0.0)
            if self.bottom is not None:
                out = out + jnp.where(self.bottom, v, 0.0)
            return out

    chunks = [Chunk(first) for first in range(0, depth, LAYERS)]

    def left(v):
        return pltpu.roll(v, width - 1, 1)

    def right(v):
        return pltpu.roll(v, 1, 1)

    def over(indices, body):
        first, stride, number = indices

        def go(j, carry):
            body(first + stride * j)
            return carry

        lax.fori_loop(0, number, go, 0)

    own = (1, 1, rows)
    inner = (2, 1, rows - 2)
    edges = (1, rows - 1, 2)
    halo = (0, rows + 1, 2)

    def params(i):
        block = PB[(i + 1) // 2]
        return block[0:1], block[1:2], block[2:3]

    def face(i):
        return jnp.where(i == 0, lower_open, jnp.where(i == rows, upper_open, 1.0))

    def level_of(step, i):
        return jnp.where(i > 2, plan_ref[step, 1], plan_ref[step, 0]).astype(F32)

    def cell(step, i):
        sat, alpha, n = params(i)
        m = 1.0 - 1.0 / n
        n1 = n - 1.0
        half_m = -0.5 * m
        scale = WATER_RANGE * n1 * alpha
        for c in chunks:
            if step == 0:
                head = HB[0, i, c.here]
            else:
                head = HB[0, i, c.here] + dt0 * AB[0, i, c.bare]
                HB[1, i, c.here] = head
            x = alpha * -head
            log_x = jnp.log(x)
            power = jnp.exp(n1 * log_x)
            v = 1.0 + x * power
            log_v = jnp.log(v)
            root = jnp.exp(half_m * log_v)
            w = power * (root * root)
            rest = 1.0 - w
            q = sat * root * rest
            KB[step, i, c.here] = q * rest
            IC[step, i, c.bare] = v / (scale * w)
            LG[step, i, c.bare] = log_x
            LV[step, i, c.bare] = log_v
            WW[step, i, c.bare] = w
            RV[step, i, c.bare] = 1.0 / v
            QQ[step, i, c.bare] = q

    def flow(step, i):
        s_up, s_down = 0.5 * face(i - 1), 0.5 * face(i)
        level = level_of(step, i)
        top_rate = None
        for c in chunks:
            h, k = HB[step, i, c.here], KB[step, i, c.here]
            inv = IC[step, i, c.bare]
            k_up = s_up * (KB[step, i - 1, c.here] + k)
            k_down = s_down * (k + KB[step, i + 1, c.here])
            k_y = right_half * (k + left(k))
            f_y = k_y * (left(h) - h)
            k_above = c.half_above * (KB[step, i, c.above] + k)
            k_below = c.half_below * (k + KB[step, i, c.below])
            net = (
                k_down * (HB[step, i + 1, c.here] - h)
                + k_up * (HB[step, i - 1, c.here] - h)
                + (f_y - right(f_y))
                + k_above * (1.0 + HB[step, i, c.above] - h)
                - k_below * (1.0 + h - HB[step, i, c.below])
                + c.forcing(level, k)
            )
            total = k_up + k_down + (k_y + right(k_y)) + (k_above + k_below) + c.ends(k)
            AB[step, i, c.bare] = net * inv
            rate = jnp.max((total * inv).reshape(LAYERS // 8, 8, width), axis=0)
            top_rate = rate if top_rate is None else jnp.maximum(top_rate, rate)
        RATE[step] = jnp.maximum(RATE[step], top_rate)

    def max_copy(step, k):
        return pltpu.make_async_remote_copy(
            src_ref=MX.at[step, pos],
            dst_ref=MX.at[step, pos],
            send_sem=max_send.at[step, k],
            recv_sem=max_recv.at[step, pos],
            device_id=dev(lax.rem(pos + k, count)),
            device_id_type=pl.DeviceIdType.MESH,
        )

    def max_got(step, k):
        src = lax.rem(pos + k, count)
        return pltpu.make_async_remote_copy(
            src_ref=MX.at[step, src],
            dst_ref=MX.at[step, src],
            send_sem=max_send.at[step, k],
            recv_sem=max_recv.at[step, src],
            device_id=dev(src),
            device_id_type=pl.DeviceIdType.MESH,
        )

    def send_rate(step):
        rate = RATE[step]
        tile = rate[:, :128]
        for start_lane in range(128, width, 128):
            tile = jnp.maximum(tile, rate[:, start_lane : start_lane + 128])
        MX[step, pos] = tile
        for k in range(1, count):
            max_copy(step, k).start()

    def step_size(step):
        for k in range(1, count):
            max_got(step, k).wait_recv()
        top = jnp.max(MX[step], axis=0)
        return CFL / jnp.max(top, keepdims=True)

    RATE[...] = jnp.zeros_like(RATE)

    def first_cell(i):
        cell(0, i)

    over(own, first_cell)
    over(inner, functools.partial(flow, 0))
    recv(0)
    recv(1)
    over(halo, first_cell)
    over(edges, functools.partial(flow, 0))
    send_rate(0)
    start(4)

    for pair in (0, 3):
        OH[pair] = jnp.where(zone_of == PB[pair][3:4], 1.0, 0.0).astype(BF16)

    def places(cells):
        index = cells.astype(F32)
        line = jnp.floor((index + 0.5) * (1.0 / width))
        col = index - width * line
        level = jnp.floor((line + 0.5) * (1.0 / rows))
        return level, line - rows * level, col

    sensors = cells_ref.shape[1]
    col_of = lax.broadcasted_iota(jnp.int32, (width, sensors), 0).astype(F32)

    def counts(cells, targets, wanted):
        level, row, col = places(cells)
        cols16 = jnp.where(col_of == col, 1.0, 0.0).astype(BF16)
        if wanted is None:
            spot = row * depth + level
            lines = rows * depth
        else:
            spot = jnp.where(row == wanted, level, -1.0)
            lines = depth
        line_of = lax.broadcasted_iota(jnp.int32, (lines, sensors), 0).astype(F32)
        hit = line_of == spot
        parts = [jnp.ones_like(targets), *pieces(targets)]
        out = nt_dot(stack(hit, parts), cols16)
        number = out[:lines]
        total = out[lines : 2 * lines] + out[2 * lines : 3 * lines] + out[3 * lines :]
        return number, total / jnp.maximum(number, 1.0), hit, cols16

    def stack(hit, parts):
        return jnp.concatenate([jnp.where(hit, part, 0.0) for part in parts], axis=0).astype(BF16)

    def put(values, hit, cols16):
        lines = hit.shape[0]
        out = nt_dot(stack(hit, pieces(values)), cols16)
        return out[:lines] + out[lines : 2 * lines] + out[2 * lines :]

    def take(field, hit, cols16):
        at_sensor = three(field, lambda t: jnp.dot(t, cols16, preferred_element_type=F32))
        return jnp.where(hit, at_sensor, 0.0)

    def column_sum(v):
        return jnp.sum(v, axis=0, keepdims=True)

    number, mean, own_hit, own_cols = counts(cells_ref[...], heads_ref[...], None)
    WB[1 : rows + 1] = number.reshape(rows, depth, width)
    TM[1 : rows + 1] = mean.reshape(rows, depth, width)
    recv(2)
    recv(3)
    halo_spots = []
    for side, wanted, place in ((0, rows - 1, 0), (1, 0, rows + 1)):
        number, mean, hit, cols = counts(NC[side], NT[side], wanted)
        WB[place] = number
        TM[place] = mean
        halo_spots.append((side, place, hit, cols))

    dt0 = step_size(0)

    def next_cell(i):
        cell(1, i)

    over(own, next_cell)
    over(inner, functools.partial(flow, 1))
    recv(4)
    over(halo, next_cell)
    over(edges, functools.partial(flow, 1))
    send_rate(1)
    brims = jnp.concatenate([AB[1, 1], AB[1, rows]], axis=0)
    brim_hit = jnp.concatenate([own_hit[:depth], own_hit[(rows - 1) * depth :]], axis=0)
    picked = take(brims, brim_hit, own_cols)
    SV[0] = column_sum(picked[:depth])
    SV[1] = column_sum(picked[depth:])
    start(5)
    own_mean = column_sum(take(TM[1 : rows + 1].reshape(rows * depth, width), own_hit, own_cols))
    spread_sum = jnp.sum((heads_ref[...] - own_mean) ** 2, keepdims=True)
    recv(5)
    for side, place, hit, cols in halo_spots:
        AB[1, place] = put(NV[side], hit, cols) / jnp.maximum(WB[place], 1.0)
    dt1 = step_size(1)
    scale = 1.0 / events

    def last_head(i):
        head = HB[1, i, deep] + dt1 * AB[1, i]
        off = head - TM[i]
        pull = (scale * WB[i]) * off
        GB[1, i, deep] = pull * dt1 * IC[1, i]
        return head, off * pull, pull

    def finish(i):
        head, square, pull = last_head(i)
        out_ref[i - 1] = head
        LAM[1, i] = pull
        ACC[4, 0] += fold(square)

    over(own, finish)
    over(halo, lambda i: (last_head(i), None)[1])

    def slopes(step, i, grad_k_of, change_of):
        _, _, n = params(i)
        n1 = n - 1.0
        m = 1.0 - 1.0 / n
        inv_n2 = 1.0 / (n * n)
        inv_n1 = 1.0 / n1
        half_n1 = 0.5 * n1
        sums = None
        for c in chunks:
            k, log_x, log_v = KB[step, i, c.here], LG[step, i, c.bare], LV[step, i, c.bare]
            w, r = WW[step, i, c.bare], RV[step, i, c.bare]
            grad_k = grad_k_of(c)
            f = 1.0 - r
            wq = 2.0 * w * QQ[step, i, c.bare]
            n1r = n1 * r
            fl = f * log_x
            log_v = inv_n2 * log_v
            mfl = m * fl
            d_w = log_x - log_v - mfl
            by_log = -grad_k * (half_n1 * (f * k) + n1r * wq)
            by_n = -grad_k * ((0.5 * k) * (log_v + mfl) + wq * d_w)
            by_alpha = by_log
            if change_of is not None:
                change = change_of(c)
                by_log = by_log + change * (n1r - n * f)
                by_n = by_n + change * (inv_n1 + d_w - fl)
                by_alpha = by_log + change
            parts = [fold(grad_k * k), fold(by_alpha), fold(by_n)]
            sums = parts if sums is None else [a + b for a, b in zip(sums, parts)]
            yield c, by_log
        pair = (i + 1) // 2
        for place in range(3):
            ACC[pair, place] += sums[place]

    def pull_back(step, dt, i):
        s_up, s_down = 0.5 * face(i - 1), 0.5 * face(i)
        level = level_of(step, i)

        def grad_k_of(c):
            h, g = HB[step, i, c.here], GB[step, i, c.here]
            c_y = right_half * (left(h) - h) * (left(g) - g)
            return (
                s_down * ((HB[step, i + 1, c.here] - h) * (g - GB[step, i + 1, c.here]))
                + s_up * ((HB[step, i - 1, c.here] - h) * (g - GB[step, i - 1, c.here]))
                - (c_y + right(c_y))
                + c.half_above * (1.0 + HB[step, i, c.above] - h) * (g - GB[step, i, c.above])
                + c.half_below * (1.0 + h - HB[step, i, c.below]) * (GB[step, i, c.below] - g)
                + c.forcing(level, g)
            )

        def change_of(c):
            return -LAM[step, i, c.bare] * (dt * AB[step, i, c.bare])

        for c, by_log in slopes(step, i, grad_k_of, change_of):
            if step == 0:
                continue
            h, k, g = HB[step, i, c.here], KB[step, i, c.here], GB[step, i, c.here]
            f_y = right_half * (k + left(k)) * (left(g) - g)
            lap = (
                s_down * (k + KB[step, i + 1, c.here]) * (GB[step, i + 1, c.here] - g)
                + s_up * (KB[step, i - 1, c.here] + k) * (GB[step, i - 1, c.here] - g)
                + (f_y - right(f_y))
                + c.half_above * (KB[step, i, c.above] + k) * (GB[step, i, c.above] - g)
                + c.half_below * (k + KB[step, i, c.below]) * (GB[step, i, c.below] - g)
            )
            before = LAM[step, i, c.bare] + lap + by_log / h
            LAM[0, i, c.bare] = before
            GB[0, i, c.here] = before * dt0 * IC[0, i, c.bare]

    over(own, functools.partial(pull_back, 1, dt1))

    GB[0, 0] = jnp.zeros_like(GB[0, 0])
    GB[0, rows + 1] = jnp.zeros_like(GB[0, 0])
    over(own, functools.partial(pull_back, 0, dt0))

    def pull_halo(i):
        near = jnp.where(i == 0, 1, rows)
        half = jnp.where(i == 0, 0.5 * lower_open, 0.5 * upper_open)

        def grad_k_of(c):
            return half * ((HB[0, i, c.here] - HB[0, near, c.here]) * GB[0, near, c.here])

        for _ in slopes(0, i, grad_k_of, None):
            pass

    over(halo, pull_halo)

    zone_sums = None
    line = lax.broadcasted_iota(jnp.int32, (8, width), 0)
    for pair in range(4):
        sat, alpha, _ = params(2 * pair - 1)
        grads = [
            jnp.sum(ACC[pair, 0], axis=0, keepdims=True) / sat,
            jnp.sum(ACC[pair, 1], axis=0, keepdims=True) / alpha,
            jnp.sum(ACC[pair, 2], axis=0, keepdims=True),
        ]
        block = jnp.zeros((8, width), F32)
        for place, grad in enumerate(grads):
            block = jnp.where(line == place, grad, block)
        part = three(block, lambda t: nt_dot(t, OH[pair]))
        zone_sums = part if zone_sums is None else zone_sums + part
    loss = 0.5 * (jnp.sum(ACC[4, 0], keepdims=True) + scale * spread_sum)
    if packed:
        lane = lax.broadcasted_iota(jnp.int32, (1, zp), 1) < period
        lines = [
            jnp.where(lane, zone_sums[0:1], zone_sums[1:2]),
            jnp.where(lane, zone_sums[2:3], loss),
        ]
    else:
        lines = [zone_sums[0:1], zone_sums[1:2], zone_sums[2:3], loss + jnp.zeros((1, zp), F32)]
    message = jnp.concatenate(lines, axis=0)

    def row_copy(k, src):
        return pltpu.make_async_remote_copy(
            src_ref=SUMR.at[src],
            dst_ref=SUMR.at[src],
            send_sem=sum_send.at[k],
            recv_sem=sum_recv.at[src],
            device_id=dev(lax.rem(pos + k, count)),
            device_id_type=pl.DeviceIdType.MESH,
        )

    def event_copy(k, src):
        return pltpu.make_async_remote_copy(
            src_ref=SUME.at[src],
            dst_ref=SUME.at[src],
            send_sem=ev_send.at[k],
            recv_sem=ev_recv.at[src],
            device_id=(lax.rem(me_event + k, groups), pos),
            device_id_type=pl.DeviceIdType.MESH,
        )

    def all_copy(k, src):
        return pltpu.make_async_remote_copy(
            src_ref=SUMR.at[src],
            dst_ref=SUMR.at[src],
            send_sem=sum_send.at[k],
            recv_sem=sum_recv.at[src],
            device_id=other(k),
            device_id_type=pl.DeviceIdType.MESH,
        )

    if direct:
        SUMR[index] = message
        for k in range(1, total_devices):
            all_copy(k, index).start()
        for k in range(1, total_devices):
            all_copy(k, lax.rem(index + k, total_devices)).wait_recv()
        small_ref[...] = jnp.sum(SUMR[...], axis=0)
    else:
        SUMR[pos] = message
        for k in range(1, count):
            row_copy(k, pos).start()
        for k in range(1, count):
            row_copy(k, lax.rem(pos + k, count)).wait_recv()
        SUME[me_event] = jnp.sum(SUMR[...], axis=0)
        for k in range(1, groups):
            event_copy(k, me_event).start()
        for k in range(1, groups):
            event_copy(k, lax.rem(me_event + k, groups)).wait_recv()
        small_ref[...] = jnp.sum(SUME[...], axis=0)

    for number in range(LINKS):
        sent_pair(number, *pairs[number])
    for k in range(1, count):
        max_copy(0, k).wait_send()
        max_copy(1, k).wait_send()
    if direct:
        for k in range(1, total_devices):
            all_copy(k, index).wait_send()
    else:
        for k in range(1, count):
            row_copy(k, pos).wait_send()
        for k in range(1, groups):
            event_copy(k, me_event).wait_send()


def local(
    initial_head,
    sat_conductivity,
    vg_alpha,
    vg_n,
    zone_map,
    forcing_plan,
    tensiometer_cells,
    tensiometer_heads,
):
    _, depth, rows, width = initial_head.shape
    zones = sat_conductivity.shape[0]
    zp = -(-zones // 128) * 128
    count = lax.axis_size("row")
    groups = lax.axis_size("event")
    sensors = tensiometer_cells.shape[1]
    lines = 2 if 2 * zones <= zp else 4
    senders = count * groups if count * groups <= DIRECT else count
    vmem = pl.BlockSpec(memory_space=pltpu.VMEM)
    smem = pl.BlockSpec(memory_space=pltpu.SMEM)
    deep = pltpu.VMEM((STEPS, rows + 2, depth + 2 * PAD, width), F32)
    full = pltpu.VMEM((STEPS, rows + 2, depth, width), F32)
    single = pltpu.VMEM((rows + 2, depth, width), F32)
    dma = pltpu.SemaphoreType.DMA
    head, small = pl.pallas_call(
        functools.partial(kernel, count, groups, groups * initial_head.shape[0]),
        out_shape=(
            jax.ShapeDtypeStruct((rows, depth, width), F32),
            jax.ShapeDtypeStruct((lines, zp), F32),
        ),
        in_specs=[pl.BlockSpec(memory_space=pl.ANY)] + [vmem] * 4 + [smem] + [vmem] * 2,
        out_specs=(vmem, vmem),
        scratch_shapes=[
            deep,
            deep,
            full,
            full,
            full,
            full,
            full,
            full,
            full,
            deep,
            full,
            single,
            single,
            pltpu.VMEM((4, 8, width), F32),
            pltpu.VMEM((8, zp), F32),
            pltpu.VMEM((4, zp, width), BF16),
            pltpu.VMEM((2, 1, sensors), jnp.int32),
            pltpu.VMEM((2, 1, sensors), F32),
            pltpu.VMEM((2, 1, sensors), F32),
            pltpu.VMEM((2, 1, sensors), F32),
            pltpu.VMEM((depth, rows, width), F32),
            pltpu.VMEM((STEPS, 8, width), F32),
            pltpu.VMEM((5, 3, 8, width), F32),
            pltpu.VMEM((STEPS, count, 8, 128), F32),
            pltpu.VMEM((senders, lines, zp), F32),
            pltpu.VMEM((groups, lines, zp), F32),
            dma((LINKS, 2)),
            dma((LINKS, 2)),
            dma((STEPS, count)),
            dma((STEPS, count)),
            dma((senders,)),
            dma((senders,)),
            dma((groups,)),
            dma((groups,)),
            dma,
        ],
        compiler_params=pltpu.CompilerParams(
            collective_id=0, has_side_effects=True, vmem_limit_bytes=48 * 1024 * 1024
        ),
    )(
        initial_head[0],
        sat_conductivity[None],
        vg_alpha[None],
        vg_n[None],
        zone_map,
        forcing_plan[0],
        tensiometer_cells,
        tensiometer_heads,
    )
    final = jnp.transpose(head, (1, 0, 2))[None]
    if lines == 2:
        half = zp // 2
        grads = (small[0, :zones], small[0, half : half + zones], small[1, :zones])
        return (final, small[1, half], *grads)
    return (final, small[3, 0], small[0, :zones], small[1, :zones], small[2, :zones])


def solution(mesh):
    return jax.shard_map(
        local,
        mesh=mesh,
        in_specs=(
            P("event", None, "row", None),
            P(),
            P(),
            P(),
            P("row", None),
            P("event", None, "row"),
            P("event", "row"),
            P("event", "row"),
        ),
        out_specs=(P("event", None, "row", None), P(), P(), P(), P()),
        check_vma=False,
    )
```

```python
import functools

import jax
import jax.numpy as jnp
from jax import lax
from jax.experimental import pallas as pl
from jax.experimental.pallas import tpu as pltpu
from jax.sharding import PartitionSpec as P

STEPS = 2
CFL = 0.4
IRRIGATION = 0.2
WATER_RANGE = 0.35
HIGHEST = lax.Precision.HIGHEST
F32 = jnp.float32
BF16 = jnp.bfloat16
LAYERS = 16
PAD = 8
LINKS = 6
DIRECT = 64
VMEM_BYTES = 63 * 1024 * 1024


def nt_dot(a, b):
    return lax.dot_general(a, b, (((1,), (1,)), ((), ())), preferred_element_type=F32)


def pieces(t):
    one = t.astype(BF16).astype(F32)
    two = (t - one).astype(BF16).astype(F32)
    return one, two, t - one - two


def three(t, product):
    size = t.shape[0]
    out = product(jnp.concatenate(pieces(t), axis=0).astype(BF16))
    return out[:size] + out[size : 2 * size] + out[2 * size :]


def fold(x):
    return jnp.sum(x.reshape(x.shape[0] // 8, 8, x.shape[1]), axis=0)


def kernel(
    count,
    groups,
    events,
    x_hbm,
    sat_hbm,
    alpha_hbm,
    n_hbm,
    zone_hbm,
    plan_hbm,
    cells_hbm,
    heads_hbm,
    out_hbm,
    small_ref,
    HB,
    KB,
    AB,
    IC,
    LG,
    LV,
    WW,
    RV,
    QQ,
    GB,
    LAM,
    WB,
    TM,
    PB,
    TAB,
    OH,
    NC,
    NT,
    SV,
    NV,
    XV,
    OUT,
    sat_ref,
    alpha_ref,
    n_ref,
    zone_ref,
    plan_ref,
    cells_ref,
    heads_ref,
    RATE,
    ACC,
    MX,
    SUMR,
    SUME,
    link_send,
    link_recv,
    max_send,
    max_recv,
    sum_send,
    sum_recv,
    ev_send,
    ev_recv,
    x_sem,
):
    fetches = [
        pltpu.make_async_copy(src, dst, x_sem.at[place])
        for place, (src, dst) in enumerate(
            (
                (zone_hbm, zone_ref),
                (sat_hbm, sat_ref),
                (alpha_hbm, alpha_ref),
                (n_hbm, n_ref),
                (x_hbm, XV),
                (cells_hbm, cells_ref),
                (heads_hbm, heads_ref),
                (plan_hbm, plan_ref),
            )
        )
    ]
    for fetch in fetches:
        fetch.start()
    depth, rows, width = XV.shape
    zp = OH.shape[1]
    zones = sat_ref.shape[1]
    pos = lax.axis_index("row")
    me_event = lax.axis_index("event")
    up, down = pos - 1, pos + 1
    has_up, has_down = pos > 0, pos < count - 1
    lower_open = has_up.astype(F32)
    upper_open = has_down.astype(F32)

    def dev(row):
        return (me_event, row)

    total_devices = count * groups
    direct = total_devices <= DIRECT
    index = me_event * count + pos

    def ring(at, size):
        return [at] + [
            jnp.where(at + k >= size, at + k - size, at + k) for k in range(1, size)
        ]

    row_ring, event_ring = ring(pos, count), ring(me_event, groups)
    others = [(e, r) for r in row_ring for e in event_ring][1:]
    row_others = [(me_event, r) for r in row_ring[1:]]
    event_others = [(e, pos) for e in event_ring[1:]]

    def place_of(device):
        return device[0] * count + device[1]

    barrier = pltpu.get_barrier_semaphore()
    greeted = others if direct else row_others + event_others
    for device in greeted:
        pl.semaphore_signal(barrier, 1, device_id=device, device_id_type=pl.DeviceIdType.MESH)

    deep = pl.ds(PAD, depth)

    def link(number, side, src, dst):
        return pltpu.make_async_remote_copy(
            src_ref=src,
            dst_ref=dst,
            send_sem=link_send.at[number, side],
            recv_sem=link_recv.at[number, side],
            device_id=dev(up if side == 0 else down),
            device_id_type=pl.DeviceIdType.MESH,
        )

    def start_pair(number, to_up, to_down):
        @pl.when(has_up)
        def _():
            link(number, 0, *to_up).start()

        @pl.when(has_down)
        def _():
            link(number, 1, *to_down).start()

    def recv_pair(number, to_up, to_down):
        @pl.when(has_down)
        def _():
            link(number, 0, *to_up).wait_recv()

        @pl.when(has_up)
        def _():
            link(number, 1, *to_down).wait_recv()

    def sent_pair(number, to_up, to_down):
        @pl.when(has_up)
        def _():
            link(number, 0, *to_up).wait_send()

        @pl.when(has_down)
        def _():
            link(number, 1, *to_down).wait_send()

    pairs = [
        ((HB.at[0, 1, deep], HB.at[0, rows + 1, deep]), (HB.at[0, rows, deep], HB.at[0, 0, deep])),
        ((PB.at[1], PB.at[3]), (PB.at[2], PB.at[0])),
        ((cells_ref, NC.at[1]), (cells_ref, NC.at[0])),
        ((heads_ref, NT.at[1]), (heads_ref, NT.at[0])),
        ((AB.at[0, 1], AB.at[0, rows + 1]), (AB.at[0, rows], AB.at[0, 0])),
        ((SV.at[0], NV.at[1]), (SV.at[1], NV.at[0])),
    ]

    def start(number):
        start_pair(number, *pairs[number])

    def recv(number):
        recv_pair(number, *pairs[number])

    for fetch in fetches[:4]:
        fetch.wait()
    TAB[...] = jnp.zeros_like(TAB)
    TAB[0:1, :zones] = sat_ref[...]
    TAB[1:2, :zones] = alpha_ref[...]
    TAB[2:3, :zones] = n_ref[...]
    blocks = zone_ref.shape[1]
    spread = (
        lax.broadcasted_iota(jnp.int32, (blocks, width), 1) // 2
        == lax.broadcasted_iota(jnp.int32, (blocks, width), 0)
    ).astype(F32)
    exact = None if zones <= 256 else HIGHEST
    ids = jnp.dot(
        zone_ref[...].astype(F32), spread, preferred_element_type=F32, precision=exact
    )
    packed = 2 * zones <= zp
    period = zp // 2 if packed else zp
    zone_of = (lax.broadcasted_iota(jnp.int32, (zp, width), 0) % period).astype(F32)
    part_line = lax.broadcasted_iota(jnp.int32, (8, width), 0)
    for pair in range(2):
        own_ids = ids[pair : pair + 1]
        OH[pair + 1] = jnp.where(zone_of == own_ids, 1.0, 0.0).astype(BF16)
        block = three(TAB[...], lambda t: jnp.dot(t, OH[pair + 1], preferred_element_type=F32))
        PB[pair + 1] = jnp.where(part_line == 3, own_ids, block)
    for ref in (HB, KB, GB):
        for step in range(STEPS):
            for i in range(1, rows + 1):
                ref[step, i, 0:PAD] = jnp.zeros((PAD, width), F32)
                ref[step, i, PAD + depth :] = jnp.zeros((PAD, width), F32)
    for fetch in fetches[4:]:
        fetch.wait()
    for i in range(rows):
        HB[0, i + 1, deep] = XV[:, i, :]
    pl.semaphore_wait(barrier, len(greeted))
    start(0)
    start(1)
    start(2)
    start(3)

    @pl.when(jnp.logical_not(has_up))
    def _():
        HB[0, 0, deep] = HB[0, 1, deep]
        PB[0] = PB[1]
        NC[0] = cells_ref[...]
        NT[0] = heads_ref[...]
        NV[0] = jnp.zeros_like(NV[0])
        AB[0, 0] = jnp.zeros((depth, width), F32)

    @pl.when(jnp.logical_not(has_down))
    def _():
        HB[0, rows + 1, deep] = HB[0, rows, deep]
        PB[3] = PB[2]
        NC[1] = cells_ref[...]
        NT[1] = heads_ref[...]
        NV[1] = jnp.zeros_like(NV[1])
        AB[0, rows + 1] = jnp.zeros((depth, width), F32)

    ACC[...] = jnp.zeros_like(ACC)

    column = lax.broadcasted_iota(jnp.int32, (1, width), 1)
    layer = lax.broadcasted_iota(jnp.int32, (depth, 1), 0)
    right_half = jnp.where(column < width - 1, 0.5, 0.0)
    chunk_layer = lax.broadcasted_iota(jnp.int32, (LAYERS, 1), 0)

    class Chunk:
        def __init__(self, first):
            last = first + LAYERS == depth
            self.bare = pl.ds(first, LAYERS)
            self.here = pl.ds(PAD + first, LAYERS)
            self.above = pl.ds(PAD + first - 1, LAYERS)
            self.below = pl.ds(PAD + first + 1, LAYERS)
            self.top = chunk_layer == 0 if first == 0 else None
            self.bottom = chunk_layer == LAYERS - 1 if last else None
            self.half_above = 0.5 if self.top is None else jnp.where(self.top, 0.0, 0.5)
            self.half_below = 0.5 if self.bottom is None else jnp.where(self.bottom, 0.0, 0.5)

        def forcing(self, level, v):
            out = 0.0
            if self.top is not None:
                out = out + jnp.where(self.top, level * IRRIGATION, 0.0) * v
            if self.bottom is not None:
                out = out - jnp.where(self.bottom, v, 0.0)
            return out

        def ends(self, v):
            out = 0.0
            if self.top is not None:
                out = out + jnp.where(self.top, v, 0.0)
            if self.bottom is not None:
                out = out + jnp.where(self.bottom, v, 0.0)
            return out

    chunks = [Chunk(first) for first in range(0, depth, LAYERS)]

    def left(v):
        return pltpu.roll(v, width - 1, 1)

    def right(v):
        return pltpu.roll(v, 1, 1)

    def over(indices, body):
        first, stride, number = indices

        def go(j, carry):
            body(first + stride * j)
            return carry

        lax.fori_loop(0, number, go, 0)

    own = (1, 1, rows)
    inner = (2, 1, rows - 2)
    edges = (1, rows - 1, 2)
    halo = (0, rows + 1, 2)

    def params(i):
        block = PB[(i + 1) // 2]
        return block[0:1], block[1:2], block[2:3]

    def face(i):
        return jnp.where(i == 0, lower_open, jnp.where(i == rows, upper_open, 1.0))

    def level_of(step, i):
        levels = plan_ref[step : step + 1].astype(F32)
        return jnp.where(i > 2, levels[:, 1:2], levels[:, 0:1])

    def cell(step, i, outer=False):
        sat, alpha, n = params(i)
        m = 1.0 - 1.0 / n
        n1 = n - 1.0
        half_m = -0.5 * m
        scale = WATER_RANGE * n1 * alpha
        for c in chunks:
            if step == 0:
                head = HB[0, i, c.here]
            else:
                head = HB[0, i, c.here] + dt0 * AB[0, i, c.bare]
                HB[1, i, c.here] = head
            x = alpha * -head
            log_x = jnp.log(x)
            power = jnp.exp(n1 * log_x)
            v = 1.0 + x * power
            log_v = jnp.log(v)
            root = jnp.exp(half_m * log_v)
            w = power * (root * root)
            rest = 1.0 - w
            q = sat * root * rest
            KB[step, i, c.here] = q * rest
            if step == 1 or not outer:
                IC[step, i, c.bare] = v / (scale * w)
            if step == 1 and outer:
                continue
            LG[step, i, c.bare] = log_x
            LV[step, i, c.bare] = log_v
            WW[step, i, c.bare] = w
            RV[step, i, c.bare] = 1.0 / v
            QQ[step, i, c.bare] = q

    def flow(step, i):
        s_up, s_down = 0.5 * face(i - 1), 0.5 * face(i)
        level = level_of(step, i)
        top_rate = None
        for c in chunks:
            h, k = HB[step, i, c.here], KB[step, i, c.here]
            inv = IC[step, i, c.bare]
            k_up = s_up * (KB[step, i - 1, c.here] + k)
            k_down = s_down * (k + KB[step, i + 1, c.here])
            k_y = right_half * (k + left(k))
            f_y = k_y * (left(h) - h)
            k_above = c.half_above * (KB[step, i, c.above] + k)
            k_below = c.half_below * (k + KB[step, i, c.below])
            net = (
                k_down * (HB[step, i + 1, c.here] - h)
                + k_up * (HB[step, i - 1, c.here] - h)
                + (f_y - right(f_y))
                + k_above * (1.0 + HB[step, i, c.above] - h)
                - k_below * (1.0 + h - HB[step, i, c.below])
                + c.forcing(level, k)
            )
            total = k_up + k_down + (k_y + right(k_y)) + (k_above + k_below) + c.ends(k)
            AB[step, i, c.bare] = net * inv
            rate = jnp.max((total * inv).reshape(LAYERS // 8, 8, width), axis=0)
            top_rate = rate if top_rate is None else jnp.maximum(top_rate, rate)
        RATE[step] = jnp.maximum(RATE[step], top_rate)

    def max_copy(step, device, src):
        return pltpu.make_async_remote_copy(
            src_ref=MX.at[step, src],
            dst_ref=MX.at[step, src],
            send_sem=max_send.at[step, device[1]],
            recv_sem=max_recv.at[step, src],
            device_id=device,
            device_id_type=pl.DeviceIdType.MESH,
        )

    def send_rate(step):
        rate = RATE[step]
        tile = rate[:, :128]
        for start_lane in range(128, width, 128):
            tile = jnp.maximum(tile, rate[:, start_lane : start_lane + 128])
        MX[step, pos] = tile
        for device in row_others:
            max_copy(step, device, pos).start()

    def step_size(step):
        for device in row_others:
            max_copy(step, device, device[1]).wait_recv()
        top = jnp.max(MX[step], axis=0)
        return CFL / jnp.max(top, keepdims=True)

    RATE[...] = jnp.zeros_like(RATE)

    def first_cell(i):
        cell(0, i)

    over(own, first_cell)
    over(inner, functools.partial(flow, 0))
    recv(0)
    recv(1)
    over(halo, lambda i: cell(0, i, True))
    over(edges, functools.partial(flow, 0))
    send_rate(0)
    start(4)

    for pair in (0, 3):
        OH[pair] = jnp.where(zone_of == PB[pair][3:4], 1.0, 0.0).astype(BF16)

    def places(cells):
        index = cells.astype(F32)
        line = jnp.floor((index + 0.5) * (1.0 / width))
        col = index - width * line
        level = jnp.floor((line + 0.5) * (1.0 / rows))
        return level, line - rows * level, col

    sensors = cells_ref.shape[1]
    col_of = lax.broadcasted_iota(jnp.int32, (width, sensors), 0).astype(F32)

    def counts(cells, targets, wanted):
        level, row, col = places(cells)
        cols16 = jnp.where(col_of == col, 1.0, 0.0).astype(BF16)
        if wanted is None:
            spot = row * depth + level
            lines = rows * depth
        else:
            spot = jnp.where(row == wanted, level, -1.0)
            lines = depth
        line_of = lax.broadcasted_iota(jnp.int32, (lines, sensors), 0).astype(F32)
        hit = line_of == spot
        parts = [jnp.ones_like(targets), *pieces(targets)]
        out = nt_dot(stack(hit, parts), cols16)
        number = out[:lines]
        total = out[lines : 2 * lines] + out[2 * lines : 3 * lines] + out[3 * lines :]
        return number, total / jnp.maximum(number, 1.0), hit, cols16

    def stack(hit, parts):
        return jnp.concatenate([jnp.where(hit, part, 0.0) for part in parts], axis=0).astype(BF16)

    def put(values, hit, cols16):
        lines = hit.shape[0]
        out = nt_dot(stack(hit, pieces(values)), cols16)
        return out[:lines] + out[lines : 2 * lines] + out[2 * lines :]

    def take(field, hit, cols16):
        at_sensor = three(field, lambda t: jnp.dot(t, cols16, preferred_element_type=F32))
        return jnp.where(hit, at_sensor, 0.0)

    def column_sum(v):
        return jnp.sum(v, axis=0, keepdims=True)

    number, mean, own_hit, own_cols = counts(cells_ref[...], heads_ref[...], None)
    WB[1 : rows + 1] = number.reshape(rows, depth, width)
    TM[1 : rows + 1] = mean.reshape(rows, depth, width)
    recv(2)
    recv(3)
    halo_spots = []
    for side, wanted, place in ((0, rows - 1, 0), (1, 0, rows + 1)):
        number, mean, hit, cols = counts(NC[side], NT[side], wanted)
        WB[place] = number
        TM[place] = mean
        halo_spots.append((side, place, hit, cols))

    dt0 = step_size(0)

    def next_cell(i):
        cell(1, i)

    over(own, next_cell)
    over(inner, functools.partial(flow, 1))
    recv(4)
    over(halo, lambda i: cell(1, i, True))
    over(edges, functools.partial(flow, 1))
    send_rate(1)
    brims = jnp.concatenate([AB[1, 1], AB[1, rows]], axis=0)
    brim_hit = jnp.concatenate([own_hit[:depth], own_hit[(rows - 1) * depth :]], axis=0)
    picked = take(brims, brim_hit, own_cols)
    SV[0] = column_sum(picked[:depth])
    SV[1] = column_sum(picked[depth:])
    start(5)
    own_mean = column_sum(take(TM[1 : rows + 1].reshape(rows * depth, width), own_hit, own_cols))
    spread_sum = jnp.sum((heads_ref[...] - own_mean) ** 2, keepdims=True)
    recv(5)
    for side, place, hit, cols in halo_spots:
        AB[1, place] = put(NV[side], hit, cols) / jnp.maximum(WB[place], 1.0)
    dt1 = step_size(1)
    scale = 1.0 / events

    def last_head(i):
        head = HB[1, i, deep] + dt1 * AB[1, i]
        off = head - TM[i]
        pull = (scale * WB[i]) * off
        GB[1, i, deep] = pull * dt1 * IC[1, i]
        return head, off * pull, pull

    def finish(i):
        head, square, pull = last_head(i)
        OUT[:, i - 1, :] = head
        LAM[1, i] = pull
        ACC[4, 0] += fold(square)

    for i in range(1, rows + 1):
        finish(i)
    write = pltpu.make_async_copy(OUT, out_hbm, x_sem.at[0])
    write.start()
    over(halo, lambda i: (last_head(i), None)[1])

    def slopes(step, i, grad_k_of, change_of):
        _, _, n = params(i)
        n1 = n - 1.0
        m = 1.0 - 1.0 / n
        inv_n2 = 1.0 / (n * n)
        inv_n1 = 1.0 / n1
        half_n1 = 0.5 * n1
        sums = None
        for c in chunks:
            k, log_x, log_v = KB[step, i, c.here], LG[step, i, c.bare], LV[step, i, c.bare]
            w, r = WW[step, i, c.bare], RV[step, i, c.bare]
            grad_k = grad_k_of(c)
            f = 1.0 - r
            wq = 2.0 * w * QQ[step, i, c.bare]
            n1r = n1 * r
            fl = f * log_x
            log_v = inv_n2 * log_v
            mfl = m * fl
            d_w = log_x - log_v - mfl
            by_log = -grad_k * (half_n1 * (f * k) + n1r * wq)
            by_n = -grad_k * ((0.5 * k) * (log_v + mfl) + wq * d_w)
            by_alpha = by_log
            if change_of is not None:
                change = change_of(c)
                by_log = by_log + change * (n1r - n * f)
                by_n = by_n + change * (inv_n1 + d_w - fl)
                by_alpha = by_log + change
            parts = [fold(grad_k * k), fold(by_alpha), fold(by_n)]
            sums = parts if sums is None else [a + b for a, b in zip(sums, parts)]
            yield c, by_log
        pair = (i + 1) // 2
        for place in range(3):
            ACC[pair, place] += sums[place]

    def pull_back(step, dt, i):
        s_up, s_down = 0.5 * face(i - 1), 0.5 * face(i)
        level = level_of(step, i)

        def grad_k_of(c):
            h, g = HB[step, i, c.here], GB[step, i, c.here]
            c_y = right_half * (left(h) - h) * (left(g) - g)
            return (
                s_down * ((HB[step, i + 1, c.here] - h) * (g - GB[step, i + 1, c.here]))
                + s_up * ((HB[step, i - 1, c.here] - h) * (g - GB[step, i - 1, c.here]))
                - (c_y + right(c_y))
                + c.half_above * (1.0 + HB[step, i, c.above] - h) * (g - GB[step, i, c.above])
                + c.half_below * (1.0 + h - HB[step, i, c.below]) * (GB[step, i, c.below] - g)
                + c.forcing(level, g)
            )

        def change_of(c):
            return -LAM[step, i, c.bare] * (dt * AB[step, i, c.bare])

        for c, by_log in slopes(step, i, grad_k_of, change_of):
            if step == 0:
                continue
            h, k, g = HB[step, i, c.here], KB[step, i, c.here], GB[step, i, c.here]
            f_y = right_half * (k + left(k)) * (left(g) - g)
            lap = (
                s_down * (k + KB[step, i + 1, c.here]) * (GB[step, i + 1, c.here] - g)
                + s_up * (KB[step, i - 1, c.here] + k) * (GB[step, i - 1, c.here] - g)
                + (f_y - right(f_y))
                + c.half_above * (KB[step, i, c.above] + k) * (GB[step, i, c.above] - g)
                + c.half_below * (k + KB[step, i, c.below]) * (GB[step, i, c.below] - g)
            )
            before = LAM[step, i, c.bare] + lap + by_log / h
            LAM[0, i, c.bare] = before
            GB[0, i, c.here] = before * dt0 * IC[0, i, c.bare]

    over(own, functools.partial(pull_back, 1, dt1))

    GB[0, 0] = jnp.zeros_like(GB[0, 0])
    GB[0, rows + 1] = jnp.zeros_like(GB[0, 0])
    over(own, functools.partial(pull_back, 0, dt0))

    def pull_halo(i):
        near = jnp.where(i == 0, 1, rows)
        half = jnp.where(i == 0, 0.5 * lower_open, 0.5 * upper_open)

        def grad_k_of(c):
            return half * ((HB[0, i, c.here] - HB[0, near, c.here]) * GB[0, near, c.here])

        for _ in slopes(0, i, grad_k_of, None):
            pass

    over(halo, pull_halo)

    zone_sums = None
    line = lax.broadcasted_iota(jnp.int32, (8, width), 0)
    for pair in range(4):
        sat, alpha, _ = params(2 * pair - 1)
        grads = [
            jnp.sum(ACC[pair, 0], axis=0, keepdims=True) / sat,
            jnp.sum(ACC[pair, 1], axis=0, keepdims=True) / alpha,
            jnp.sum(ACC[pair, 2], axis=0, keepdims=True),
        ]
        block = jnp.zeros((8, width), F32)
        for place, grad in enumerate(grads):
            block = jnp.where(line == place, grad, block)
        part = three(block, lambda t: nt_dot(t, OH[pair]))
        zone_sums = part if zone_sums is None else zone_sums + part
    loss = 0.5 * (jnp.sum(ACC[4, 0], keepdims=True) + scale * spread_sum)
    if packed:
        lane = lax.broadcasted_iota(jnp.int32, (1, zp), 1) < period
        lines = [
            jnp.where(lane, zone_sums[0:1], zone_sums[1:2]),
            jnp.where(lane, zone_sums[2:3], loss),
        ]
    else:
        lines = [zone_sums[0:1], zone_sums[1:2], zone_sums[2:3], loss + jnp.zeros((1, zp), F32)]
    message = jnp.concatenate(lines, axis=0)

    def sum_copy(buffer, sends, recvs, device, src, dst):
        return pltpu.make_async_remote_copy(
            src_ref=buffer.at[src],
            dst_ref=buffer.at[src],
            send_sem=sends.at[dst],
            recv_sem=recvs.at[src],
            device_id=device,
            device_id_type=pl.DeviceIdType.MESH,
        )

    def add_up(value, buffer, sends, recvs, devices, me, place):
        buffer[me] = value
        for device in devices:
            sum_copy(buffer, sends, recvs, device, me, place(device)).start()
        for device in devices:
            sum_copy(buffer, sends, recvs, device, place(device), place(device)).wait_recv()
        return jnp.sum(buffer[...], axis=0)

    if direct:
        exchanges = [(SUMR, sum_send, sum_recv, others, index, place_of)]
    else:
        exchanges = [
            (SUMR, sum_send, sum_recv, row_others, pos, lambda d: d[1]),
            (SUME, ev_send, ev_recv, event_others, me_event, lambda d: d[0]),
        ]
    for exchange in exchanges:
        message = add_up(message, *exchange)
    small_ref[...] = message
    write.wait()

    for number in range(LINKS):
        sent_pair(number, *pairs[number])
    for device in row_others:
        max_copy(0, device, pos).wait_send()
        max_copy(1, device, pos).wait_send()
    for buffer, sends, recvs, devices, me, place in exchanges:
        for device in devices:
            sum_copy(buffer, sends, recvs, device, me, place(device)).wait_send()


def hand_over(
    head_hbm, small_hbm, out_hbm, loss_ref, grad_sat_ref, grad_alpha_ref, grad_n_ref, small, sem
):
    move = pltpu.make_async_copy(head_hbm, out_hbm, sem.at[0])
    fetch = pltpu.make_async_copy(small_hbm, small, sem.at[1])
    fetch.start()
    move.start()
    fetch.wait()
    zones = grad_sat_ref.shape[1]
    lines, zp = small.shape
    grad_sat_ref[...] = small[0:1, :zones]
    if lines == 2:
        period = zp // 2
        grad_alpha_ref[...] = small[0:1, period : period + zones]
        grad_n_ref[...] = small[1:2, :zones]
        loss_ref[...] = small[1:2, period : period + 1]
    else:
        grad_alpha_ref[...] = small[1:2, :zones]
        grad_n_ref[...] = small[2:3, :zones]
        loss_ref[...] = small[3:4, :1]
    move.wait()


def local(
    initial_head,
    sat_conductivity,
    vg_alpha,
    vg_n,
    zone_map,
    forcing_plan,
    tensiometer_cells,
    tensiometer_heads,
):
    _, depth, rows, width = initial_head.shape
    zones = sat_conductivity.shape[0]
    zp = -(-zones // 128) * 128
    count = lax.axis_size("row")
    groups = lax.axis_size("event")
    sensors = tensiometer_cells.shape[1]
    lines = 2 if 2 * zones <= zp else 4
    senders = count * groups if count * groups <= DIRECT else count
    vmem = pl.BlockSpec(memory_space=pltpu.VMEM)
    hbm = pl.BlockSpec(memory_space=pltpu.HBM)
    deep = pltpu.VMEM((STEPS, rows + 2, depth + 2 * PAD, width), F32)
    full = pltpu.VMEM((STEPS, rows + 2, depth, width), F32)
    single = pltpu.VMEM((rows + 2, depth, width), F32)
    dma = pltpu.SemaphoreType.DMA
    head, small = pl.pallas_call(
        functools.partial(kernel, count, groups, groups * initial_head.shape[0]),
        out_shape=(
            jax.ShapeDtypeStruct((depth, rows, width), F32),
            jax.ShapeDtypeStruct((lines, zp), F32),
        ),
        in_specs=[hbm] * 8,
        out_specs=(hbm, vmem),
        scratch_shapes=[
            deep,
            deep,
            full,
            full,
            full,
            full,
            full,
            full,
            full,
            deep,
            full,
            single,
            single,
            pltpu.VMEM((4, 8, width), F32),
            pltpu.VMEM((8, zp), F32),
            pltpu.VMEM((4, zp, width), BF16),
            pltpu.VMEM((2, 1, sensors), jnp.int32),
            pltpu.VMEM((2, 1, sensors), F32),
            pltpu.VMEM((2, 1, sensors), F32),
            pltpu.VMEM((2, 1, sensors), F32),
            *[pltpu.VMEM((depth, rows, width), F32)] * 2,
            *[pltpu.VMEM((1, zones), F32)] * 3,
            pltpu.VMEM(zone_map.shape, jnp.int32),
            pltpu.VMEM(forcing_plan.shape[1:], jnp.int32),
            pltpu.VMEM((1, sensors), jnp.int32),
            pltpu.VMEM((1, sensors), F32),
            pltpu.VMEM((STEPS, 8, width), F32),
            pltpu.VMEM((5, 3, 8, width), F32),
            pltpu.VMEM((STEPS, count, 8, 128), F32),
            pltpu.VMEM((senders, lines, zp), F32),
            pltpu.VMEM((groups, lines, zp), F32),
            dma((LINKS, 2)),
            dma((LINKS, 2)),
            dma((STEPS, count)),
            dma((STEPS, count)),
            dma((senders,)),
            dma((senders,)),
            dma((groups,)),
            dma((groups,)),
            dma((8,)),
        ],
        compiler_params=pltpu.CompilerParams(
            collective_id=0, has_side_effects=True, vmem_limit_bytes=VMEM_BYTES
        ),
    )(
        initial_head[0],
        sat_conductivity[None],
        vg_alpha[None],
        vg_n[None],
        zone_map,
        forcing_plan[0],
        tensiometer_cells,
        tensiometer_heads,
    )
    final, loss, grad_sat, grad_alpha, grad_n = pl.pallas_call(
        hand_over,
        out_shape=(
            jax.ShapeDtypeStruct((depth, rows, width), F32),
            jax.ShapeDtypeStruct((1, 1), F32),
            *[jax.ShapeDtypeStruct((1, zones), F32)] * 3,
        ),
        in_specs=[hbm] * 2,
        out_specs=(hbm, *[vmem] * 4),
        scratch_shapes=[pltpu.VMEM((lines, zp), F32), dma((2,))],
        compiler_params=pltpu.CompilerParams(vmem_limit_bytes=VMEM_BYTES),
    )(head, small)
    return (final[None], loss[0, 0], grad_sat[0], grad_alpha[0], grad_n[0])


def solution(mesh):
    return jax.shard_map(
        local,
        mesh=mesh,
        in_specs=(
            P("event", None, "row", None),
            P(),
            P(),
            P(),
            P("row", None),
            P("event", None, "row"),
            P("event", "row"),
            P("event", "row"),
        ),
        out_specs=(P("event", None, "row", None), P(), P(), P(), P()),
        check_vma=False,
    )
```

```python
import functools

import jax
import jax.numpy as jnp
from jax import lax
from jax.experimental import pallas as pl
from jax.experimental.pallas import tpu as pltpu
from jax.sharding import PartitionSpec as P

STEPS = 2
CFL = 0.4
IRRIGATION = 0.2
WATER_RANGE = 0.35
HIGHEST = lax.Precision.HIGHEST
F32 = jnp.float32
BF16 = jnp.bfloat16
LAYERS = 16
PAD = 8
LINKS = 6
DIRECT = 64
PARTS = 4
VMEM_BYTES = 63 * 1024 * 1024


def nt_dot(a, b):
    return lax.dot_general(a, b, (((1,), (1,)), ((), ())), preferred_element_type=F32)


def pieces(t):
    one = t.astype(BF16).astype(F32)
    two = (t - one).astype(BF16).astype(F32)
    return one, two, t - one - two


def three(t, product):
    size = t.shape[0]
    out = product(jnp.concatenate(pieces(t), axis=0).astype(BF16))
    return out[:size] + out[size : 2 * size] + out[2 * size :]


def fold(x):
    return jnp.sum(x.reshape(x.shape[0] // 8, 8, x.shape[1]), axis=0)


def kernel(
    count,
    groups,
    events,
    x_hbm,
    sat_hbm,
    alpha_hbm,
    n_hbm,
    zone_hbm,
    plan_hbm,
    cells_hbm,
    heads_hbm,
    out_hbm,
    small_ref,
    HB,
    KB,
    AB,
    IC,
    LG,
    LV,
    WW,
    RV,
    QQ,
    GB,
    LAM,
    WB,
    TM,
    PB,
    TAB,
    OH,
    NC,
    NT,
    SV,
    NV,
    XV,
    OUT,
    sat_ref,
    alpha_ref,
    n_ref,
    zone_ref,
    plan_ref,
    cells_ref,
    heads_ref,
    RATE,
    ACC,
    MX,
    SUMR,
    SUME,
    link_send,
    link_recv,
    max_send,
    max_recv,
    sum_send,
    sum_recv,
    ev_send,
    ev_recv,
    x_sem,
):
    fetches = [
        pltpu.make_async_copy(src, dst, x_sem.at[place])
        for place, (src, dst) in enumerate(
            (
                (zone_hbm, zone_ref),
                (sat_hbm, sat_ref),
                (alpha_hbm, alpha_ref),
                (n_hbm, n_ref),
                (x_hbm, XV),
                (cells_hbm, cells_ref),
                (heads_hbm, heads_ref),
                (plan_hbm, plan_ref),
            )
        )
    ]
    for fetch in fetches:
        fetch.start()
    depth, rows, width = XV.shape
    zp = OH.shape[1]
    zones = sat_ref.shape[1]
    pos = lax.axis_index("row")
    me_event = lax.axis_index("event")
    up, down = pos - 1, pos + 1
    has_up, has_down = pos > 0, pos < count - 1
    lower_open = has_up.astype(F32)
    upper_open = has_down.astype(F32)

    def dev(row):
        return (me_event, row)

    total_devices = count * groups
    direct = total_devices <= DIRECT
    index = me_event * count + pos

    def ring(at, size):
        return [at] + [
            jnp.where(at + k >= size, at + k - size, at + k) for k in range(1, size)
        ]

    row_ring, event_ring = ring(pos, count), ring(me_event, groups)
    others = [(e, r) for r in row_ring for e in event_ring][1:]
    row_others = [(me_event, r) for r in row_ring[1:]]
    event_others = [(e, pos) for e in event_ring[1:]]

    def place_of(device):
        return device[0] * count + device[1]

    barrier = pltpu.get_barrier_semaphore()
    greeted = others if direct else row_others + event_others
    for device in greeted:
        pl.semaphore_signal(barrier, 1, device_id=device, device_id_type=pl.DeviceIdType.MESH)

    deep = pl.ds(PAD, depth)

    def link(number, side, src, dst):
        return pltpu.make_async_remote_copy(
            src_ref=src,
            dst_ref=dst,
            send_sem=link_send.at[number, side],
            recv_sem=link_recv.at[number, side],
            device_id=dev(up if side == 0 else down),
            device_id_type=pl.DeviceIdType.MESH,
        )

    def start_pair(number, to_up, to_down):
        @pl.when(has_up)
        def _():
            link(number, 0, *to_up).start()

        @pl.when(has_down)
        def _():
            link(number, 1, *to_down).start()

    def recv_pair(number, to_up, to_down):
        @pl.when(has_down)
        def _():
            link(number, 0, *to_up).wait_recv()

        @pl.when(has_up)
        def _():
            link(number, 1, *to_down).wait_recv()

    def sent_pair(number, to_up, to_down):
        @pl.when(has_up)
        def _():
            link(number, 0, *to_up).wait_send()

        @pl.when(has_down)
        def _():
            link(number, 1, *to_down).wait_send()

    pairs = [
        ((HB.at[0, 1, deep], HB.at[0, rows + 1, deep]), (HB.at[0, rows, deep], HB.at[0, 0, deep])),
        ((PB.at[1], PB.at[3]), (PB.at[2], PB.at[0])),
        ((cells_ref, NC.at[1]), (cells_ref, NC.at[0])),
        ((heads_ref, NT.at[1]), (heads_ref, NT.at[0])),
        ((AB.at[0, 1], AB.at[0, rows + 1]), (AB.at[0, rows], AB.at[0, 0])),
        ((SV.at[0], NV.at[1]), (SV.at[1], NV.at[0])),
    ]

    def start(number):
        start_pair(number, *pairs[number])

    def recv(number):
        recv_pair(number, *pairs[number])

    for fetch in fetches[:4]:
        fetch.wait()
    TAB[...] = jnp.zeros_like(TAB)
    TAB[0:1, :zones] = sat_ref[...]
    TAB[1:2, :zones] = alpha_ref[...]
    TAB[2:3, :zones] = n_ref[...]
    blocks = zone_ref.shape[1]
    spread = (
        lax.broadcasted_iota(jnp.int32, (blocks, width), 1) // 2
        == lax.broadcasted_iota(jnp.int32, (blocks, width), 0)
    ).astype(F32)
    exact = None if zones <= 256 else HIGHEST
    ids = jnp.dot(
        zone_ref[...].astype(F32), spread, preferred_element_type=F32, precision=exact
    )
    packed = 2 * zones <= zp
    period = zp // 2 if packed else zp
    zone_of = (lax.broadcasted_iota(jnp.int32, (zp, width), 0) % period).astype(F32)
    part_line = lax.broadcasted_iota(jnp.int32, (8, width), 0)
    for pair in range(2):
        own_ids = ids[pair : pair + 1]
        OH[pair + 1] = jnp.where(zone_of == own_ids, 1.0, 0.0).astype(BF16)
        block = three(TAB[...], lambda t: jnp.dot(t, OH[pair + 1], preferred_element_type=F32))
        PB[pair + 1] = jnp.where(part_line == 3, own_ids, block)
    for ref in (HB, KB, GB):
        for step in range(STEPS):
            for i in range(1, rows + 1):
                ref[step, i, 0:PAD] = jnp.zeros((PAD, width), F32)
                ref[step, i, PAD + depth :] = jnp.zeros((PAD, width), F32)
    for fetch in fetches[4:]:
        fetch.wait()
    for i in range(rows):
        HB[0, i + 1, deep] = XV[:, i, :]
    pl.semaphore_wait(barrier, len(greeted))
    start(0)
    start(1)
    start(2)
    start(3)

    @pl.when(jnp.logical_not(has_up))
    def _():
        HB[0, 0, deep] = HB[0, 1, deep]
        PB[0] = PB[1]
        NC[0] = cells_ref[...]
        NT[0] = heads_ref[...]
        NV[0] = jnp.zeros_like(NV[0])
        AB[0, 0] = jnp.zeros((depth, width), F32)

    @pl.when(jnp.logical_not(has_down))
    def _():
        HB[0, rows + 1, deep] = HB[0, rows, deep]
        PB[3] = PB[2]
        NC[1] = cells_ref[...]
        NT[1] = heads_ref[...]
        NV[1] = jnp.zeros_like(NV[1])
        AB[0, rows + 1] = jnp.zeros((depth, width), F32)

    ACC[...] = jnp.zeros_like(ACC)

    column = lax.broadcasted_iota(jnp.int32, (1, width), 1)
    layer = lax.broadcasted_iota(jnp.int32, (depth, 1), 0)
    right_half = jnp.where(column < width - 1, 0.5, 0.0)
    chunk_layer = lax.broadcasted_iota(jnp.int32, (LAYERS, 1), 0)

    class Chunk:
        def __init__(self, first):
            last = first + LAYERS == depth
            self.bare = pl.ds(first, LAYERS)
            self.here = pl.ds(PAD + first, LAYERS)
            self.above = pl.ds(PAD + first - 1, LAYERS)
            self.below = pl.ds(PAD + first + 1, LAYERS)
            self.top = chunk_layer == 0 if first == 0 else None
            self.bottom = chunk_layer == LAYERS - 1 if last else None
            self.half_above = 0.5 if self.top is None else jnp.where(self.top, 0.0, 0.5)
            self.half_below = 0.5 if self.bottom is None else jnp.where(self.bottom, 0.0, 0.5)

        def forcing(self, level, v):
            out = 0.0
            if self.top is not None:
                out = out + jnp.where(self.top, level * IRRIGATION, 0.0) * v
            if self.bottom is not None:
                out = out - jnp.where(self.bottom, v, 0.0)
            return out

        def ends(self, v):
            out = 0.0
            if self.top is not None:
                out = out + jnp.where(self.top, v, 0.0)
            if self.bottom is not None:
                out = out + jnp.where(self.bottom, v, 0.0)
            return out

    chunks = [Chunk(first) for first in range(0, depth, LAYERS)]

    def left(v):
        return pltpu.roll(v, width - 1, 1)

    def right(v):
        return pltpu.roll(v, 1, 1)

    def over(indices, body):
        first, stride, number = indices

        def go(j, carry):
            body(first + stride * j)
            return carry

        lax.fori_loop(0, number, go, 0)

    own = (1, 1, rows)
    inner = (2, 1, rows - 2)
    edges = (1, rows - 1, 2)
    halo = (0, rows + 1, 2)

    def params(i):
        block = PB[(i + 1) // 2]
        return block[0:1], block[1:2], block[2:3]

    def face(i):
        return jnp.where(i == 0, lower_open, jnp.where(i == rows, upper_open, 1.0))

    def level_of(step, i):
        levels = plan_ref[step : step + 1].astype(F32)
        return jnp.where(i > 2, levels[:, 1:2], levels[:, 0:1])

    def cell(step, i, outer=False):
        sat, alpha, n = params(i)
        m = 1.0 - 1.0 / n
        n1 = n - 1.0
        half_m = -0.5 * m
        scale = WATER_RANGE * n1 * alpha
        for c in chunks:
            if step == 0:
                head = HB[0, i, c.here]
            else:
                head = HB[0, i, c.here] + dt0 * AB[0, i, c.bare]
                HB[1, i, c.here] = head
            x = alpha * -head
            log_x = jnp.log(x)
            power = jnp.exp(n1 * log_x)
            v = 1.0 + x * power
            log_v = jnp.log(v)
            root = jnp.exp(half_m * log_v)
            w = power * (root * root)
            rest = 1.0 - w
            q = sat * root * rest
            KB[step, i, c.here] = q * rest
            if step == 1 or not outer:
                IC[step, i, c.bare] = v / (scale * w)
            if step == 1 and outer:
                continue
            LG[step, i, c.bare] = log_x
            LV[step, i, c.bare] = log_v
            WW[step, i, c.bare] = w
            RV[step, i, c.bare] = 1.0 / v
            QQ[step, i, c.bare] = q

    def flow(step, i):
        s_up, s_down = 0.5 * face(i - 1), 0.5 * face(i)
        level = level_of(step, i)
        top_rate = None
        for c in chunks:
            h, k = HB[step, i, c.here], KB[step, i, c.here]
            inv = IC[step, i, c.bare]
            k_up = s_up * (KB[step, i - 1, c.here] + k)
            k_down = s_down * (k + KB[step, i + 1, c.here])
            k_y = right_half * (k + left(k))
            f_y = k_y * (left(h) - h)
            k_above = c.half_above * (KB[step, i, c.above] + k)
            k_below = c.half_below * (k + KB[step, i, c.below])
            net = (
                k_down * (HB[step, i + 1, c.here] - h)
                + k_up * (HB[step, i - 1, c.here] - h)
                + (f_y - right(f_y))
                + k_above * (1.0 + HB[step, i, c.above] - h)
                - k_below * (1.0 + h - HB[step, i, c.below])
                + c.forcing(level, k)
            )
            total = k_up + k_down + (k_y + right(k_y)) + (k_above + k_below) + c.ends(k)
            AB[step, i, c.bare] = net * inv
            rate = jnp.max((total * inv).reshape(LAYERS // 8, 8, width), axis=0)
            top_rate = rate if top_rate is None else jnp.maximum(top_rate, rate)
        RATE[step] = jnp.maximum(RATE[step], top_rate)

    def max_copy(step, device, src):
        return pltpu.make_async_remote_copy(
            src_ref=MX.at[step, src],
            dst_ref=MX.at[step, src],
            send_sem=max_send.at[step, device[1]],
            recv_sem=max_recv.at[step, src],
            device_id=device,
            device_id_type=pl.DeviceIdType.MESH,
        )

    def send_rate(step):
        rate = RATE[step]
        tile = rate[:, :128]
        for start_lane in range(128, width, 128):
            tile = jnp.maximum(tile, rate[:, start_lane : start_lane + 128])
        MX[step, pos] = tile
        for device in row_others:
            max_copy(step, device, pos).start()

    def step_size(step):
        for device in row_others:
            max_copy(step, device, device[1]).wait_recv()
        top = jnp.max(MX[step], axis=0)
        return CFL / jnp.max(top, keepdims=True)

    RATE[...] = jnp.zeros_like(RATE)

    def first_cell(i):
        cell(0, i)

    over(own, first_cell)
    over(inner, functools.partial(flow, 0))
    recv(0)
    recv(1)
    over(halo, lambda i: cell(0, i, True))
    over(edges, functools.partial(flow, 0))
    send_rate(0)
    start(4)

    for pair in (0, 3):
        OH[pair] = jnp.where(zone_of == PB[pair][3:4], 1.0, 0.0).astype(BF16)

    def places(cells):
        index = cells.astype(F32)
        line = jnp.floor((index + 0.5) * (1.0 / width))
        col = index - width * line
        level = jnp.floor((line + 0.5) * (1.0 / rows))
        return level, line - rows * level, col

    sensors = cells_ref.shape[1]
    col_of = lax.broadcasted_iota(jnp.int32, (width, sensors), 0).astype(F32)

    def counts(cells, targets, wanted):
        level, row, col = places(cells)
        cols16 = jnp.where(col_of == col, 1.0, 0.0).astype(BF16)
        if wanted is None:
            spot = row * depth + level
            lines = rows * depth
        else:
            spot = jnp.where(row == wanted, level, -1.0)
            lines = depth
        line_of = lax.broadcasted_iota(jnp.int32, (lines, sensors), 0).astype(F32)
        hit = line_of == spot
        parts = [jnp.ones_like(targets), *pieces(targets)]
        out = nt_dot(stack(hit, parts), cols16)
        number = out[:lines]
        total = out[lines : 2 * lines] + out[2 * lines : 3 * lines] + out[3 * lines :]
        return number, total / jnp.maximum(number, 1.0), hit, cols16

    def stack(hit, parts):
        return jnp.concatenate([jnp.where(hit, part, 0.0) for part in parts], axis=0).astype(BF16)

    def put(values, hit, cols16):
        lines = hit.shape[0]
        out = nt_dot(stack(hit, pieces(values)), cols16)
        return out[:lines] + out[lines : 2 * lines] + out[2 * lines :]

    def take(field, hit, cols16):
        at_sensor = three(field, lambda t: jnp.dot(t, cols16, preferred_element_type=F32))
        return jnp.where(hit, at_sensor, 0.0)

    def column_sum(v):
        return jnp.sum(v, axis=0, keepdims=True)

    number, mean, own_hit, own_cols = counts(cells_ref[...], heads_ref[...], None)
    WB[1 : rows + 1] = number.reshape(rows, depth, width)
    TM[1 : rows + 1] = mean.reshape(rows, depth, width)
    recv(2)
    recv(3)
    halo_spots = []
    for side, wanted, place in ((0, rows - 1, 0), (1, 0, rows + 1)):
        number, mean, hit, cols = counts(NC[side], NT[side], wanted)
        WB[place] = number
        TM[place] = mean
        halo_spots.append((side, place, hit, cols))

    dt0 = step_size(0)

    def next_cell(i):
        cell(1, i)

    over(own, next_cell)
    over(inner, functools.partial(flow, 1))
    recv(4)
    over(halo, lambda i: cell(1, i, True))
    over(edges, functools.partial(flow, 1))
    send_rate(1)
    brims = jnp.concatenate([AB[1, 1], AB[1, rows]], axis=0)
    brim_hit = jnp.concatenate([own_hit[:depth], own_hit[(rows - 1) * depth :]], axis=0)
    picked = take(brims, brim_hit, own_cols)
    SV[0] = column_sum(picked[:depth])
    SV[1] = column_sum(picked[depth:])
    start(5)
    own_mean = column_sum(take(TM[1 : rows + 1].reshape(rows * depth, width), own_hit, own_cols))
    spread_sum = jnp.sum((heads_ref[...] - own_mean) ** 2, keepdims=True)
    recv(5)
    for side, place, hit, cols in halo_spots:
        AB[1, place] = put(NV[side], hit, cols) / jnp.maximum(WB[place], 1.0)
    dt1 = step_size(1)
    scale = 1.0 / events

    def last_head(i):
        head = HB[1, i, deep] + dt1 * AB[1, i]
        off = head - TM[i]
        pull = (scale * WB[i]) * off
        GB[1, i, deep] = pull * dt1 * IC[1, i]
        return head, off * pull, pull

    def finish(i):
        head, square, pull = last_head(i)
        OUT[:, i - 1, :] = head
        LAM[1, i] = pull
        ACC[4, 0] += fold(square)

    for i in range(1, rows + 1):
        finish(i)
    write = pltpu.make_async_copy(OUT, out_hbm, x_sem.at[0])
    write.start()
    over(halo, lambda i: (last_head(i), None)[1])

    def slopes(step, i, grad_k_of, change_of):
        _, _, n = params(i)
        n1 = n - 1.0
        m = 1.0 - 1.0 / n
        inv_n2 = 1.0 / (n * n)
        inv_n1 = 1.0 / n1
        half_n1 = 0.5 * n1
        sums = None
        for c in chunks:
            k, log_x, log_v = KB[step, i, c.here], LG[step, i, c.bare], LV[step, i, c.bare]
            w, r = WW[step, i, c.bare], RV[step, i, c.bare]
            grad_k = grad_k_of(c)
            f = 1.0 - r
            wq = 2.0 * w * QQ[step, i, c.bare]
            n1r = n1 * r
            fl = f * log_x
            log_v = inv_n2 * log_v
            mfl = m * fl
            d_w = log_x - log_v - mfl
            by_log = -grad_k * (half_n1 * (f * k) + n1r * wq)
            by_n = -grad_k * ((0.5 * k) * (log_v + mfl) + wq * d_w)
            by_alpha = by_log
            if change_of is not None:
                change = change_of(c)
                by_log = by_log + change * (n1r - n * f)
                by_n = by_n + change * (inv_n1 + d_w - fl)
                by_alpha = by_log + change
            parts = [fold(grad_k * k), fold(by_alpha), fold(by_n)]
            sums = parts if sums is None else [a + b for a, b in zip(sums, parts)]
            yield c, by_log
        pair = (i + 1) // 2
        for place in range(3):
            ACC[pair, place] += sums[place]

    def pull_back(step, dt, i):
        s_up, s_down = 0.5 * face(i - 1), 0.5 * face(i)
        level = level_of(step, i)

        def grad_k_of(c):
            h, g = HB[step, i, c.here], GB[step, i, c.here]
            c_y = right_half * (left(h) - h) * (left(g) - g)
            return (
                s_down * ((HB[step, i + 1, c.here] - h) * (g - GB[step, i + 1, c.here]))
                + s_up * ((HB[step, i - 1, c.here] - h) * (g - GB[step, i - 1, c.here]))
                - (c_y + right(c_y))
                + c.half_above * (1.0 + HB[step, i, c.above] - h) * (g - GB[step, i, c.above])
                + c.half_below * (1.0 + h - HB[step, i, c.below]) * (GB[step, i, c.below] - g)
                + c.forcing(level, g)
            )

        def change_of(c):
            return -LAM[step, i, c.bare] * (dt * AB[step, i, c.bare])

        for c, by_log in slopes(step, i, grad_k_of, change_of):
            if step == 0:
                continue
            h, k, g = HB[step, i, c.here], KB[step, i, c.here], GB[step, i, c.here]
            f_y = right_half * (k + left(k)) * (left(g) - g)
            lap = (
                s_down * (k + KB[step, i + 1, c.here]) * (GB[step, i + 1, c.here] - g)
                + s_up * (KB[step, i - 1, c.here] + k) * (GB[step, i - 1, c.here] - g)
                + (f_y - right(f_y))
                + c.half_above * (KB[step, i, c.above] + k) * (GB[step, i, c.above] - g)
                + c.half_below * (k + KB[step, i, c.below]) * (GB[step, i, c.below] - g)
            )
            before = LAM[step, i, c.bare] + lap + by_log / h
            LAM[0, i, c.bare] = before
            GB[0, i, c.here] = before * dt0 * IC[0, i, c.bare]

    over(own, functools.partial(pull_back, 1, dt1))

    GB[0, 0] = jnp.zeros_like(GB[0, 0])
    GB[0, rows + 1] = jnp.zeros_like(GB[0, 0])
    over(own, functools.partial(pull_back, 0, dt0))

    def pull_halo(i):
        near = jnp.where(i == 0, 1, rows)
        half = jnp.where(i == 0, 0.5 * lower_open, 0.5 * upper_open)

        def grad_k_of(c):
            return half * ((HB[0, i, c.here] - HB[0, near, c.here]) * GB[0, near, c.here])

        for _ in slopes(0, i, grad_k_of, None):
            pass

    over(halo, pull_halo)

    zone_sums = None
    line = lax.broadcasted_iota(jnp.int32, (8, width), 0)
    for pair in range(4):
        sat, alpha, _ = params(2 * pair - 1)
        grads = [
            jnp.sum(ACC[pair, 0], axis=0, keepdims=True) / sat,
            jnp.sum(ACC[pair, 1], axis=0, keepdims=True) / alpha,
            jnp.sum(ACC[pair, 2], axis=0, keepdims=True),
        ]
        block = jnp.zeros((8, width), F32)
        for place, grad in enumerate(grads):
            block = jnp.where(line == place, grad, block)
        part = three(block, lambda t: nt_dot(t, OH[pair]))
        zone_sums = part if zone_sums is None else zone_sums + part
    loss = 0.5 * (jnp.sum(ACC[4, 0], keepdims=True) + scale * spread_sum)
    if packed:
        lane = lax.broadcasted_iota(jnp.int32, (1, zp), 1) < period
        lines = [
            jnp.where(lane, zone_sums[0:1], zone_sums[1:2]),
            jnp.where(lane, zone_sums[2:3], loss),
        ]
    else:
        lines = [zone_sums[0:1], zone_sums[1:2], zone_sums[2:3], loss + jnp.zeros((1, zp), F32)]
    message = jnp.concatenate(lines, axis=0)

    def sum_copy(buffer, sends, recvs, device, src, dst):
        return pltpu.make_async_remote_copy(
            src_ref=buffer.at[src],
            dst_ref=buffer.at[src],
            send_sem=sends.at[dst],
            recv_sem=recvs.at[src],
            device_id=device,
            device_id_type=pl.DeviceIdType.MESH,
        )

    def add_up(value, buffer, sends, recvs, devices, me, place):
        buffer[me] = value
        for device in devices:
            sum_copy(buffer, sends, recvs, device, me, place(device)).start()
        for device in devices:
            sum_copy(buffer, sends, recvs, device, place(device), place(device)).wait_recv()
        return jnp.sum(buffer[...], axis=0)

    if direct:
        exchanges = [(SUMR, sum_send, sum_recv, others, index, place_of)]
    else:
        exchanges = [
            (SUMR, sum_send, sum_recv, row_others, pos, lambda d: d[1]),
            (SUME, ev_send, ev_recv, event_others, me_event, lambda d: d[0]),
        ]
    for exchange in exchanges:
        message = add_up(message, *exchange)
    small_ref[...] = message
    write.wait()

    for number in range(LINKS):
        sent_pair(number, *pairs[number])
    for device in row_others:
        max_copy(0, device, pos).wait_send()
        max_copy(1, device, pos).wait_send()
    for buffer, sends, recvs, devices, me, place in exchanges:
        for device in devices:
            sum_copy(buffer, sends, recvs, device, me, place(device)).wait_send()


def hand_over(
    head_hbm,
    small_hbm,
    out_hbm,
    loss_ref,
    grad_sat_ref,
    grad_alpha_ref,
    grad_n_ref,
    head,
    small,
    sem,
):
    fetch = pltpu.make_async_copy(small_hbm, small, sem.at[0, PARTS])
    size = head.shape[0] // PARTS
    spans = [pl.ds(part * size, size) for part in range(PARTS)]
    moves = [
        (
            pltpu.make_async_copy(head_hbm.at[span], head.at[span], sem.at[0, part]),
            pltpu.make_async_copy(head.at[span], out_hbm.at[span], sem.at[1, part]),
        )
        for part, span in enumerate(spans)
    ]
    for inward, _ in moves:
        inward.start()
    fetch.start()
    for inward, outward in moves:
        inward.wait()
        outward.start()
    fetch.wait()
    zones = grad_sat_ref.shape[1]
    lines, zp = small.shape
    grad_sat_ref[...] = small[0:1, :zones]
    if lines == 2:
        period = zp // 2
        grad_alpha_ref[...] = small[0:1, period : period + zones]
        grad_n_ref[...] = small[1:2, :zones]
        loss_ref[...] = small[1:2, period : period + 1]
    else:
        grad_alpha_ref[...] = small[1:2, :zones]
        grad_n_ref[...] = small[2:3, :zones]
        loss_ref[...] = small[3:4, :1]
    for _, outward in moves:
        outward.wait()


def local(
    initial_head,
    sat_conductivity,
    vg_alpha,
    vg_n,
    zone_map,
    forcing_plan,
    tensiometer_cells,
    tensiometer_heads,
):
    _, depth, rows, width = initial_head.shape
    zones = sat_conductivity.shape[0]
    zp = -(-zones // 128) * 128
    count = lax.axis_size("row")
    groups = lax.axis_size("event")
    sensors = tensiometer_cells.shape[1]
    lines = 2 if 2 * zones <= zp else 4
    senders = count * groups if count * groups <= DIRECT else count
    vmem = pl.BlockSpec(memory_space=pltpu.VMEM)
    hbm = pl.BlockSpec(memory_space=pltpu.HBM)
    deep = pltpu.VMEM((STEPS, rows + 2, depth + 2 * PAD, width), F32)
    full = pltpu.VMEM((STEPS, rows + 2, depth, width), F32)
    single = pltpu.VMEM((rows + 2, depth, width), F32)
    dma = pltpu.SemaphoreType.DMA
    head, small = pl.pallas_call(
        functools.partial(kernel, count, groups, groups * initial_head.shape[0]),
        out_shape=(
            jax.ShapeDtypeStruct((depth, rows, width), F32),
            jax.ShapeDtypeStruct((lines, zp), F32),
        ),
        in_specs=[hbm] * 8,
        out_specs=(hbm, vmem),
        scratch_shapes=[
            deep,
            deep,
            full,
            full,
            full,
            full,
            full,
            full,
            full,
            deep,
            full,
            single,
            single,
            pltpu.VMEM((4, 8, width), F32),
            pltpu.VMEM((8, zp), F32),
            pltpu.VMEM((4, zp, width), BF16),
            pltpu.VMEM((2, 1, sensors), jnp.int32),
            pltpu.VMEM((2, 1, sensors), F32),
            pltpu.VMEM((2, 1, sensors), F32),
            pltpu.VMEM((2, 1, sensors), F32),
            *[pltpu.VMEM((depth, rows, width), F32)] * 2,
            *[pltpu.VMEM((1, zones), F32)] * 3,
            pltpu.VMEM(zone_map.shape, jnp.int32),
            pltpu.VMEM(forcing_plan.shape[1:], jnp.int32),
            pltpu.VMEM((1, sensors), jnp.int32),
            pltpu.VMEM((1, sensors), F32),
            pltpu.VMEM((STEPS, 8, width), F32),
            pltpu.VMEM((5, 3, 8, width), F32),
            pltpu.VMEM((STEPS, count, 8, 128), F32),
            pltpu.VMEM((senders, lines, zp), F32),
            pltpu.VMEM((groups, lines, zp), F32),
            dma((LINKS, 2)),
            dma((LINKS, 2)),
            dma((STEPS, count)),
            dma((STEPS, count)),
            dma((senders,)),
            dma((senders,)),
            dma((groups,)),
            dma((groups,)),
            dma((8,)),
        ],
        compiler_params=pltpu.CompilerParams(
            collective_id=0, has_side_effects=True, vmem_limit_bytes=VMEM_BYTES
        ),
    )(
        initial_head[0],
        sat_conductivity[None],
        vg_alpha[None],
        vg_n[None],
        zone_map,
        forcing_plan[0],
        tensiometer_cells,
        tensiometer_heads,
    )
    final, loss, grad_sat, grad_alpha, grad_n = pl.pallas_call(
        hand_over,
        out_shape=(
            jax.ShapeDtypeStruct((depth, rows, width), F32),
            jax.ShapeDtypeStruct((1, 1), F32),
            *[jax.ShapeDtypeStruct((1, zones), F32)] * 3,
        ),
        in_specs=[hbm] * 2,
        out_specs=(hbm, *[vmem] * 4),
        scratch_shapes=[
            pltpu.VMEM((depth, rows, width), F32),
            pltpu.VMEM((lines, zp), F32),
            dma((2, PARTS + 1)),
        ],
        compiler_params=pltpu.CompilerParams(vmem_limit_bytes=VMEM_BYTES),
    )(head, small)
    return (final[None], loss[0, 0], grad_sat[0], grad_alpha[0], grad_n[0])


def solution(mesh):
    return jax.shard_map(
        local,
        mesh=mesh,
        in_specs=(
            P("event", None, "row", None),
            P(),
            P(),
            P(),
            P("row", None),
            P("event", None, "row"),
            P("event", "row"),
            P("event", "row"),
        ),
        out_specs=(P("event", None, "row", None), P(), P(), P(), P()),
        check_vma=False,
    )
```

```python
import functools

import jax
import jax.numpy as jnp
from jax import lax
from jax.experimental import pallas as pl
from jax.experimental.pallas import tpu as pltpu
from jax.sharding import PartitionSpec as P

STEPS = 2
CFL = 0.4
IRRIGATION = 0.2
WATER_RANGE = 0.35
HIGHEST = lax.Precision.HIGHEST
F32 = jnp.float32
BF16 = jnp.bfloat16
LAYERS = 16
PAD = 8
LINKS = 6
DIRECT = 64
PARTS = 4
VMEM_BYTES = 63 * 1024 * 1024


def nt_dot(a, b):
    return lax.dot_general(a, b, (((1,), (1,)), ((), ())), preferred_element_type=F32)


def pieces(t):
    one = t.astype(BF16).astype(F32)
    two = (t - one).astype(BF16).astype(F32)
    return one, two, t - one - two


def three(t, product):
    size = t.shape[0]
    out = product(jnp.concatenate(pieces(t), axis=0).astype(BF16))
    return out[:size] + out[size : 2 * size] + out[2 * size :]


def fold(x):
    return jnp.sum(x.reshape(x.shape[0] // 8, 8, x.shape[1]), axis=0)


def kernel(
    count,
    groups,
    events,
    x_hbm,
    sat_hbm,
    alpha_hbm,
    n_hbm,
    zone_hbm,
    plan_hbm,
    cells_hbm,
    heads_hbm,
    out_hbm,
    small_ref,
    HB,
    KB,
    AB,
    IC,
    LG,
    LV,
    WW,
    RV,
    QQ,
    GB,
    LAM,
    WB,
    TM,
    PB,
    TAB,
    OH,
    NC,
    NT,
    SV,
    NV,
    XV,
    OUT,
    sat_ref,
    alpha_ref,
    n_ref,
    zone_ref,
    plan_ref,
    cells_ref,
    heads_ref,
    RATE,
    ACC,
    MX,
    SUMR,
    SUME,
    link_send,
    link_recv,
    max_send,
    max_recv,
    sum_send,
    sum_recv,
    ev_send,
    ev_recv,
    x_sem,
):
    fetches = [
        pltpu.make_async_copy(src, dst, x_sem.at[place])
        for place, (src, dst) in enumerate(
            (
                (x_hbm, XV),
                (zone_hbm, zone_ref),
                (sat_hbm, sat_ref),
                (alpha_hbm, alpha_ref),
                (n_hbm, n_ref),
                (cells_hbm, cells_ref),
                (heads_hbm, heads_ref),
                (plan_hbm, plan_ref),
            )
        )
    ]
    for fetch in fetches:
        fetch.start()
    depth, rows, width = XV.shape
    zp = OH.shape[1]
    zones = sat_ref.shape[1]
    pos = lax.axis_index("row")
    me_event = lax.axis_index("event")
    up, down = pos - 1, pos + 1
    has_up, has_down = pos > 0, pos < count - 1
    lower_open = has_up.astype(F32)
    upper_open = has_down.astype(F32)

    def dev(row):
        return (me_event, row)

    total_devices = count * groups
    direct = total_devices <= DIRECT
    index = me_event * count + pos

    def ring(at, size):
        return [at] + [
            jnp.where(at + k >= size, at + k - size, at + k) for k in range(1, size)
        ]

    row_ring, event_ring = ring(pos, count), ring(me_event, groups)
    others = [(e, r) for r in row_ring for e in event_ring][1:]
    row_others = [(me_event, r) for r in row_ring[1:]]
    event_others = [(e, pos) for e in event_ring[1:]]

    def place_of(device):
        return device[0] * count + device[1]

    barrier = pltpu.get_barrier_semaphore()
    greeted = others if direct else row_others + event_others
    for device in greeted:
        pl.semaphore_signal(barrier, 1, device_id=device, device_id_type=pl.DeviceIdType.MESH)

    deep = pl.ds(PAD, depth)

    def link(number, side, src, dst):
        return pltpu.make_async_remote_copy(
            src_ref=src,
            dst_ref=dst,
            send_sem=link_send.at[number, side],
            recv_sem=link_recv.at[number, side],
            device_id=dev(up if side == 0 else down),
            device_id_type=pl.DeviceIdType.MESH,
        )

    def start_pair(number, to_up, to_down):
        @pl.when(has_up)
        def _():
            link(number, 0, *to_up).start()

        @pl.when(has_down)
        def _():
            link(number, 1, *to_down).start()

    def recv_pair(number, to_up, to_down):
        @pl.when(has_down)
        def _():
            link(number, 0, *to_up).wait_recv()

        @pl.when(has_up)
        def _():
            link(number, 1, *to_down).wait_recv()

    def sent_pair(number, to_up, to_down):
        @pl.when(has_up)
        def _():
            link(number, 0, *to_up).wait_send()

        @pl.when(has_down)
        def _():
            link(number, 1, *to_down).wait_send()

    pairs = [
        ((HB.at[0, 1, deep], HB.at[0, rows + 1, deep]), (HB.at[0, rows, deep], HB.at[0, 0, deep])),
        ((PB.at[1], PB.at[3]), (PB.at[2], PB.at[0])),
        ((cells_ref, NC.at[1]), (cells_ref, NC.at[0])),
        ((heads_ref, NT.at[1]), (heads_ref, NT.at[0])),
        ((AB.at[0, 1], AB.at[0, rows + 1]), (AB.at[0, rows], AB.at[0, 0])),
        ((SV.at[0], NV.at[1]), (SV.at[1], NV.at[0])),
    ]

    def start(number):
        start_pair(number, *pairs[number])

    def recv(number):
        recv_pair(number, *pairs[number])

    fetches[0].wait()
    for i in (0, rows - 1):
        HB[0, i + 1, deep] = XV[:, i, :]
    pl.semaphore_wait(barrier, len(greeted))
    start(0)
    for fetch in fetches[1:]:
        fetch.wait()
    start(2)
    start(3)
    TAB[...] = jnp.zeros_like(TAB)
    TAB[0:1, :zones] = sat_ref[...]
    TAB[1:2, :zones] = alpha_ref[...]
    TAB[2:3, :zones] = n_ref[...]
    blocks = zone_ref.shape[1]
    spread = (
        lax.broadcasted_iota(jnp.int32, (blocks, width), 1) // 2
        == lax.broadcasted_iota(jnp.int32, (blocks, width), 0)
    ).astype(F32)
    exact = None if zones <= 256 else HIGHEST
    ids = jnp.dot(
        zone_ref[...].astype(F32), spread, preferred_element_type=F32, precision=exact
    )
    packed = 2 * zones <= zp
    period = zp // 2 if packed else zp
    zone_of = (lax.broadcasted_iota(jnp.int32, (zp, width), 0) % period).astype(F32)
    part_line = lax.broadcasted_iota(jnp.int32, (8, width), 0)
    for pair in range(2):
        own_ids = ids[pair : pair + 1]
        OH[pair + 1] = jnp.where(zone_of == own_ids, 1.0, 0.0).astype(BF16)
        block = three(TAB[...], lambda t: jnp.dot(t, OH[pair + 1], preferred_element_type=F32))
        PB[pair + 1] = jnp.where(part_line == 3, own_ids, block)
    start(1)
    for ref in (HB, KB, GB):
        for step in range(STEPS):
            for i in range(1, rows + 1):
                ref[step, i, 0:PAD] = jnp.zeros((PAD, width), F32)
                ref[step, i, PAD + depth :] = jnp.zeros((PAD, width), F32)
    for i in range(1, rows - 1):
        HB[0, i + 1, deep] = XV[:, i, :]

    @pl.when(jnp.logical_not(has_up))
    def _():
        HB[0, 0, deep] = HB[0, 1, deep]
        PB[0] = PB[1]
        NC[0] = cells_ref[...]
        NT[0] = heads_ref[...]
        NV[0] = jnp.zeros_like(NV[0])
        AB[0, 0] = jnp.zeros((depth, width), F32)

    @pl.when(jnp.logical_not(has_down))
    def _():
        HB[0, rows + 1, deep] = HB[0, rows, deep]
        PB[3] = PB[2]
        NC[1] = cells_ref[...]
        NT[1] = heads_ref[...]
        NV[1] = jnp.zeros_like(NV[1])
        AB[0, rows + 1] = jnp.zeros((depth, width), F32)

    ACC[...] = jnp.zeros_like(ACC)

    column = lax.broadcasted_iota(jnp.int32, (1, width), 1)
    layer = lax.broadcasted_iota(jnp.int32, (depth, 1), 0)
    right_half = jnp.where(column < width - 1, 0.5, 0.0)
    chunk_layer = lax.broadcasted_iota(jnp.int32, (LAYERS, 1), 0)

    class Chunk:
        def __init__(self, first):
            last = first + LAYERS == depth
            self.bare = pl.ds(first, LAYERS)
            self.here = pl.ds(PAD + first, LAYERS)
            self.above = pl.ds(PAD + first - 1, LAYERS)
            self.below = pl.ds(PAD + first + 1, LAYERS)
            self.top = chunk_layer == 0 if first == 0 else None
            self.bottom = chunk_layer == LAYERS - 1 if last else None
            self.half_above = 0.5 if self.top is None else jnp.where(self.top, 0.0, 0.5)
            self.half_below = 0.5 if self.bottom is None else jnp.where(self.bottom, 0.0, 0.5)

        def forcing(self, level, v):
            out = 0.0
            if self.top is not None:
                out = out + jnp.where(self.top, level * IRRIGATION, 0.0) * v
            if self.bottom is not None:
                out = out - jnp.where(self.bottom, v, 0.0)
            return out

        def ends(self, v):
            out = 0.0
            if self.top is not None:
                out = out + jnp.where(self.top, v, 0.0)
            if self.bottom is not None:
                out = out + jnp.where(self.bottom, v, 0.0)
            return out

    chunks = [Chunk(first) for first in range(0, depth, LAYERS)]

    def left(v):
        return pltpu.roll(v, width - 1, 1)

    def right(v):
        return pltpu.roll(v, 1, 1)

    def over(indices, body):
        first, stride, number = indices

        def go(j, carry):
            body(first + stride * j)
            return carry

        lax.fori_loop(0, number, go, 0)

    own = (1, 1, rows)
    inner = (2, 1, rows - 2)
    edges = (1, rows - 1, 2)
    halo = (0, rows + 1, 2)

    def params(i):
        block = PB[(i + 1) // 2]
        return block[0:1], block[1:2], block[2:3]

    def face(i):
        return jnp.where(i == 0, lower_open, jnp.where(i == rows, upper_open, 1.0))

    def level_of(step, i):
        levels = plan_ref[step : step + 1].astype(F32)
        return jnp.where(i > 2, levels[:, 1:2], levels[:, 0:1])

    def cell(step, i, outer=False):
        sat, alpha, n = params(i)
        m = 1.0 - 1.0 / n
        n1 = n - 1.0
        half_m = -0.5 * m
        scale = WATER_RANGE * n1 * alpha
        for c in chunks:
            if step == 0:
                head = HB[0, i, c.here]
            else:
                head = HB[0, i, c.here] + dt0 * AB[0, i, c.bare]
                HB[1, i, c.here] = head
            x = alpha * -head
            log_x = jnp.log(x)
            power = jnp.exp(n1 * log_x)
            v = 1.0 + x * power
            log_v = jnp.log(v)
            root = jnp.exp(half_m * log_v)
            w = power * (root * root)
            rest = 1.0 - w
            q = sat * root * rest
            KB[step, i, c.here] = q * rest
            if step == 1 or not outer:
                IC[step, i, c.bare] = v / (scale * w)
            if step == 1 and outer:
                continue
            LG[step, i, c.bare] = log_x
            LV[step, i, c.bare] = log_v
            WW[step, i, c.bare] = w
            RV[step, i, c.bare] = 1.0 / v
            QQ[step, i, c.bare] = q

    def flow(step, i):
        s_up, s_down = 0.5 * face(i - 1), 0.5 * face(i)
        level = level_of(step, i)
        top_rate = None
        for c in chunks:
            h, k = HB[step, i, c.here], KB[step, i, c.here]
            inv = IC[step, i, c.bare]
            k_up = s_up * (KB[step, i - 1, c.here] + k)
            k_down = s_down * (k + KB[step, i + 1, c.here])
            k_y = right_half * (k + left(k))
            f_y = k_y * (left(h) - h)
            k_above = c.half_above * (KB[step, i, c.above] + k)
            k_below = c.half_below * (k + KB[step, i, c.below])
            net = (
                k_down * (HB[step, i + 1, c.here] - h)
                + k_up * (HB[step, i - 1, c.here] - h)
                + (f_y - right(f_y))
                + k_above * (1.0 + HB[step, i, c.above] - h)
                - k_below * (1.0 + h - HB[step, i, c.below])
                + c.forcing(level, k)
            )
            total = k_up + k_down + (k_y + right(k_y)) + (k_above + k_below) + c.ends(k)
            AB[step, i, c.bare] = net * inv
            rate = jnp.max((total * inv).reshape(LAYERS // 8, 8, width), axis=0)
            top_rate = rate if top_rate is None else jnp.maximum(top_rate, rate)
        RATE[step] = jnp.maximum(RATE[step], top_rate)

    def max_copy(step, device, src):
        return pltpu.make_async_remote_copy(
            src_ref=MX.at[step, src],
            dst_ref=MX.at[step, src],
            send_sem=max_send.at[step, device[1]],
            recv_sem=max_recv.at[step, src],
            device_id=device,
            device_id_type=pl.DeviceIdType.MESH,
        )

    def send_rate(step):
        rate = RATE[step]
        tile = rate[:, :128]
        for start_lane in range(128, width, 128):
            tile = jnp.maximum(tile, rate[:, start_lane : start_lane + 128])
        MX[step, pos] = tile
        for device in row_others:
            max_copy(step, device, pos).start()

    def step_size(step):
        for device in row_others:
            max_copy(step, device, device[1]).wait_recv()
        top = jnp.max(MX[step], axis=0)
        return CFL / jnp.max(top, keepdims=True)

    RATE[...] = jnp.zeros_like(RATE)

    def first_cell(i):
        cell(0, i)

    over(own, first_cell)
    over(inner, functools.partial(flow, 0))
    recv(0)
    recv(1)
    over(halo, lambda i: cell(0, i, True))
    over(edges, functools.partial(flow, 0))
    send_rate(0)
    start(4)

    for pair in (0, 3):
        OH[pair] = jnp.where(zone_of == PB[pair][3:4], 1.0, 0.0).astype(BF16)

    def places(cells):
        index = cells.astype(F32)
        line = jnp.floor((index + 0.5) * (1.0 / width))
        col = index - width * line
        level = jnp.floor((line + 0.5) * (1.0 / rows))
        return level, line - rows * level, col

    sensors = cells_ref.shape[1]
    col_of = lax.broadcasted_iota(jnp.int32, (width, sensors), 0).astype(F32)

    def counts(cells, targets, wanted):
        level, row, col = places(cells)
        cols16 = jnp.where(col_of == col, 1.0, 0.0).astype(BF16)
        if wanted is None:
            spot = row * depth + level
            lines = rows * depth
        else:
            spot = jnp.where(row == wanted, level, -1.0)
            lines = depth
        line_of = lax.broadcasted_iota(jnp.int32, (lines, sensors), 0).astype(F32)
        hit = line_of == spot
        parts = [jnp.ones_like(targets), *pieces(targets)]
        out = nt_dot(stack(hit, parts), cols16)
        number = out[:lines]
        total = out[lines : 2 * lines] + out[2 * lines : 3 * lines] + out[3 * lines :]
        return number, total / jnp.maximum(number, 1.0), hit, cols16

    def stack(hit, parts):
        return jnp.concatenate([jnp.where(hit, part, 0.0) for part in parts], axis=0).astype(BF16)

    def put(values, hit, cols16):
        lines = hit.shape[0]
        out = nt_dot(stack(hit, pieces(values)), cols16)
        return out[:lines] + out[lines : 2 * lines] + out[2 * lines :]

    def take(field, hit, cols16):
        at_sensor = three(field, lambda t: jnp.dot(t, cols16, preferred_element_type=F32))
        return jnp.where(hit, at_sensor, 0.0)

    def column_sum(v):
        return jnp.sum(v, axis=0, keepdims=True)

    number, mean, own_hit, own_cols = counts(cells_ref[...], heads_ref[...], None)
    WB[1 : rows + 1] = number.reshape(rows, depth, width)
    TM[1 : rows + 1] = mean.reshape(rows, depth, width)
    recv(2)
    recv(3)
    halo_spots = []
    for side, wanted, place in ((0, rows - 1, 0), (1, 0, rows + 1)):
        number, mean, hit, cols = counts(NC[side], NT[side], wanted)
        WB[place] = number
        TM[place] = mean
        halo_spots.append((side, place, hit, cols))

    dt0 = step_size(0)

    def next_cell(i):
        cell(1, i)

    over(own, next_cell)
    over(inner, functools.partial(flow, 1))
    recv(4)
    over(halo, lambda i: cell(1, i, True))
    over(edges, functools.partial(flow, 1))
    send_rate(1)
    brims = jnp.concatenate([AB[1, 1], AB[1, rows]], axis=0)
    brim_hit = jnp.concatenate([own_hit[:depth], own_hit[(rows - 1) * depth :]], axis=0)
    picked = take(brims, brim_hit, own_cols)
    SV[0] = column_sum(picked[:depth])
    SV[1] = column_sum(picked[depth:])
    start(5)
    own_mean = column_sum(take(TM[1 : rows + 1].reshape(rows * depth, width), own_hit, own_cols))
    spread_sum = jnp.sum((heads_ref[...] - own_mean) ** 2, keepdims=True)
    recv(5)
    for side, place, hit, cols in halo_spots:
        AB[1, place] = put(NV[side], hit, cols) / jnp.maximum(WB[place], 1.0)
    dt1 = step_size(1)
    scale = 1.0 / events

    def last_head(i):
        head = HB[1, i, deep] + dt1 * AB[1, i]
        off = head - TM[i]
        pull = (scale * WB[i]) * off
        GB[1, i, deep] = pull * dt1 * IC[1, i]
        return head, off * pull, pull

    def finish(i):
        head, square, pull = last_head(i)
        OUT[:, i - 1, :] = head
        LAM[1, i] = pull
        ACC[4, 0] += fold(square)

    for i in range(1, rows + 1):
        finish(i)
    write = pltpu.make_async_copy(OUT, out_hbm, x_sem.at[0])
    write.start()
    over(halo, lambda i: (last_head(i), None)[1])

    def slopes(step, i, grad_k_of, change_of):
        _, _, n = params(i)
        n1 = n - 1.0
        m = 1.0 - 1.0 / n
        inv_n2 = 1.0 / (n * n)
        inv_n1 = 1.0 / n1
        half_n1 = 0.5 * n1
        sums = None
        for c in chunks:
            k, log_x, log_v = KB[step, i, c.here], LG[step, i, c.bare], LV[step, i, c.bare]
            w, r = WW[step, i, c.bare], RV[step, i, c.bare]
            grad_k = grad_k_of(c)
            f = 1.0 - r
            wq = 2.0 * w * QQ[step, i, c.bare]
            n1r = n1 * r
            fl = f * log_x
            log_v = inv_n2 * log_v
            mfl = m * fl
            d_w = log_x - log_v - mfl
            by_log = -grad_k * (half_n1 * (f * k) + n1r * wq)
            by_n = -grad_k * ((0.5 * k) * (log_v + mfl) + wq * d_w)
            by_alpha = by_log
            if change_of is not None:
                change = change_of(c)
                by_log = by_log + change * (n1r - n * f)
                by_n = by_n + change * (inv_n1 + d_w - fl)
                by_alpha = by_log + change
            parts = [fold(grad_k * k), fold(by_alpha), fold(by_n)]
            sums = parts if sums is None else [a + b for a, b in zip(sums, parts)]
            yield c, by_log
        pair = (i + 1) // 2
        for place in range(3):
            ACC[pair, place] += sums[place]

    def pull_back(step, dt, i):
        s_up, s_down = 0.5 * face(i - 1), 0.5 * face(i)
        level = level_of(step, i)

        def grad_k_of(c):
            h, g = HB[step, i, c.here], GB[step, i, c.here]
            c_y = right_half * (left(h) - h) * (left(g) - g)
            return (
                s_down * ((HB[step, i + 1, c.here] - h) * (g - GB[step, i + 1, c.here]))
                + s_up * ((HB[step, i - 1, c.here] - h) * (g - GB[step, i - 1, c.here]))
                - (c_y + right(c_y))
                + c.half_above * (1.0 + HB[step, i, c.above] - h) * (g - GB[step, i, c.above])
                + c.half_below * (1.0 + h - HB[step, i, c.below]) * (GB[step, i, c.below] - g)
                + c.forcing(level, g)
            )

        def change_of(c):
            return -LAM[step, i, c.bare] * (dt * AB[step, i, c.bare])

        for c, by_log in slopes(step, i, grad_k_of, change_of):
            if step == 0:
                continue
            h, k, g = HB[step, i, c.here], KB[step, i, c.here], GB[step, i, c.here]
            f_y = right_half * (k + left(k)) * (left(g) - g)
            lap = (
                s_down * (k + KB[step, i + 1, c.here]) * (GB[step, i + 1, c.here] - g)
                + s_up * (KB[step, i - 1, c.here] + k) * (GB[step, i - 1, c.here] - g)
                + (f_y - right(f_y))
                + c.half_above * (KB[step, i, c.above] + k) * (GB[step, i, c.above] - g)
                + c.half_below * (k + KB[step, i, c.below]) * (GB[step, i, c.below] - g)
            )
            before = LAM[step, i, c.bare] + lap + by_log / h
            LAM[0, i, c.bare] = before
            GB[0, i, c.here] = before * dt0 * IC[0, i, c.bare]

    over(own, functools.partial(pull_back, 1, dt1))

    GB[0, 0] = jnp.zeros_like(GB[0, 0])
    GB[0, rows + 1] = jnp.zeros_like(GB[0, 0])
    over(own, functools.partial(pull_back, 0, dt0))

    def pull_halo(i):
        near = jnp.where(i == 0, 1, rows)
        half = jnp.where(i == 0, 0.5 * lower_open, 0.5 * upper_open)

        def grad_k_of(c):
            return half * ((HB[0, i, c.here] - HB[0, near, c.here]) * GB[0, near, c.here])

        for _ in slopes(0, i, grad_k_of, None):
            pass

    over(halo, pull_halo)

    zone_sums = None
    line = lax.broadcasted_iota(jnp.int32, (8, width), 0)
    for pair in range(4):
        sat, alpha, _ = params(2 * pair - 1)
        grads = [
            jnp.sum(ACC[pair, 0], axis=0, keepdims=True) / sat,
            jnp.sum(ACC[pair, 1], axis=0, keepdims=True) / alpha,
            jnp.sum(ACC[pair, 2], axis=0, keepdims=True),
        ]
        block = jnp.zeros((8, width), F32)
        for place, grad in enumerate(grads):
            block = jnp.where(line == place, grad, block)
        part = three(block, lambda t: nt_dot(t, OH[pair]))
        zone_sums = part if zone_sums is None else zone_sums + part
    loss = 0.5 * (jnp.sum(ACC[4, 0], keepdims=True) + scale * spread_sum)
    if packed:
        lane = lax.broadcasted_iota(jnp.int32, (1, zp), 1) < period
        lines = [
            jnp.where(lane, zone_sums[0:1], zone_sums[1:2]),
            jnp.where(lane, zone_sums[2:3], loss),
        ]
    else:
        lines = [zone_sums[0:1], zone_sums[1:2], zone_sums[2:3], loss + jnp.zeros((1, zp), F32)]
    message = jnp.concatenate(lines, axis=0)

    def sum_copy(buffer, sends, recvs, device, src, dst):
        return pltpu.make_async_remote_copy(
            src_ref=buffer.at[src],
            dst_ref=buffer.at[src],
            send_sem=sends.at[dst],
            recv_sem=recvs.at[src],
            device_id=device,
            device_id_type=pl.DeviceIdType.MESH,
        )

    def add_up(value, buffer, sends, recvs, devices, me, place):
        buffer[me] = value
        for device in devices:
            sum_copy(buffer, sends, recvs, device, me, place(device)).start()
        for device in devices:
            sum_copy(buffer, sends, recvs, device, place(device), place(device)).wait_recv()
        return jnp.sum(buffer[...], axis=0)

    if direct:
        exchanges = [(SUMR, sum_send, sum_recv, others, index, place_of)]
    else:
        exchanges = [
            (SUMR, sum_send, sum_recv, row_others, pos, lambda d: d[1]),
            (SUME, ev_send, ev_recv, event_others, me_event, lambda d: d[0]),
        ]
    for exchange in exchanges:
        message = add_up(message, *exchange)
    small_ref[...] = message
    write.wait()

    for number in range(LINKS):
        sent_pair(number, *pairs[number])
    for device in row_others:
        max_copy(0, device, pos).wait_send()
        max_copy(1, device, pos).wait_send()
    for buffer, sends, recvs, devices, me, place in exchanges:
        for device in devices:
            sum_copy(buffer, sends, recvs, device, me, place(device)).wait_send()


def hand_over(
    head_hbm,
    small_hbm,
    out_hbm,
    loss_ref,
    grad_sat_ref,
    grad_alpha_ref,
    grad_n_ref,
    head,
    small,
    sem,
):
    fetch = pltpu.make_async_copy(small_hbm, small, sem.at[0, PARTS])
    size = head.shape[0] // PARTS
    spans = [pl.ds(part * size, size) for part in range(PARTS)]
    moves = [
        (
            pltpu.make_async_copy(head_hbm.at[span], head.at[span], sem.at[0, part]),
            pltpu.make_async_copy(head.at[span], out_hbm.at[span], sem.at[1, part]),
        )
        for part, span in enumerate(spans)
    ]
    for inward, _ in moves:
        inward.start()
    fetch.start()
    for inward, outward in moves:
        inward.wait()
        outward.start()
    fetch.wait()
    zones = grad_sat_ref.shape[1]
    lines, zp = small.shape
    grad_sat_ref[...] = small[0:1, :zones]
    if lines == 2:
        period = zp // 2
        grad_alpha_ref[...] = small[0:1, period : period + zones]
        grad_n_ref[...] = small[1:2, :zones]
        loss_ref[...] = small[1:2, period : period + 1]
    else:
        grad_alpha_ref[...] = small[1:2, :zones]
        grad_n_ref[...] = small[2:3, :zones]
        loss_ref[...] = small[3:4, :1]
    for _, outward in moves:
        outward.wait()


def local(
    initial_head,
    sat_conductivity,
    vg_alpha,
    vg_n,
    zone_map,
    forcing_plan,
    tensiometer_cells,
    tensiometer_heads,
):
    _, depth, rows, width = initial_head.shape
    zones = sat_conductivity.shape[0]
    zp = -(-zones // 128) * 128
    count = lax.axis_size("row")
    groups = lax.axis_size("event")
    sensors = tensiometer_cells.shape[1]
    lines = 2 if 2 * zones <= zp else 4
    senders = count * groups if count * groups <= DIRECT else count
    vmem = pl.BlockSpec(memory_space=pltpu.VMEM)
    hbm = pl.BlockSpec(memory_space=pltpu.HBM)
    deep = pltpu.VMEM((STEPS, rows + 2, depth + 2 * PAD, width), F32)
    full = pltpu.VMEM((STEPS, rows + 2, depth, width), F32)
    single = pltpu.VMEM((rows + 2, depth, width), F32)
    dma = pltpu.SemaphoreType.DMA
    head, small = pl.pallas_call(
        functools.partial(kernel, count, groups, groups * initial_head.shape[0]),
        out_shape=(
            jax.ShapeDtypeStruct((depth, rows, width), F32),
            jax.ShapeDtypeStruct((lines, zp), F32),
        ),
        in_specs=[hbm] * 8,
        out_specs=(hbm, vmem),
        scratch_shapes=[
            deep,
            deep,
            full,
            full,
            full,
            full,
            full,
            full,
            full,
            deep,
            full,
            single,
            single,
            pltpu.VMEM((4, 8, width), F32),
            pltpu.VMEM((8, zp), F32),
            pltpu.VMEM((4, zp, width), BF16),
            pltpu.VMEM((2, 1, sensors), jnp.int32),
            pltpu.VMEM((2, 1, sensors), F32),
            pltpu.VMEM((2, 1, sensors), F32),
            pltpu.VMEM((2, 1, sensors), F32),
            *[pltpu.VMEM((depth, rows, width), F32)] * 2,
            *[pltpu.VMEM((1, zones), F32)] * 3,
            pltpu.VMEM(zone_map.shape, jnp.int32),
            pltpu.VMEM(forcing_plan.shape[1:], jnp.int32),
            pltpu.VMEM((1, sensors), jnp.int32),
            pltpu.VMEM((1, sensors), F32),
            pltpu.VMEM((STEPS, 8, width), F32),
            pltpu.VMEM((5, 3, 8, width), F32),
            pltpu.VMEM((STEPS, count, 8, 128), F32),
            pltpu.VMEM((senders, lines, zp), F32),
            pltpu.VMEM((groups, lines, zp), F32),
            dma((LINKS, 2)),
            dma((LINKS, 2)),
            dma((STEPS, count)),
            dma((STEPS, count)),
            dma((senders,)),
            dma((senders,)),
            dma((groups,)),
            dma((groups,)),
            dma((8,)),
        ],
        compiler_params=pltpu.CompilerParams(
            collective_id=0, has_side_effects=True, vmem_limit_bytes=VMEM_BYTES
        ),
    )(
        initial_head[0],
        sat_conductivity[None],
        vg_alpha[None],
        vg_n[None],
        zone_map,
        forcing_plan[0],
        tensiometer_cells,
        tensiometer_heads,
    )
    final, loss, grad_sat, grad_alpha, grad_n = pl.pallas_call(
        hand_over,
        out_shape=(
            jax.ShapeDtypeStruct((depth, rows, width), F32),
            jax.ShapeDtypeStruct((1, 1), F32),
            *[jax.ShapeDtypeStruct((1, zones), F32)] * 3,
        ),
        in_specs=[hbm] * 2,
        out_specs=(hbm, *[vmem] * 4),
        scratch_shapes=[
            pltpu.VMEM((depth, rows, width), F32),
            pltpu.VMEM((lines, zp), F32),
            dma((2, PARTS + 1)),
        ],
        compiler_params=pltpu.CompilerParams(vmem_limit_bytes=VMEM_BYTES),
    )(head, small)
    return (final[None], loss[0, 0], grad_sat[0], grad_alpha[0], grad_n[0])


def solution(mesh):
    return jax.shard_map(
        local,
        mesh=mesh,
        in_specs=(
            P("event", None, "row", None),
            P(),
            P(),
            P(),
            P("row", None),
            P("event", None, "row"),
            P("event", "row"),
            P("event", "row"),
        ),
        out_specs=(P("event", None, "row", None), P(), P(), P(), P()),
        check_vma=False,
    )
```

```python
import functools

import jax
import jax.numpy as jnp
from jax import lax
from jax.experimental import pallas as pl
from jax.experimental.pallas import tpu as pltpu
from jax.sharding import PartitionSpec as P

STEPS = 2
CFL = 0.4
IRRIGATION = 0.2
WATER_RANGE = 0.35
HIGHEST = lax.Precision.HIGHEST
F32 = jnp.float32
BF16 = jnp.bfloat16
LAYERS = 16
PAD = 8
LINKS = 6
DIRECT = 16
PARTS = 4
VMEM_BYTES = 63 * 1024 * 1024


def nt_dot(a, b):
    return lax.dot_general(a, b, (((1,), (1,)), ((), ())), preferred_element_type=F32)


def pieces(t):
    one = t.astype(BF16).astype(F32)
    two = (t - one).astype(BF16).astype(F32)
    return one, two, t - one - two


def three(t, product):
    size = t.shape[0]
    out = product(jnp.concatenate(pieces(t), axis=0).astype(BF16))
    return out[:size] + out[size : 2 * size] + out[2 * size :]


def fold(x):
    return jnp.sum(x.reshape(x.shape[0] // 8, 8, x.shape[1]), axis=0)


def kernel(
    count,
    groups,
    events,
    x_hbm,
    sat_hbm,
    alpha_hbm,
    n_hbm,
    zone_hbm,
    plan_hbm,
    cells_hbm,
    heads_hbm,
    out_hbm,
    small_ref,
    HB,
    KB,
    AB,
    IC,
    LG,
    LV,
    WW,
    RV,
    QQ,
    GB,
    LAM,
    WB,
    TM,
    PB,
    TAB,
    OH,
    NC,
    NT,
    SV,
    NV,
    XV,
    OUT,
    sat_ref,
    alpha_ref,
    n_ref,
    zone_ref,
    plan_ref,
    cells_ref,
    heads_ref,
    RATE,
    ACC,
    MX,
    SUMR,
    SUME,
    link_send,
    link_recv,
    max_send,
    max_recv,
    sum_send,
    sum_recv,
    ev_send,
    ev_recv,
    x_sem,
):
    fetches = [
        pltpu.make_async_copy(src, dst, x_sem.at[place])
        for place, (src, dst) in enumerate(
            (
                (x_hbm, XV),
                (zone_hbm, zone_ref),
                (sat_hbm, sat_ref),
                (alpha_hbm, alpha_ref),
                (n_hbm, n_ref),
                (cells_hbm, cells_ref),
                (heads_hbm, heads_ref),
                (plan_hbm, plan_ref),
            )
        )
    ]
    for fetch in fetches:
        fetch.start()
    depth, rows, width = XV.shape
    zp = OH.shape[1]
    zones = sat_ref.shape[1]
    pos = lax.axis_index("row")
    me_event = lax.axis_index("event")
    up, down = pos - 1, pos + 1
    has_up, has_down = pos > 0, pos < count - 1
    lower_open = has_up.astype(F32)
    upper_open = has_down.astype(F32)

    def dev(row):
        return (me_event, row)

    total_devices = count * groups
    direct = total_devices <= DIRECT
    index = me_event * count + pos

    def ring(at, size):
        return [at] + [
            jnp.where(at + k >= size, at + k - size, at + k) for k in range(1, size)
        ]

    row_ring, event_ring = ring(pos, count), ring(me_event, groups)
    others = [(e, r) for r in row_ring for e in event_ring][1:]
    row_others = [(me_event, r) for r in row_ring[1:]]
    event_others = [(e, pos) for e in event_ring[1:]]

    def place_of(device):
        return device[0] * count + device[1]

    barrier = pltpu.get_barrier_semaphore()
    greeted = others if direct else row_others + event_others
    for device in greeted:
        pl.semaphore_signal(barrier, 1, device_id=device, device_id_type=pl.DeviceIdType.MESH)

    deep = pl.ds(PAD, depth)

    def link(number, side, src, dst):
        return pltpu.make_async_remote_copy(
            src_ref=src,
            dst_ref=dst,
            send_sem=link_send.at[number, side],
            recv_sem=link_recv.at[number, side],
            device_id=dev(up if side == 0 else down),
            device_id_type=pl.DeviceIdType.MESH,
        )

    def start_pair(number, to_up, to_down):
        @pl.when(has_up)
        def _():
            link(number, 0, *to_up).start()

        @pl.when(has_down)
        def _():
            link(number, 1, *to_down).start()

    def recv_pair(number, to_up, to_down):
        @pl.when(has_down)
        def _():
            link(number, 0, *to_up).wait_recv()

        @pl.when(has_up)
        def _():
            link(number, 1, *to_down).wait_recv()

    def sent_pair(number, to_up, to_down):
        @pl.when(has_up)
        def _():
            link(number, 0, *to_up).wait_send()

        @pl.when(has_down)
        def _():
            link(number, 1, *to_down).wait_send()

    pairs = [
        ((HB.at[0, 1, deep], HB.at[0, rows + 1, deep]), (HB.at[0, rows, deep], HB.at[0, 0, deep])),
        ((PB.at[1], PB.at[3]), (PB.at[2], PB.at[0])),
        ((cells_ref, NC.at[1]), (cells_ref, NC.at[0])),
        ((heads_ref, NT.at[1]), (heads_ref, NT.at[0])),
        ((AB.at[0, 1], AB.at[0, rows + 1]), (AB.at[0, rows], AB.at[0, 0])),
        ((SV.at[0], NV.at[1]), (SV.at[1], NV.at[0])),
    ]

    def start(number):
        start_pair(number, *pairs[number])

    def recv(number):
        recv_pair(number, *pairs[number])

    fetches[0].wait()
    for i in (0, rows - 1):
        HB[0, i + 1, deep] = XV[:, i, :]
    pl.semaphore_wait(barrier, len(greeted))
    start(0)
    for fetch in fetches[1:]:
        fetch.wait()
    start(2)
    start(3)
    TAB[...] = jnp.zeros_like(TAB)
    TAB[0:1, :zones] = sat_ref[...]
    TAB[1:2, :zones] = alpha_ref[...]
    TAB[2:3, :zones] = n_ref[...]
    blocks = zone_ref.shape[1]
    spread = (
        lax.broadcasted_iota(jnp.int32, (blocks, width), 1) // 2
        == lax.broadcasted_iota(jnp.int32, (blocks, width), 0)
    ).astype(F32)
    exact = None if zones <= 256 else HIGHEST
    ids = jnp.dot(
        zone_ref[...].astype(F32), spread, preferred_element_type=F32, precision=exact
    )
    packed = 2 * zones <= zp
    period = zp // 2 if packed else zp
    zone_of = (lax.broadcasted_iota(jnp.int32, (zp, width), 0) % period).astype(F32)
    part_line = lax.broadcasted_iota(jnp.int32, (8, width), 0)
    for pair in range(2):
        own_ids = ids[pair : pair + 1]
        OH[pair + 1] = jnp.where(zone_of == own_ids, 1.0, 0.0).astype(BF16)
        block = three(TAB[...], lambda t: jnp.dot(t, OH[pair + 1], preferred_element_type=F32))
        PB[pair + 1] = jnp.where(part_line == 3, own_ids, block)
    start(1)
    for ref in (HB, KB, GB):
        for step in range(STEPS):
            for i in range(1, rows + 1):
                ref[step, i, 0:PAD] = jnp.zeros((PAD, width), F32)
                ref[step, i, PAD + depth :] = jnp.zeros((PAD, width), F32)
    for i in range(1, rows - 1):
        HB[0, i + 1, deep] = XV[:, i, :]

    @pl.when(jnp.logical_not(has_up))
    def _():
        HB[0, 0, deep] = HB[0, 1, deep]
        PB[0] = PB[1]
        NC[0] = cells_ref[...]
        NT[0] = heads_ref[...]
        NV[0] = jnp.zeros_like(NV[0])
        AB[0, 0] = jnp.zeros((depth, width), F32)

    @pl.when(jnp.logical_not(has_down))
    def _():
        HB[0, rows + 1, deep] = HB[0, rows, deep]
        PB[3] = PB[2]
        NC[1] = cells_ref[...]
        NT[1] = heads_ref[...]
        NV[1] = jnp.zeros_like(NV[1])
        AB[0, rows + 1] = jnp.zeros((depth, width), F32)

    ACC[...] = jnp.zeros_like(ACC)

    column = lax.broadcasted_iota(jnp.int32, (1, width), 1)
    layer = lax.broadcasted_iota(jnp.int32, (depth, 1), 0)
    right_half = jnp.where(column < width - 1, 0.5, 0.0)
    chunk_layer = lax.broadcasted_iota(jnp.int32, (LAYERS, 1), 0)

    class Chunk:
        def __init__(self, first):
            last = first + LAYERS == depth
            self.bare = pl.ds(first, LAYERS)
            self.here = pl.ds(PAD + first, LAYERS)
            self.above = pl.ds(PAD + first - 1, LAYERS)
            self.below = pl.ds(PAD + first + 1, LAYERS)
            self.top = chunk_layer == 0 if first == 0 else None
            self.bottom = chunk_layer == LAYERS - 1 if last else None
            self.half_above = 0.5 if self.top is None else jnp.where(self.top, 0.0, 0.5)
            self.half_below = 0.5 if self.bottom is None else jnp.where(self.bottom, 0.0, 0.5)

        def forcing(self, level, v):
            out = 0.0
            if self.top is not None:
                out = out + jnp.where(self.top, level * IRRIGATION, 0.0) * v
            if self.bottom is not None:
                out = out - jnp.where(self.bottom, v, 0.0)
            return out

        def ends(self, v):
            out = 0.0
            if self.top is not None:
                out = out + jnp.where(self.top, v, 0.0)
            if self.bottom is not None:
                out = out + jnp.where(self.bottom, v, 0.0)
            return out

    chunks = [Chunk(first) for first in range(0, depth, LAYERS)]

    def left(v):
        return pltpu.roll(v, width - 1, 1)

    def right(v):
        return pltpu.roll(v, 1, 1)

    def over(indices, body):
        first, stride, number = indices

        def go(j, carry):
            body(first + stride * j)
            return carry

        lax.fori_loop(0, number, go, 0)

    own = (1, 1, rows)
    inner = (2, 1, rows - 2)
    edges = (1, rows - 1, 2)
    halo = (0, rows + 1, 2)

    def params(i):
        block = PB[(i + 1) // 2]
        return block[0:1], block[1:2], block[2:3]

    def face(i):
        return jnp.where(i == 0, lower_open, jnp.where(i == rows, upper_open, 1.0))

    def level_of(step, i):
        levels = plan_ref[step : step + 1].astype(F32)
        return jnp.where(i > 2, levels[:, 1:2], levels[:, 0:1])

    def cell(step, i, outer=False):
        sat, alpha, n = params(i)
        m = 1.0 - 1.0 / n
        n1 = n - 1.0
        half_m = -0.5 * m
        scale = WATER_RANGE * n1 * alpha
        for c in chunks:
            if step == 0:
                head = HB[0, i, c.here]
            else:
                head = HB[0, i, c.here] + dt0 * AB[0, i, c.bare]
                HB[1, i, c.here] = head
            x = alpha * -head
            log_x = jnp.log(x)
            power = jnp.exp(n1 * log_x)
            v = 1.0 + x * power
            log_v = jnp.log(v)
            root = jnp.exp(half_m * log_v)
            w = power * (root * root)
            rest = 1.0 - w
            q = sat * root * rest
            KB[step, i, c.here] = q * rest
            if step == 1 or not outer:
                IC[step, i, c.bare] = v / (scale * w)
            if step == 1 and outer:
                continue
            LG[step, i, c.bare] = log_x
            LV[step, i, c.bare] = log_v
            WW[step, i, c.bare] = w
            RV[step, i, c.bare] = 1.0 / v
            QQ[step, i, c.bare] = q

    def flow(step, i):
        s_up, s_down = 0.5 * face(i - 1), 0.5 * face(i)
        level = level_of(step, i)
        top_rate = None
        for c in chunks:
            h, k = HB[step, i, c.here], KB[step, i, c.here]
            inv = IC[step, i, c.bare]
            k_up = s_up * (KB[step, i - 1, c.here] + k)
            k_down = s_down * (k + KB[step, i + 1, c.here])
            k_y = right_half * (k + left(k))
            f_y = k_y * (left(h) - h)
            k_above = c.half_above * (KB[step, i, c.above] + k)
            k_below = c.half_below * (k + KB[step, i, c.below])
            net = (
                k_down * (HB[step, i + 1, c.here] - h)
                + k_up * (HB[step, i - 1, c.here] - h)
                + (f_y - right(f_y))
                + k_above * (1.0 + HB[step, i, c.above] - h)
                - k_below * (1.0 + h - HB[step, i, c.below])
                + c.forcing(level, k)
            )
            total = k_up + k_down + (k_y + right(k_y)) + (k_above + k_below) + c.ends(k)
            AB[step, i, c.bare] = net * inv
            rate = jnp.max((total * inv).reshape(LAYERS // 8, 8, width), axis=0)
            top_rate = rate if top_rate is None else jnp.maximum(top_rate, rate)
        RATE[step] = jnp.maximum(RATE[step], top_rate)

    def max_copy(step, device, src):
        return pltpu.make_async_remote_copy(
            src_ref=MX.at[step, src],
            dst_ref=MX.at[step, src],
            send_sem=max_send.at[step, device[1]],
            recv_sem=max_recv.at[step, src],
            device_id=device,
            device_id_type=pl.DeviceIdType.MESH,
        )

    def send_rate(step):
        rate = RATE[step]
        tile = rate[:, :128]
        for start_lane in range(128, width, 128):
            tile = jnp.maximum(tile, rate[:, start_lane : start_lane + 128])
        MX[step, pos] = tile
        for device in row_others:
            max_copy(step, device, pos).start()

    def step_size(step):
        for device in row_others:
            max_copy(step, device, device[1]).wait_recv()
        top = jnp.max(MX[step], axis=0)
        return CFL / jnp.max(top, keepdims=True)

    RATE[...] = jnp.zeros_like(RATE)

    def first_cell(i):
        cell(0, i)

    over(own, first_cell)
    over(inner, functools.partial(flow, 0))
    recv(0)
    recv(1)
    over(halo, lambda i: cell(0, i, True))
    over(edges, functools.partial(flow, 0))
    send_rate(0)
    start(4)

    for pair in (0, 3):
        OH[pair] = jnp.where(zone_of == PB[pair][3:4], 1.0, 0.0).astype(BF16)

    def places(cells):
        index = cells.astype(F32)
        line = jnp.floor((index + 0.5) * (1.0 / width))
        col = index - width * line
        level = jnp.floor((line + 0.5) * (1.0 / rows))
        return level, line - rows * level, col

    sensors = cells_ref.shape[1]
    col_of = lax.broadcasted_iota(jnp.int32, (width, sensors), 0).astype(F32)

    def counts(cells, targets, wanted):
        level, row, col = places(cells)
        cols16 = jnp.where(col_of == col, 1.0, 0.0).astype(BF16)
        if wanted is None:
            spot = row * depth + level
            lines = rows * depth
        else:
            spot = jnp.where(row == wanted, level, -1.0)
            lines = depth
        line_of = lax.broadcasted_iota(jnp.int32, (lines, sensors), 0).astype(F32)
        hit = line_of == spot
        parts = [jnp.ones_like(targets), *pieces(targets)]
        out = nt_dot(stack(hit, parts), cols16)
        number = out[:lines]
        total = out[lines : 2 * lines] + out[2 * lines : 3 * lines] + out[3 * lines :]
        return number, total / jnp.maximum(number, 1.0), hit, cols16

    def stack(hit, parts):
        return jnp.concatenate([jnp.where(hit, part, 0.0) for part in parts], axis=0).astype(BF16)

    def put(values, hit, cols16):
        lines = hit.shape[0]
        out = nt_dot(stack(hit, pieces(values)), cols16)
        return out[:lines] + out[lines : 2 * lines] + out[2 * lines :]

    def take(field, hit, cols16):
        at_sensor = three(field, lambda t: jnp.dot(t, cols16, preferred_element_type=F32))
        return jnp.where(hit, at_sensor, 0.0)

    def column_sum(v):
        return jnp.sum(v, axis=0, keepdims=True)

    number, mean, own_hit, own_cols = counts(cells_ref[...], heads_ref[...], None)
    WB[1 : rows + 1] = number.reshape(rows, depth, width)
    TM[1 : rows + 1] = mean.reshape(rows, depth, width)
    recv(2)
    recv(3)
    halo_spots = []
    for side, wanted, place in ((0, rows - 1, 0), (1, 0, rows + 1)):
        number, mean, hit, cols = counts(NC[side], NT[side], wanted)
        WB[place] = number
        TM[place] = mean
        halo_spots.append((side, place, hit, cols))

    dt0 = step_size(0)

    def next_cell(i):
        cell(1, i)

    over(own, next_cell)
    over(inner, functools.partial(flow, 1))
    recv(4)
    over(halo, lambda i: cell(1, i, True))
    over(edges, functools.partial(flow, 1))
    send_rate(1)
    brims = jnp.concatenate([AB[1, 1], AB[1, rows]], axis=0)
    brim_hit = jnp.concatenate([own_hit[:depth], own_hit[(rows - 1) * depth :]], axis=0)
    picked = take(brims, brim_hit, own_cols)
    SV[0] = column_sum(picked[:depth])
    SV[1] = column_sum(picked[depth:])
    start(5)
    own_mean = column_sum(take(TM[1 : rows + 1].reshape(rows * depth, width), own_hit, own_cols))
    spread_sum = jnp.sum((heads_ref[...] - own_mean) ** 2, keepdims=True)
    recv(5)
    for side, place, hit, cols in halo_spots:
        AB[1, place] = put(NV[side], hit, cols) / jnp.maximum(WB[place], 1.0)
    dt1 = step_size(1)
    scale = 1.0 / events

    def last_head(i):
        head = HB[1, i, deep] + dt1 * AB[1, i]
        off = head - TM[i]
        pull = (scale * WB[i]) * off
        GB[1, i, deep] = pull * dt1 * IC[1, i]
        return head, off * pull, pull

    def finish(i):
        head, square, pull = last_head(i)
        OUT[:, i - 1, :] = head
        LAM[1, i] = pull
        ACC[4, 0] += fold(square)

    for i in range(1, rows + 1):
        finish(i)
    write = pltpu.make_async_copy(OUT, out_hbm, x_sem.at[0])
    write.start()
    over(halo, lambda i: (last_head(i), None)[1])

    def slopes(step, i, grad_k_of, change_of):
        _, _, n = params(i)
        n1 = n - 1.0
        m = 1.0 - 1.0 / n
        inv_n2 = 1.0 / (n * n)
        inv_n1 = 1.0 / n1
        half_n1 = 0.5 * n1
        sums = None
        for c in chunks:
            k, log_x, log_v = KB[step, i, c.here], LG[step, i, c.bare], LV[step, i, c.bare]
            w, r = WW[step, i, c.bare], RV[step, i, c.bare]
            grad_k = grad_k_of(c)
            f = 1.0 - r
            wq = 2.0 * w * QQ[step, i, c.bare]
            n1r = n1 * r
            fl = f * log_x
            log_v = inv_n2 * log_v
            mfl = m * fl
            d_w = log_x - log_v - mfl
            by_log = -grad_k * (half_n1 * (f * k) + n1r * wq)
            by_n = -grad_k * ((0.5 * k) * (log_v + mfl) + wq * d_w)
            by_alpha = by_log
            if change_of is not None:
                change = change_of(c)
                by_log = by_log + change * (n1r - n * f)
                by_n = by_n + change * (inv_n1 + d_w - fl)
                by_alpha = by_log + change
            parts = [fold(grad_k * k), fold(by_alpha), fold(by_n)]
            sums = parts if sums is None else [a + b for a, b in zip(sums, parts)]
            yield c, by_log
        pair = (i + 1) // 2
        for place in range(3):
            ACC[pair, place] += sums[place]

    def pull_back(step, dt, i):
        s_up, s_down = 0.5 * face(i - 1), 0.5 * face(i)
        level = level_of(step, i)

        def grad_k_of(c):
            h, g = HB[step, i, c.here], GB[step, i, c.here]
            c_y = right_half * (left(h) - h) * (left(g) - g)
            return (
                s_down * ((HB[step, i + 1, c.here] - h) * (g - GB[step, i + 1, c.here]))
                + s_up * ((HB[step, i - 1, c.here] - h) * (g - GB[step, i - 1, c.here]))
                - (c_y + right(c_y))
                + c.half_above * (1.0 + HB[step, i, c.above] - h) * (g - GB[step, i, c.above])
                + c.half_below * (1.0 + h - HB[step, i, c.below]) * (GB[step, i, c.below] - g)
                + c.forcing(level, g)
            )

        def change_of(c):
            return -LAM[step, i, c.bare] * (dt * AB[step, i, c.bare])

        for c, by_log in slopes(step, i, grad_k_of, change_of):
            if step == 0:
                continue
            h, k, g = HB[step, i, c.here], KB[step, i, c.here], GB[step, i, c.here]
            f_y = right_half * (k + left(k)) * (left(g) - g)
            lap = (
                s_down * (k + KB[step, i + 1, c.here]) * (GB[step, i + 1, c.here] - g)
                + s_up * (KB[step, i - 1, c.here] + k) * (GB[step, i - 1, c.here] - g)
                + (f_y - right(f_y))
                + c.half_above * (KB[step, i, c.above] + k) * (GB[step, i, c.above] - g)
                + c.half_below * (k + KB[step, i, c.below]) * (GB[step, i, c.below] - g)
            )
            before = LAM[step, i, c.bare] + lap + by_log / h
            LAM[0, i, c.bare] = before
            GB[0, i, c.here] = before * dt0 * IC[0, i, c.bare]

    over(own, functools.partial(pull_back, 1, dt1))

    GB[0, 0] = jnp.zeros_like(GB[0, 0])
    GB[0, rows + 1] = jnp.zeros_like(GB[0, 0])
    over(own, functools.partial(pull_back, 0, dt0))

    def pull_halo(i):
        near = jnp.where(i == 0, 1, rows)
        half = jnp.where(i == 0, 0.5 * lower_open, 0.5 * upper_open)

        def grad_k_of(c):
            return half * ((HB[0, i, c.here] - HB[0, near, c.here]) * GB[0, near, c.here])

        for _ in slopes(0, i, grad_k_of, None):
            pass

    over(halo, pull_halo)

    zone_sums = None
    line = lax.broadcasted_iota(jnp.int32, (8, width), 0)
    for pair in range(4):
        sat, alpha, _ = params(2 * pair - 1)
        grads = [
            jnp.sum(ACC[pair, 0], axis=0, keepdims=True) / sat,
            jnp.sum(ACC[pair, 1], axis=0, keepdims=True) / alpha,
            jnp.sum(ACC[pair, 2], axis=0, keepdims=True),
        ]
        block = jnp.zeros((8, width), F32)
        for place, grad in enumerate(grads):
            block = jnp.where(line == place, grad, block)
        part = three(block, lambda t: nt_dot(t, OH[pair]))
        zone_sums = part if zone_sums is None else zone_sums + part
    loss = 0.5 * (jnp.sum(ACC[4, 0], keepdims=True) + scale * spread_sum)
    if packed:
        lane = lax.broadcasted_iota(jnp.int32, (1, zp), 1) < period
        lines = [
            jnp.where(lane, zone_sums[0:1], zone_sums[1:2]),
            jnp.where(lane, zone_sums[2:3], loss),
        ]
    else:
        lines = [zone_sums[0:1], zone_sums[1:2], zone_sums[2:3], loss + jnp.zeros((1, zp), F32)]
    message = jnp.concatenate(lines, axis=0)

    def sum_copy(buffer, sends, recvs, device, src, dst):
        return pltpu.make_async_remote_copy(
            src_ref=buffer.at[src],
            dst_ref=buffer.at[src],
            send_sem=sends.at[dst],
            recv_sem=recvs.at[src],
            device_id=device,
            device_id_type=pl.DeviceIdType.MESH,
        )

    def add_up(value, buffer, sends, recvs, devices, me, place):
        buffer[me] = value
        for device in devices:
            sum_copy(buffer, sends, recvs, device, me, place(device)).start()
        for device in devices:
            sum_copy(buffer, sends, recvs, device, place(device), place(device)).wait_recv()
        return jnp.sum(buffer[...], axis=0)

    if direct:
        exchanges = [(SUMR, sum_send, sum_recv, others, index, place_of)]
    else:
        exchanges = [
            (SUMR, sum_send, sum_recv, row_others, pos, lambda d: d[1]),
            (SUME, ev_send, ev_recv, event_others, me_event, lambda d: d[0]),
        ]
    for exchange in exchanges:
        message = add_up(message, *exchange)
    small_ref[...] = message
    write.wait()

    for number in range(LINKS):
        sent_pair(number, *pairs[number])
    for device in row_others:
        max_copy(0, device, pos).wait_send()
        max_copy(1, device, pos).wait_send()
    for buffer, sends, recvs, devices, me, place in exchanges:
        for device in devices:
            sum_copy(buffer, sends, recvs, device, me, place(device)).wait_send()


def hand_over(
    head_hbm,
    small_hbm,
    out_hbm,
    loss_ref,
    grad_sat_ref,
    grad_alpha_ref,
    grad_n_ref,
    head,
    small,
    sem,
):
    fetch = pltpu.make_async_copy(small_hbm, small, sem.at[0, PARTS])
    size = head.shape[0] // PARTS
    spans = [pl.ds(part * size, size) for part in range(PARTS)]
    moves = [
        (
            pltpu.make_async_copy(head_hbm.at[span], head.at[span], sem.at[0, part]),
            pltpu.make_async_copy(head.at[span], out_hbm.at[span], sem.at[1, part]),
        )
        for part, span in enumerate(spans)
    ]
    for inward, _ in moves:
        inward.start()
    fetch.start()
    for inward, outward in moves:
        inward.wait()
        outward.start()
    fetch.wait()
    zones = grad_sat_ref.shape[1]
    lines, zp = small.shape
    grad_sat_ref[...] = small[0:1, :zones]
    if lines == 2:
        period = zp // 2
        grad_alpha_ref[...] = small[0:1, period : period + zones]
        grad_n_ref[...] = small[1:2, :zones]
        loss_ref[...] = small[1:2, period : period + 1]
    else:
        grad_alpha_ref[...] = small[1:2, :zones]
        grad_n_ref[...] = small[2:3, :zones]
        loss_ref[...] = small[3:4, :1]
    for _, outward in moves:
        outward.wait()


def local(
    initial_head,
    sat_conductivity,
    vg_alpha,
    vg_n,
    zone_map,
    forcing_plan,
    tensiometer_cells,
    tensiometer_heads,
):
    _, depth, rows, width = initial_head.shape
    zones = sat_conductivity.shape[0]
    zp = -(-zones // 128) * 128
    count = lax.axis_size("row")
    groups = lax.axis_size("event")
    sensors = tensiometer_cells.shape[1]
    lines = 2 if 2 * zones <= zp else 4
    senders = count * groups if count * groups <= DIRECT else count
    vmem = pl.BlockSpec(memory_space=pltpu.VMEM)
    hbm = pl.BlockSpec(memory_space=pltpu.HBM)
    deep = pltpu.VMEM((STEPS, rows + 2, depth + 2 * PAD, width), F32)
    full = pltpu.VMEM((STEPS, rows + 2, depth, width), F32)
    single = pltpu.VMEM((rows + 2, depth, width), F32)
    dma = pltpu.SemaphoreType.DMA
    head, small = pl.pallas_call(
        functools.partial(kernel, count, groups, groups * initial_head.shape[0]),
        out_shape=(
            jax.ShapeDtypeStruct((depth, rows, width), F32),
            jax.ShapeDtypeStruct((lines, zp), F32),
        ),
        in_specs=[hbm] * 8,
        out_specs=(hbm, vmem),
        scratch_shapes=[
            deep,
            deep,
            full,
            full,
            full,
            full,
            full,
            full,
            full,
            deep,
            full,
            single,
            single,
            pltpu.VMEM((4, 8, width), F32),
            pltpu.VMEM((8, zp), F32),
            pltpu.VMEM((4, zp, width), BF16),
            pltpu.VMEM((2, 1, sensors), jnp.int32),
            pltpu.VMEM((2, 1, sensors), F32),
            pltpu.VMEM((2, 1, sensors), F32),
            pltpu.VMEM((2, 1, sensors), F32),
            *[pltpu.VMEM((depth, rows, width), F32)] * 2,
            *[pltpu.VMEM((1, zones), F32)] * 3,
            pltpu.VMEM(zone_map.shape, jnp.int32),
            pltpu.VMEM(forcing_plan.shape[1:], jnp.int32),
            pltpu.VMEM((1, sensors), jnp.int32),
            pltpu.VMEM((1, sensors), F32),
            pltpu.VMEM((STEPS, 8, width), F32),
            pltpu.VMEM((5, 3, 8, width), F32),
            pltpu.VMEM((STEPS, count, 8, 128), F32),
            pltpu.VMEM((senders, lines, zp), F32),
            pltpu.VMEM((groups, lines, zp), F32),
            dma((LINKS, 2)),
            dma((LINKS, 2)),
            dma((STEPS, count)),
            dma((STEPS, count)),
            dma((senders,)),
            dma((senders,)),
            dma((groups,)),
            dma((groups,)),
            dma((8,)),
        ],
        compiler_params=pltpu.CompilerParams(
            collective_id=0, has_side_effects=True, vmem_limit_bytes=VMEM_BYTES
        ),
    )(
        initial_head[0],
        sat_conductivity[None],
        vg_alpha[None],
        vg_n[None],
        zone_map,
        forcing_plan[0],
        tensiometer_cells,
        tensiometer_heads,
    )
    final, loss, grad_sat, grad_alpha, grad_n = pl.pallas_call(
        hand_over,
        out_shape=(
            jax.ShapeDtypeStruct((depth, rows, width), F32),
            jax.ShapeDtypeStruct((1, 1), F32),
            *[jax.ShapeDtypeStruct((1, zones), F32)] * 3,
        ),
        in_specs=[hbm] * 2,
        out_specs=(hbm, *[vmem] * 4),
        scratch_shapes=[
            pltpu.VMEM((depth, rows, width), F32),
            pltpu.VMEM((lines, zp), F32),
            dma((2, PARTS + 1)),
        ],
        compiler_params=pltpu.CompilerParams(vmem_limit_bytes=VMEM_BYTES),
    )(head, small)
    return (final[None], loss[0, 0], grad_sat[0], grad_alpha[0], grad_n[0])


def solution(mesh):
    return jax.shard_map(
        local,
        mesh=mesh,
        in_specs=(
            P("event", None, "row", None),
            P(),
            P(),
            P(),
            P("row", None),
            P("event", None, "row"),
            P("event", "row"),
            P("event", "row"),
        ),
        out_specs=(P("event", None, "row", None), P(), P(), P(), P()),
        check_vma=False,
    )
```
